32 devices in a mesh: dp: 4 (over y, x), fsdp: 8 (over z, core).
Axes of the slice: x: 2, y: 2, z: 4, core: 2. Of those that a mesh axis runs over, the one named last changes fastest.
Arguments:
- tokens: bfloat16 [32768, 768], P(('dp', 'fsdp')), may hold values from -6 to 6
- lengths: int32 [64, 4], P(('dp', 'fsdp')), may hold values from 0 to 512, as said below
- bucket: int32 [32], replicated, may hold values from 0 to 1, as said below
- position_table: bfloat16 [512, 768], P(None, 'fsdp'), may hold values from -3 to 3
- in_projection: bfloat16 [768, 2304], P('fsdp'), may hold values from -0.21875 to 0.21875
- query_bias: bfloat16 [768], P('fsdp'), may hold values from -1.25 to 1.25
- value_bias: bfloat16 [768], P('fsdp'), may hold values from -1.25 to 1.25
- out_projection: bfloat16 [768, 768], P('fsdp'), may hold values from -0.875 to 0.875
- out_bias: bfloat16 [768], P('fsdp'), may hold values from -1.25 to 1.25
- first_gain: bfloat16 [768], P('fsdp'), may hold values from 0.5 to 1.5
- first_shift: bfloat16 [768], P('fsdp'), may hold values from -0.625 to 0.625
- up_projection: bfloat16 [768, 3072], P('fsdp'), may hold values from -0.21875 to 0.21875
- up_bias: bfloat16 [3072], P('fsdp'), may hold values from -1.25 to 1.25
- down_projection: bfloat16 [3072, 768], P('fsdp'), may hold values from -0.109375 to 0.109375
- down_bias: bfloat16 [768], P('fsdp'), may hold values from -1.25 to 1.25
- second_gain: bfloat16 [768], P('fsdp'), may hold values from 0.5 to 1.5
- second_shift: bfloat16 [768], P('fsdp'), may hold values from -0.625 to 0.625
Outputs:
- loss: float32 [], replicated
- pooled: float32 [256, 768], P(('dp', 'fsdp'))
- tokens_grad: float32 [32768, 768], P(('dp', 'fsdp'))
- position_table_grad: float32 [512, 768], P(None, 'fsdp')
- in_projection_grad: float32 [768, 2304], P('fsdp')
- query_bias_grad: float32 [768], P('fsdp')
- value_bias_grad: float32 [768], P('fsdp')
- out_projection_grad: float32 [768, 768], P('fsdp')
- out_bias_grad: float32 [768], P('fsdp')
- first_gain_grad: float32 [768], P('fsdp')
- first_shift_grad: float32 [768], P('fsdp')
- up_projection_grad: float32 [768, 3072], P('fsdp')
- up_bias_grad: float32 [3072], P('fsdp')
- down_projection_grad: float32 [3072, 768], P('fsdp')
- down_bias_grad: float32 [768], P('fsdp')
- second_gain_grad: float32 [768], P('fsdp')
- second_shift_grad: float32 [768], P('fsdp')
The draws below stay inside these ranges and needn't reach their ends.
Inputs may be any that keep to these rules, and one draw needn't show every extreme that they name: bucket[p] = 1: groups 2p and 2p+1 each hold one sequence of up to 512 positions, the first a query, the second its passage; bucket[p] = 0: both hold four sequences of up to 128 positions, query and passage alternating. Both kinds occur in every draw. lengths[g, s] is the true length of the sequence that begins at slot s of group g: 32 to 128 in four-sequence groups; 128 to 512 in slot 0 of one-sequence groups, 0 in their other slots. A long sequence of 512 and a short one of 128 occur in every draw.
All inputs are finite; a program needn't handle non-finite values.
Results may differ from the reference program's by a relative error of at most 0.015.
Values may be sent and summed in bfloat16 or wider, within the bound.
A program may use at most 192 MiB of HBM per device.

```python
import jax
import jax.numpy as jnp
from jax import lax

D = 768
H = 12
HD = 64
FF = 3072
SLOT = 128
GROUPS = 64
GROUP_PAIRS = 32
SLOTS = 256
TOKENS = 32768


def pair_layout(key):
    pairs = GROUP_PAIRS
    coins = jax.random.randint(jax.random.fold_in(key, 101), (pairs,), 0, 3)
    bucket = (coins < 2).astype(jnp.int32)
    picks = jax.random.randint(jax.random.fold_in(key, 102), (2,), 0, pairs)
    long_pick = picks[0]
    short_pick = (long_pick + 1 + picks[1] % (pairs - 1)) % pairs
    places = jnp.arange(pairs, dtype=jnp.int32)
    bucket = jnp.where(places == long_pick, 1, bucket)
    bucket = jnp.where(places == short_pick, 0, bucket)
    return (bucket.astype(jnp.int32), long_pick, short_pick)


def draw_bucket(key, part):
    bucket, long_pick, short_pick = pair_layout(key)
    return bucket


def draw_lengths(key, part):
    bucket, long_pick, short_pick = pair_layout(key)
    key = jax.random.fold_in(key, 7)
    streams = jax.random.split(key, 3)
    short = jax.random.randint(streams[0], (GROUPS, 4), SLOT // 4, SLOT + 1)
    long_len = jax.random.randint(streams[1], (GROUPS,), SLOT, 4 * SLOT + 1)
    group_ids = jnp.arange(GROUPS, dtype=jnp.int32)
    long_len = jnp.where(group_ids == 2 * long_pick, 4 * SLOT, long_len)
    corner = jax.random.randint(streams[2], (), 0, 4)
    column_ids = jnp.arange(4, dtype=jnp.int32)
    mark = (group_ids[:, None] == 2 * short_pick) & (column_ids[None, :] == corner)
    short = jnp.where(mark, SLOT, short)
    long_group = jnp.repeat(bucket, 2) > 0
    long_rows = jnp.where(column_ids[None, :] == 0, long_len[:, None], 0)
    return jnp.where(long_group[:, None], long_rows, short).astype(jnp.int32)


def block_levels(own_key, extent, shards, smallest, top_value):
    loudness = 1.0
    for dim, shards_of in shards:
        draws = jax.random.uniform(jax.random.fold_in(jax.random.fold_in(own_key, 6), dim), (shards_of,), jnp.float32, smallest / len(shards), top_value / len(shards))
        loudness = loudness * jnp.repeat(jnp.exp(draws), extent[dim] // shards_of).reshape((-1,) + (1,) * (len(extent) - 1 - dim))
    return loudness


def scatter_about(stream_key, shape, scale, bound, cuts=(), held_as=jnp.bfloat16):
    loudness = block_levels(stream_key, shape, cuts, -0.22, 0.18) if cuts else 1.0
    array = jax.random.normal(stream_key, shape, jnp.float32) * scale * loudness
    return jnp.minimum(jnp.maximum(array, -bound), bound).astype(held_as)


def setup_inputs(seed: int = 0) -> dict:
    key_of = jax.random.split(jax.random.key(seed), 18)
    tokens = scatter_about(key_of[0], (TOKENS, D), 1.0, 6.0, ((0, 32),))
    lengths = draw_lengths(jax.random.fold_in(key_of[17], 71), 0)
    bucket = draw_bucket(jax.random.fold_in(key_of[17], 71), 0)
    position_table = scatter_about(key_of[3], (4 * SLOT, D), 0.5, 3.0, ((1, 8),))
    in_projection = scatter_about(key_of[4], (D, 3 * D), D ** -0.5, 0.21875, ((0, 8),))
    query_bias = scatter_about(key_of[5], (D,), 0.2, 1.25, ((0, 8),))
    value_bias = scatter_about(key_of[6], (D,), 0.2, 1.25, ((0, 8),))
    out_projection = scatter_about(key_of[7], (D, D), (D // 16) ** -0.5, 0.875, ((0, 8),))
    out_bias = scatter_about(key_of[8], (D,), 0.2, 1.25, ((0, 8),))
    first_gain = jnp.clip(1.0 + 0.1 * jax.random.normal(key_of[9], (D,), jnp.float32), 0.5, 1.5).astype(jnp.bfloat16)
    first_shift = scatter_about(key_of[10], (D,), 0.1, 0.625, ((0, 8),))
    up_projection = scatter_about(key_of[11], (D, FF), D ** -0.5, 0.21875, ((0, 8),))
    up_bias = scatter_about(key_of[12], (FF,), 0.2, 1.25, ((0, 8),))
    down_projection = scatter_about(key_of[13], (FF, D), FF ** -0.5, 0.109375, ((0, 8),))
    down_bias = scatter_about(key_of[14], (D,), 0.2, 1.25, ((0, 8),))
    second_gain = jnp.clip(1.0 + 0.1 * jax.random.normal(key_of[15], (D,), jnp.float32), 0.5, 1.5).astype(jnp.bfloat16)
    second_shift = scatter_about(key_of[16], (D,), 0.1, 0.625, ((0, 8),))
    return dict(tokens=tokens, lengths=lengths, bucket=bucket, position_table=position_table, in_projection=in_projection, query_bias=query_bias, value_bias=value_bias, out_projection=out_projection, out_bias=out_bias, first_gain=first_gain, first_shift=first_shift, up_projection=up_projection, up_bias=up_bias, down_projection=down_projection, down_bias=down_bias, second_gain=second_gain, second_shift=second_shift)


highest = lax.Precision.HIGHEST
block_groups = 8

@jax.custom_vjp
def low(v):
    return lax.optimization_barrier(v.astype(jnp.bfloat16)).astype(jnp.float32)

@jax.custom_vjp
def low_back(v):
    return v

def low_keep(v):
    return (low(v), None)

def low_pass(kept, grad):
    return (grad,)

def back_keep(v):
    return (v, None)

def back_low(kept, grad):
    return (low(grad),)
low.defvjp(low_keep, low_pass)
low_back.defvjp(back_keep, back_low)

def norm_forward(value, gain, shift):
    mean = lax.optimization_barrier(jnp.mean(value, -1, keepdims=True))
    centred = value - mean
    spread = lax.optimization_barrier(jnp.mean(centred * centred, -1, keepdims=True))
    return centred * lax.rsqrt(spread + 1e-06) * gain + shift

def encode(block, long_flag, lengths_row, params):
    table, w_in, query_bias, value_bias, w_out, out_bias, gain_one, shift_one, w_up, up_bias, w_down, down_bias, gain_two, shift_two = params
    count = 4 * SLOT
    places = jnp.arange(count, dtype=jnp.int32)
    segment = jnp.where(long_flag > 0, 0, places // SLOT)
    inside = jnp.where(long_flag > 0, places, places % SLOT)
    choose = segment[:, None] == jnp.arange(4, dtype=jnp.int32)[None, :]
    live = inside < lax.optimization_barrier(jnp.sum(jnp.where(choose, lengths_row[None, :], 0), 1))
    positions = jnp.where(long_flag > 0, table, jnp.tile(table[:SLOT], (4, 1)))
    resid = block + positions
    in_bias = jnp.concatenate([query_bias, jnp.zeros_like(query_bias), value_bias])
    mixed = low_back(low(jnp.dot(low(resid), w_in, precision=highest) + in_bias))
    query = mixed[:, :D].reshape(count, H, HD)
    keys = mixed[:, D:2 * D].reshape(count, H, HD)
    vals = mixed[:, 2 * D:].reshape(count, H, HD)
    allowed = (segment[:, None] == segment[None, :]) & live[None, :]
    scores = jnp.einsum('qhd,khd->hqk', query, keys, precision=highest) * HD ** (-0.5)
    scores = low_back(jnp.where(allowed[None], scores, -1000000000.0))
    top = lax.optimization_barrier(jnp.max(scores, -1, keepdims=True))
    raised = jnp.exp(scores - top)
    prob = low(raised / lax.optimization_barrier(jnp.sum(raised, -1, keepdims=True)))
    context = jnp.einsum('hqk,khd->qhd', prob, vals, precision=highest).reshape(count, D)
    context = low_back(low(context))
    attended = low_back(jnp.dot(context, w_out, precision=highest) + out_bias)
    hidden = norm_forward(resid + attended, gain_one, shift_one)
    upward = low_back(jnp.dot(low(hidden), w_up, precision=highest) + up_bias)
    active = low(jax.nn.gelu(upward, approximate=False))
    downward = low_back(jnp.dot(active, w_down, precision=highest) + down_bias)
    output = norm_forward(hidden + downward, gain_two, shift_two)
    picker = jnp.transpose((choose & live[:, None]).astype(output.dtype))
    divisor = jnp.maximum(lengths_row, 1).astype(output.dtype)
    return jnp.dot(picker, output, precision=highest) / divisor[:, None]

def slot_roles(bucket):
    long_slot = jnp.repeat(jnp.repeat(bucket, 2), 4) > 0
    slots = jnp.arange(long_slot.shape[0], dtype=jnp.int32)
    within = slots % 4
    odd_group = slots // 4 % 2
    query = jnp.where(long_slot, (within == 0) & (odd_group == 0), within % 2 == 0)
    passage = jnp.where(long_slot, (within == 0) & (odd_group == 1), within % 2 == 1)
    partner = jnp.where(long_slot, slots + 4, slots + 1)
    return (query, passage, partner)

def contrast(pooled, bucket):
    embedded = low(pooled * lax.rsqrt(lax.optimization_barrier(jnp.sum(pooled * pooled, -1, keepdims=True)) + 1e-06))
    logits = low_back(jnp.dot(embedded, embedded.T, precision=highest) * 100.0)
    query, passage, partner = slot_roles(bucket)
    columns = jnp.arange(SLOTS, dtype=jnp.int32)
    masked = jnp.where(passage[None, :], logits, -1000000000.0)
    top = lax.optimization_barrier(jnp.max(masked, -1, keepdims=True))
    total = lax.optimization_barrier(jnp.sum(jnp.exp(masked - top), -1))
    spread = top[:, 0] + jnp.log(total)
    positive = lax.optimization_barrier(jnp.sum(jnp.where(columns[None, :] == partner[:, None], logits, 0.0), -1))
    count = jnp.sum(4 - 3 * bucket).astype(jnp.float32)
    return jnp.sum(jnp.where(query, spread - positive, 0.0)) / count

def forward(tokens, lengths, bucket, params):
    long_group = jnp.repeat(bucket, 2)
    blocks = tokens.reshape(GROUPS // block_groups, block_groups, 4 * SLOT, D)
    flags = long_group.reshape(GROUPS // block_groups, block_groups)
    rows = lengths.reshape(GROUPS // block_groups, block_groups, 4)

    def one_block(item):
        return jax.vmap(lambda x, f, r: encode(x, f, r, params))(item[0], item[1], item[2])
    pooled = lax.map(jax.checkpoint(one_block), (blocks, flags, rows)).reshape(SLOTS, D)
    return (contrast(pooled, bucket), pooled)

def reference(tokens, lengths, bucket, position_table, in_projection, query_bias, value_bias, out_projection, out_bias, first_gain, first_shift, up_projection, up_bias, down_projection, down_bias, second_gain, second_shift):
    params = tuple((piece.astype(jnp.float32) for piece in (position_table, in_projection, query_bias, value_bias, out_projection, out_bias, first_gain, first_shift, up_projection, up_bias, down_projection, down_bias, second_gain, second_shift)))

    def run(tok, *prm):
        return forward(tok, lengths, bucket, prm)
    loss, back, pooled = jax.vjp(run, tokens.astype(jnp.float32), *params, has_aux=True)
    grads = back(jnp.ones_like(loss))
    return (loss, pooled, grads[0], grads[1], grads[2], grads[3], grads[4], grads[5], grads[6], grads[7], grads[8], grads[9], grads[10], grads[11], grads[12], grads[13], grads[14])
```

```python
import functools

import jax
import jax.numpy as jnp
from jax import lax
from jax.experimental import pallas as pl
from jax.experimental.pallas import tpu as pltpu
from jax.sharding import PartitionSpec as P

H = 12
narrow = jnp.bfloat16
single = jnp.float32
ANY = pl.ANY
VM = pltpu.VMEM
SM = pltpu.SMEM
LIMIT = 60 * 2**20


def dot(a, b):
    return lax.dot_general(a, b, (((1,), (0,)), ((), ())), preferred_element_type=single)


def dot_nt(a, b):
    return lax.dot_general(a, b, (((1,), (1,)), ((), ())), preferred_element_type=single)


def at(start, size):
    return pl.ds(pl.multiple_of(start, 128), size)


def gelu_pair(u):
    t = 1.0 / (1.0 + 0.23164189 * jnp.abs(u))
    e = jnp.exp(-0.5 * (u * u))
    tail = t * (
        0.127414796 + t * (-0.142248368 + t * (0.7107068705 + t * (-0.7265760135 + t * 0.5307027145)))
    )
    tail = tail * e
    phi = jnp.where(u < 0, tail, 1.0 - tail)
    return u * phi, phi + u * (e * 0.3989422804)


def norm_rows(value):
    mean = jnp.mean(value, -1, keepdims=True)
    centred = value - mean
    rstd = lax.rsqrt(jnp.mean(centred * centred, -1, keepdims=True) + 1e-06)
    return centred * rstd, rstd


def norm_back(grad, unit, rstd):
    one = jnp.mean(grad, -1, keepdims=True)
    two = jnp.mean(grad * unit, -1, keepdims=True)
    return rstd * (grad - one - unit * two)


def slot_lengths(lens, flag, g, along_rows, count, width):
    slot = count // 4
    shape = (count, width) if along_rows else (8, count)
    t = lax.broadcasted_iota(jnp.int32, shape, 0 if along_rows else 1)
    which = t // slot
    long = flag[g] > 0
    limit = jnp.where(which == 0, lens[g, 0], lens[g, 1])
    limit = jnp.where(which == 2, lens[g, 2], limit)
    limit = jnp.where(which == 3, lens[g, 3], limit)
    limit = jnp.where(long, lens[g, 0], limit)
    inside = jnp.where(long, t, t % slot)
    return which, inside < limit


def forward_kernel(
    sizes,
    lens, flag, vecs, tok, tab, w_in, w_out, w_up, w_down,
    x_o, mixed_o, prob_o, ctx_o, n1_o, r1_o, act_o, gp_o, n2_o, r2_o, pooled_o,
    v_in, v_out, v_up, v_down, tab_v, x_v, mixed, mask, pst, ctx, hid, hid_low, n_st, r1_v, r2_v, ast, gst, acc,
    in_sem, out_sem, p_sem, a_sem, g_sem,
):
    groups, count, width, ff = sizes
    rows = groups * count
    pairs = width // 128
    loads = [
        pltpu.make_async_copy(s, d, in_sem.at[i])
        for i, (s, d) in enumerate(
            ((tok, x_v), (tab, tab_v), (w_in, v_in), (w_out, v_out), (w_up, v_up), (w_down, v_down))
        )
    ]
    for c in loads:
        c.start()
    stores = []

    def store(src, dst):
        c = pltpu.make_async_copy(src, dst, out_sem.at[len(stores)])
        c.start()
        stores.append(c)

    def vec(i):
        return vecs[i : i + 1, :]

    loads[0].wait()
    loads[1].wait()
    slot = count // 4
    for g in range(groups):
        which_q, _ = slot_lengths(lens, flag, g, True, count, 128)
        which_k, live_k = slot_lengths(lens, flag, g, False, count, 128)
        long = flag[g] > 0
        wq = which_q[:, :1]
        open_ = live_k[:1] & (long | (wq == which_k[:1]))
        mask[g] = jnp.where(open_, 0.0, -1000000000.0).astype(single)
        for s in range(4):
            part = x_v[pl.ds(g * count + s * slot, slot), :].astype(single)
            place = jnp.where(long, tab_v[pl.ds(s * slot, slot), :].astype(single), tab_v[:slot, :].astype(single))
            both = part + place
            hid[pl.ds(g * count + s * slot, slot), :] = both
            x_v[pl.ds(g * count + s * slot, slot), :] = both.astype(narrow)
    store(x_v, x_o)

    loads[2].wait()
    for part in range(3):
        cols = pl.ds(part * width, width)

        def project(b, _, cols=cols, part=part):
            r = at(b * 256, 256)
            out = dot(x_v[r, :], v_in[:, cols])
            if part == 0:
                out = out + vec(0)
            if part == 2:
                out = out + vec(1)
            mixed[r, cols] = out.astype(narrow)
            return 0

        lax.fori_loop(0, rows // 256, project, 0)
    store(mixed, mixed_o)

    lane = lax.broadcasted_iota(jnp.int32, (count, 128), 1)
    half = (lane < 64, lane >= 64)

    def attend(i, _):
        g = i // pairs
        p = i % pairs
        s_ = i % 2
        r = at(g * count, count)

        @pl.when(i >= 2)
        def _():
            pltpu.make_async_copy(pst.at[s_], prob_o.at[i], p_sem.at[s_]).wait()

        q = mixed[r, at(p * 128, 128)]
        k = mixed[r, at(width + p * 128, 128)]
        v = mixed[r, at(2 * width + p * 128, 128)]
        zero = jnp.zeros_like(q)
        out = [None] * (count // 256)
        for h in range(2):
            qh = jnp.where(half[h], q, zero) * jnp.asarray(0.125, narrow)
            vh = jnp.where(half[h], v, zero)
            for b in range(count // 256):
                sc = dot_nt(qh[b * 256 : (b + 1) * 256], k) + mask[g, b * 256 : (b + 1) * 256, :]
                e = jnp.exp(sc - jnp.max(sc, -1, keepdims=True))
                low = (e * (1.0 / jnp.sum(e, -1, keepdims=True))).astype(narrow)
                pst[s_, h, b * 256 : (b + 1) * 256, :] = low
                o = dot(low, vh)
                out[b] = o if out[b] is None else out[b] + o
        for b in range(count // 256):
            ctx[at(g * count + b * 256, 256), at(p * 128, 128)] = out[b].astype(narrow)
        pltpu.make_async_copy(pst.at[s_], prob_o.at[i], p_sem.at[s_]).start()
        return 0

    n = groups * pairs
    lax.fori_loop(0, n, attend, 0)
    for i in range(max(n - 2, 0), n):
        pltpu.make_async_copy(pst.at[i % 2], prob_o.at[i], p_sem.at[i % 2]).wait()
    store(ctx, ctx_o)

    loads[3].wait()

    def first(b, _):
        r = at(b * 256, 256)
        total = hid[r, :] + dot(ctx[r, :], v_out[...]) + vec(2)
        unit, rstd = norm_rows(total)
        n_st[r, :] = unit
        r1_v[r, :] = jnp.broadcast_to(rstd, (256, 128))
        h = unit * vec(3) + vec(4)
        hid[r, :] = h
        hid_low[r, :] = h.astype(narrow)
        acc[r, :] = h + vec(5)
        return 0

    lax.fori_loop(0, rows // 256, first, 0)
    store(n_st, n1_o)
    store(r1_v, r1_o)

    loads[4].wait()
    loads[5].wait()
    wide = ff // width

    def act_copies(j, s_):
        return (
            pltpu.make_async_copy(ast.at[s_], act_o.at[j], a_sem.at[s_]),
            pltpu.make_async_copy(gst.at[s_], gp_o.at[j], g_sem.at[s_]),
        )

    for j in range(wide):
        s_ = j % 2
        if j >= 2:
            for c in act_copies(j - 2, s_):
                c.wait()
        cols = pl.ds(j * width, width)

        def feed(b, _, s_=s_, j=j, cols=cols):
            r = at(b * 256, 256)
            u = dot(hid_low[r, :], v_up[:, cols]) + vec(8 + j)
            a, d = gelu_pair(u)
            a = a.astype(narrow)
            ast[s_, r, :] = a
            gst[s_, r, :] = d.astype(narrow)
            acc[r, :] += dot(a, v_down[cols, :])
            return 0

        lax.fori_loop(0, rows // 256, feed, 0)
        for c in act_copies(j, s_):
            c.start()
    for j in range(max(wide - 2, 0), wide):
        for c in act_copies(j, j % 2):
            c.wait()

    stores[3].wait()
    for g in range(groups):
        _, live = slot_lengths(lens, flag, g, True, count, 128)
        sums = []
        for s in range(4):
            r = pl.ds(g * count + s * slot, slot)
            unit, rstd = norm_rows(acc[r, :])
            n_st[r, :] = unit
            r2_v[r, :] = jnp.broadcast_to(rstd, (slot, 128))
            out = unit * vec(6) + vec(7)
            keep = live[s * slot : (s + 1) * slot, :1]
            sums.append(jnp.sum(jnp.where(keep, out, 0.0), 0, keepdims=True))
        long = flag[g] > 0
        for s in range(4):
            div = jnp.maximum(lens[g, s], 1).astype(single)
            if s == 0:
                total = jnp.where(long, sums[0] + sums[1] + sums[2] + sums[3], sums[0])
            else:
                total = jnp.where(long, 0.0, sums[s])
            pooled_o[4 * g + s : 4 * g + s + 1, :] = total / div
    store(n_st, n2_o)
    store(r2_v, r2_o)
    for i, c in enumerate(stores):
        if i != 3:
            c.wait()


def backward_kernel(
    sizes,
    lens, flag, vecs, pg, w_in, w_out, w_up, w_down, x_i, mixed_i, prob_i, ctx_i, n1_i, r1_i, act_i, gp_i, n2_i, r2_i,
    tok_o, gin_o, gout_o, gup_o, gdown_o, gtab_o, gvec_o,
    v_in, v_out, v_up, v_down, x_v, mixed, ctx, n1, n2, r1_v, r2_v, ast, gst, pst, low, low_t, hid_t, up_low, grad, dctx, gst_a, gst_b, gsmall,
    in_sem, a_sem, p_sem, o_sem, b_sem,
):
    groups, count, width, ff = sizes
    rows = groups * count
    pairs = width // 128
    slot = count // 4
    wide = ff // width
    blocks = rows // 256
    loads = [
        pltpu.make_async_copy(s, d, in_sem.at[i])
        for i, (s, d) in enumerate(
            (
                (n2_i, n2), (r2_i, r2_v), (n1_i, n1), (w_down, v_down), (w_up, v_up), (r1_i, r1_v), (ctx_i, ctx),
                (w_out, v_out), (mixed_i, mixed), (x_i, x_v), (w_in, v_in),
            )
        )
    ]
    (l_n2, l_r2, l_n1, l_down, l_up, l_r1, l_ctx, l_wout, l_mixed, l_x, l_win) = loads

    def act_loads(j):
        return (
            pltpu.make_async_copy(act_i.at[j], ast.at[j % 2], a_sem.at[j % 2]),
            pltpu.make_async_copy(gp_i.at[j], gst.at[j % 2], a_sem.at[2 + j % 2]),
        )

    def prob_load(i, s_):
        return pltpu.make_async_copy(prob_i.at[i], pst.at[s_], p_sem.at[s_])

    l_n2.start()
    l_r2.start()
    for c in act_loads(0):
        c.start()
    for c in loads[2:5]:
        c.start()
    for c in act_loads(1):
        c.start()
    for c in loads[5:]:
        c.start()
    prob_load(0, 0).start()
    prob_load(1, 1).start()

    def vec(i):
        return vecs[i : i + 1, :]

    stores = []

    def store(src, dst):
        c = pltpu.make_async_copy(src, dst, o_sem.at[len(stores)])
        c.start()
        stores.append(c)

    l_n2.wait()
    l_r2.wait()
    gain_sum = jnp.zeros((1, width), single)
    shift_sum = jnp.zeros((1, width), single)
    bias_sum = jnp.zeros((1, width), single)
    for g in range(groups):
        _, live = slot_lengths(lens, flag, g, True, count, 128)
        long = flag[g] > 0
        for s in range(4):
            r = pl.ds(g * count + s * slot, slot)
            mine = pg[4 * g + s : 4 * g + s + 1, :] / jnp.maximum(lens[g, s], 1).astype(single)
            first = pg[4 * g : 4 * g + 1, :] / jnp.maximum(lens[g, 0], 1).astype(single)
            row = jnp.where(long, first, mine)
            keep = live[s * slot : (s + 1) * slot, :1]
            d = jnp.where(keep, row, 0.0)
            unit = n2[r, :]
            gain_sum = gain_sum + jnp.sum(d * unit, 0, keepdims=True)
            shift_sum = shift_sum + jnp.sum(d, 0, keepdims=True)
            back = norm_back(d * vec(6), unit, r2_v[r, :1])
            grad[r, :] = back
            lowered = back.astype(narrow)
            low[r, :] = lowered
            bias_sum = bias_sum + jnp.sum(lowered.astype(single), 0, keepdims=True)
            low_t[:, r] = lowered.T
    gsmall[...] = jnp.zeros_like(gsmall)
    gsmall[6:7, :] = gain_sum
    gsmall[7:8, :] = shift_sum
    gsmall[5:6, :] = bias_sum
    l_n1.wait()
    for b in range(rows // slot):
        r = pl.ds(b * slot, slot)
        hid_t[:, r] = (n1[r, :] * vec(3) + vec(4)).astype(narrow).T

    l_down.wait()
    l_up.wait()

    for j in range(wide):
        s_ = j % 2
        cols = pl.ds(j * width, width)
        for c in act_loads(j):
            c.wait()
        if j >= 1:
            pltpu.make_async_copy(gst_a, gdown_o.at[:, pl.ds((j - 1) * width, width)], b_sem.at[0]).wait()
            pltpu.make_async_copy(gst_b, gup_o.at[:, pl.ds((j - 1) * width, width)], b_sem.at[1]).wait()

        def feed(b, total, s_=s_, cols=cols):
            r = at(b * 256, 256)
            up = (dot_nt(low[r, :], v_down[cols, :]) * gst[s_, r, :].astype(single)).astype(narrow)
            up_low[r, :] = up
            grad[r, :] += dot_nt(up, v_up[:, cols])
            return total + jnp.sum(up.astype(single), 0, keepdims=True)

        gsmall[8 + j : 9 + j, :] = lax.fori_loop(0, blocks, feed, jnp.zeros((1, width), single))

        def weigh(b, _, s_=s_):
            r = at(b * 256, 256)
            gst_a[r, :] = dot(low_t[r, :], ast[s_]).astype(narrow)
            gst_b[r, :] = dot(hid_t[r, :], up_low[...]).astype(narrow)
            return 0

        lax.fori_loop(0, width // 256, weigh, 0)
        pltpu.make_async_copy(gst_a, gdown_o.at[:, cols], b_sem.at[0]).start()
        pltpu.make_async_copy(gst_b, gup_o.at[:, cols], b_sem.at[1]).start()
        if j + 2 < wide:
            for c in act_loads(j + 2):
                c.start()

    l_r1.wait()
    l_ctx.wait()
    l_wout.wait()
    gain_sum = jnp.zeros((1, width), single)
    shift_sum = jnp.zeros((1, width), single)
    bias_sum = jnp.zeros((1, width), single)
    for b in range(rows // slot):
        r = pl.ds(b * slot, slot)
        d = grad[r, :]
        unit = n1[r, :]
        gain_sum = gain_sum + jnp.sum(d * unit, 0, keepdims=True)
        shift_sum = shift_sum + jnp.sum(d, 0, keepdims=True)
        back = norm_back(d * vec(3), unit, r1_v[r, :1])
        grad[r, :] = back
        lowered = back.astype(narrow)
        low[r, :] = lowered
        bias_sum = bias_sum + jnp.sum(lowered.astype(single), 0, keepdims=True)
        hid_t[:, r] = ctx[r, :].T
    gsmall[3:4, :] = gain_sum
    gsmall[4:5, :] = shift_sum
    gsmall[2:3, :] = bias_sum
    last = pl.ds((wide - 1) * width, width)
    pltpu.make_async_copy(gst_a, gdown_o.at[:, last], b_sem.at[0]).wait()
    pltpu.make_async_copy(gst_b, gup_o.at[:, last], b_sem.at[1]).wait()

    def out_weigh(b, _):
        r = at(b * 256, 256)
        gst_a[r, :] = dot(hid_t[r, :], low[...]).astype(narrow)
        return 0

    lax.fori_loop(0, width // 256, out_weigh, 0)
    store(gst_a, gout_o)

    def context_back(b, _):
        r = at(b * 256, 256)
        dctx[r, :] = dot_nt(low[r, :], v_out[...]).astype(narrow)
        return 0

    lax.fori_loop(0, blocks, context_back, 0)

    l_mixed.wait()
    lane = lax.broadcasted_iota(jnp.int32, (count, 128), 1)
    half = (lane < 64, lane >= 64)
    scale = jnp.asarray(0.125, narrow)
    n = groups * pairs

    def attend(i, _):
        g = i // pairs
        p = i % pairs
        s_ = i % 2
        r = at(g * count, count)
        prob_load(i, s_).wait()
        c_q = at(p * 128, 128)
        c_k = at(width + p * 128, 128)
        c_v = at(2 * width + p * 128, 128)
        q = mixed[r, c_q] * scale
        k = mixed[r, c_k]
        v = mixed[r, c_v]
        dc = dctx[r, c_q]
        c = ctx[r, c_q]
        q_t = q.T
        dc_t = dc.T
        zero = jnp.zeros_like(q)
        prod = dc.astype(single) * c.astype(single)
        dq = [None] * (count // 256)
        dk_t = []
        dv_t = []
        for h in range(2):
            dch = jnp.where(half[h], dc, zero)
            kh = jnp.where(half[h], k, zero)
            d = jnp.sum(jnp.where(half[h], prod, 0.0), -1, keepdims=True)
            dkh = None
            dvh = None
            for b in range(count // 256):
                rb = slice(b * 256, (b + 1) * 256)
                prob = pst[s_, h, rb, :]
                dp = dot_nt(dch[rb], v)
                ds = (prob.astype(single) * (dp - d[rb])).astype(narrow)
                o = dot(ds, kh)
                dq[b] = o if dq[b] is None else dq[b] + o
                hr = slice(h * 64, (h + 1) * 64)
                one = dot(q_t[hr, rb], ds)
                two = dot(dc_t[hr, rb], prob)
                dkh = one if dkh is None else dkh + one
                dvh = two if dvh is None else dvh + two
            dk_t.append(dkh)
            dv_t.append(dvh)
        for b in range(count // 256):
            mixed[at(g * count + b * 256, 256), c_q] = (dq[b] * 0.125).astype(narrow)
        mixed[r, c_k] = jnp.concatenate(dk_t, 0).T.astype(narrow)
        mixed[r, c_v] = jnp.concatenate(dv_t, 0).T.astype(narrow)

        @pl.when(i + 2 < n)
        def _():
            prob_load(i + 2, s_).start()

        return 0

    lax.fori_loop(0, n, attend, 0)

    l_x.wait()
    l_win.wait()
    for b in range(rows // slot):
        r = pl.ds(b * slot, slot)
        hid_t[:, r] = x_v[r, :].T
    stores[0].wait()

    def bias(b, total):
        r = at(b * 256, 256)
        return (
            total[0] + jnp.sum(mixed[r, :width].astype(single), 0, keepdims=True),
            total[1] + jnp.sum(mixed[r, 2 * width :].astype(single), 0, keepdims=True),
        )

    zero_row = jnp.zeros((1, width), single)
    q_sum, v_sum = lax.fori_loop(0, blocks, bias, (zero_row, zero_row))
    gsmall[0:1, :] = q_sum
    gsmall[1:2, :] = v_sum
    store(gsmall, gvec_o)
    for part in range(3):
        cols = pl.ds(part * width, width)
        buf = gst_a if part % 2 == 0 else gst_b
        if part == 2:
            pltpu.make_async_copy(gst_a, gin_o.at[:, pl.ds(0, width)], b_sem.at[0]).wait()

        def in_weigh(b, _, cols=cols, buf=buf):
            r = at(b * 256, 256)
            buf[r, :] = dot(hid_t[r, :], mixed[:, cols]).astype(narrow)
            return 0

        lax.fori_loop(0, width // 256, in_weigh, 0)
        pltpu.make_async_copy(buf, gin_o.at[:, cols], b_sem.at[part % 2]).start()

    def token_back(b, _):
        r = at(b * 256, 256)
        grad[r, :] += dot_nt(mixed[r, :], v_in[...])
        return 0

    lax.fori_loop(0, blocks, token_back, 0)
    store(grad, tok_o)
    for s in range(4):
        total = None
        for g in range(groups):
            long = flag[g] > 0
            r = pl.ds(g * count + s * slot, slot)
            if s == 0:
                other = grad[r, :]
                for o in range(1, 4):
                    other = other + grad[pl.ds(g * count + o * slot, slot), :]
                piece = jnp.where(long, grad[r, :], other)
            else:
                piece = jnp.where(long, grad[r, :], 0.0)
            total = piece if total is None else total + piece
        up_low[:, s * slot : (s + 1) * slot] = jnp.zeros_like(up_low[:, s * slot : (s + 1) * slot])
        up_low[:width, s * slot : (s + 1) * slot] = total.T.astype(narrow)
    store(up_low.at[pl.ds(0, width), pl.ds(0, count)], gtab_o)
    pltpu.make_async_copy(gst_b, gin_o.at[:, pl.ds(width, width)], b_sem.at[1]).wait()
    pltpu.make_async_copy(gst_a, gin_o.at[:, pl.ds(2 * width, width)], b_sem.at[0]).wait()
    for c in stores[1:]:
        c.wait()


def shapes_of(groups, count, width, ff):
    rows = groups * count
    pairs = width // 128
    wide = ff // width
    return dict(
        x=((rows, width), narrow),
        mixed=((rows, 3 * width), narrow),
        prob=((groups * pairs, 2, count, count), narrow),
        ctx=((rows, width), narrow),
        n1=((rows, width), single),
        r1=((rows, 128), single),
        act=((wide, rows, width), narrow),
        gp=((wide, rows, width), narrow),
        n2=((rows, width), single),
        r2=((rows, 128), single),
    )


def run_forward(groups, count, width, ff, lens, flag, vecs, tok, tab, weights):
    rows = groups * count
    saved = shapes_of(groups, count, width, ff)
    outs = [jax.ShapeDtypeStruct(*v) for v in saved.values()]
    outs.append(jax.ShapeDtypeStruct((groups * 4, width), single))
    spec_any = pl.BlockSpec(memory_space=ANY)
    spec_v = pl.BlockSpec(memory_space=VM)
    spec_s = pl.BlockSpec(memory_space=SM)
    dma = pltpu.SemaphoreType.DMA
    return pl.pallas_call(
        functools.partial(forward_kernel, (groups, count, width, ff)),
        out_shape=outs,
        in_specs=[spec_s, spec_s, spec_v] + [spec_any] * 6,
        out_specs=[spec_any] * 10 + [spec_v],
        scratch_shapes=[
            VM((width, 3 * width), narrow),
            VM((width, width), narrow),
            VM((width, ff), narrow),
            VM((ff, width), narrow),
            VM((count, width), narrow),
            VM((rows, width), narrow),
            VM((rows, 3 * width), narrow),
            VM((groups, count, count), single),
            VM((2, 2, count, count), narrow),
            VM((rows, width), narrow),
            VM((rows, width), single),
            VM((rows, width), narrow),
            VM((rows, width), single),
            VM((rows, 128), single),
            VM((rows, 128), single),
            VM((2, rows, width), narrow),
            VM((2, rows, width), narrow),
            VM((rows, width), single),
            dma((6,)), dma((8,)), dma((2,)), dma((2,)), dma((2,)),
        ],
        compiler_params=pltpu.CompilerParams(vmem_limit_bytes=LIMIT),
        cost_estimate=pl.CostEstimate(flops=2 * rows * width * (4 * width + 2 * ff), bytes_accessed=80 * 2**20, transcendentals=10**7),
        name="encoder_forward",
    )(lens, flag, vecs, tok, tab, *weights)


def run_backward(groups, count, width, ff, lens, flag, vecs, pooled_grad, weights, saved):
    rows = groups * count
    spec_any = pl.BlockSpec(memory_space=ANY)
    spec_v = pl.BlockSpec(memory_space=VM)
    spec_s = pl.BlockSpec(memory_space=SM)
    dma = pltpu.SemaphoreType.DMA
    return pl.pallas_call(
        functools.partial(backward_kernel, (groups, count, width, ff)),
        out_shape=[
            jax.ShapeDtypeStruct((rows, width), single),
            jax.ShapeDtypeStruct((width, 3 * width), narrow),
            jax.ShapeDtypeStruct((width, width), narrow),
            jax.ShapeDtypeStruct((width, ff), narrow),
            jax.ShapeDtypeStruct((width, ff), narrow),
            jax.ShapeDtypeStruct((width, count), narrow),
            jax.ShapeDtypeStruct((16, width), single),
        ],
        in_specs=[spec_s, spec_s, spec_v, spec_v] + [spec_any] * 14,
        out_specs=[spec_any] * 7,
        scratch_shapes=[
            VM((width, 3 * width), narrow),
            VM((width, width), narrow),
            VM((width, ff), narrow),
            VM((ff, width), narrow),
            VM((rows, width), narrow),
            VM((rows, 3 * width), narrow),
            VM((rows, width), narrow),
            VM((rows, width), single),
            VM((rows, width), single),
            VM((rows, 128), single),
            VM((rows, 128), single),
            VM((2, rows, width), narrow),
            VM((2, rows, width), narrow),
            VM((2, 2, count, count), narrow),
            VM((rows, width), narrow),
            VM((width, rows), narrow),
            VM((width, rows), narrow),
            VM((rows, width), narrow),
            VM((rows, width), single),
            VM((rows, width), narrow),
            VM((width, width), narrow),
            VM((width, width), narrow),
            VM((16, width), single),
            dma((11,)), dma((4,)), dma((2,)), dma((4,)), dma((2,)),
        ],
        compiler_params=pltpu.CompilerParams(vmem_limit_bytes=LIMIT),
        cost_estimate=pl.CostEstimate(flops=4 * rows * width * (4 * width + 2 * ff), bytes_accessed=100 * 2**20, transcendentals=0),
        name="encoder_backward",
    )(lens, flag, vecs, pooled_grad, *weights, *saved)


def normalize_rows(pooled):
    return pooled * lax.rsqrt(jnp.sum(pooled * pooled, -1, keepdims=True) + 1e-06)


def slot_roles(bucket):
    long_slot = jnp.repeat(jnp.repeat(bucket, 2), 4) > 0
    slots = jnp.arange(long_slot.shape[0], dtype=jnp.int32)
    within = slots % 4
    odd_group = slots // 4 % 2
    query = jnp.where(long_slot, (within == 0) & (odd_group == 0), within % 2 == 0)
    passage = jnp.where(long_slot, (within == 0) & (odd_group == 1), within % 2 == 1)
    partner = jnp.where(long_slot, slots + 4, slots + 1)
    return (query, passage, partner)


def contrast(every, own, start, rows, bucket):
    query, passage, partner = slot_roles(bucket)
    pair_count = jnp.sum(4 - 3 * bucket).astype(single)
    logits = jnp.einsum("id,jd->ij", every, every, preferred_element_type=single) * 100.0
    columns = jnp.arange(logits.shape[1], dtype=jnp.int32)
    masked = jnp.where(passage[None, :], logits, -1000000000.0)
    top = jnp.max(masked, -1, keepdims=True)
    raised = jnp.exp(masked - top)
    total = jnp.sum(raised, -1, keepdims=True)
    spread = top[:, 0] + jnp.log(total[:, 0])
    match = columns[None, :] == partner[:, None]
    positive = jnp.sum(jnp.where(match, logits, 0.0), -1)
    loss = jnp.sum(jnp.where(query, spread - positive, 0.0)) / pair_count
    row_weight = jnp.where(query, 1.0, 0.0) / pair_count
    logit_grad = (row_weight[:, None] * (raised / total - match.astype(single))).astype(narrow)
    by_row = lax.dynamic_slice_in_dim(logit_grad, start, rows, 0)
    by_column = lax.dynamic_slice_in_dim(logit_grad, start, rows, 1)
    both = jnp.dot(by_row, every, preferred_element_type=single) + jnp.einsum(
        "ij,id->jd", by_column, every, preferred_element_type=single
    )
    return loss, both * 100.0


def gather_weights(tab, w_in, w_out, w_up, w_down, small):
    gat = lambda a: lax.all_gather(a, "fsdp", axis=0, tiled=True)
    return lax.all_gather(tab, "fsdp", axis=1, tiled=True), gat(w_in), gat(w_out), gat(w_up), gat(w_down), gat(small)


def reduce_all(grads, small):
    done = []
    for a, axis in grads:
        part = lax.psum_scatter(a.astype(single), "fsdp", scatter_dimension=axis, tiled=True)
        done.append(lax.psum(part.astype(narrow), "dp").astype(single))
    return done, lax.psum(small, ("dp", "fsdp"))


def local(
    tokens, lengths, bucket, position_table, in_projection, query_bias, value_bias, out_projection, out_bias,
    first_gain, first_shift, up_projection, up_bias, down_projection, down_bias, second_gain, second_shift,
):
    groups = lengths.shape[0]
    width = tokens.shape[1]
    count = tokens.shape[0] // groups
    shards = lax.axis_size("fsdp")
    ff = up_projection.shape[1]
    fs = lax.axis_index("fsdp")
    device = lax.axis_index("dp") * shards + fs
    small_parts = (query_bias, value_bias, out_bias, first_gain, first_shift, down_bias, second_gain, second_shift)
    piece = query_bias.shape[0]
    wide_piece = up_bias.shape[0]
    small = jnp.concatenate(small_parts + (up_bias,))[None, :]
    table, w_in, w_out, w_up, w_down, small_all = gather_weights(
        position_table, in_projection, out_projection, up_projection, down_projection, small
    )
    heads = small_all[:, : 8 * piece].reshape(shards, 8, piece).transpose(1, 0, 2).reshape(8, width)
    vecs = jnp.concatenate(
        [heads, small_all[:, 8 * piece :].reshape(ff // width, width), jnp.zeros((8 - ff // width, width), narrow)]
    ).astype(single)
    flag = lax.dynamic_slice_in_dim(jnp.repeat(bucket, 2), device * groups, groups)
    weights = (w_in, w_out, w_up, w_down)
    *saved, pooled = run_forward(groups, count, width, ff, lengths, flag, vecs, tokens, table, weights)
    embedded, norm_grad = jax.vjp(normalize_rows, pooled)
    every = lax.all_gather(embedded.astype(narrow), ("dp", "fsdp"), axis=0, tiled=True)
    slots = groups * 4
    loss, embed_grad = contrast(every, embedded, device * slots, slots, bucket)
    pooled_grad = norm_grad(embed_grad)[0]
    tokens_grad, gin, gout, gup, gdown, gtab, gvec = run_backward(
        groups, count, width, ff, lengths, flag, vecs, pooled_grad, weights, saved
    )
    (gin, gout, gup, gdown, gtab), gvec = reduce_all(((gin, 0), (gout, 0), (gup, 0), (gdown, 1), (gtab, 0)), gvec)
    gdown = gdown.T
    gtab = gtab.T
    own = [lax.dynamic_slice_in_dim(gvec[i], fs * piece, piece) for i in range(8)]
    up_own = lax.dynamic_slice_in_dim(gvec[8 : 8 + ff // width].reshape(ff), fs * wide_piece, wide_piece)
    return (
        loss, pooled, tokens_grad, gtab, gin, own[0], own[1], gout, own[2], own[3], own[4], gup, up_own, gdown,
        own[5], own[6], own[7],
    )


def solution(mesh):
    rows = P(("dp", "fsdp"), None)
    vec = P("fsdp")
    mat = P("fsdp", None)
    in_specs = (rows, rows, P(), P(None, "fsdp"), mat, vec, vec, mat, vec, vec, vec, mat, vec, mat, vec, vec, vec)
    out_specs = (P(), rows, rows, P(None, "fsdp"), mat, vec, vec, mat, vec, vec, vec, mat, vec, mat, vec, vec, vec)
    return jax.shard_map(local, mesh=mesh, in_specs=in_specs, out_specs=out_specs, check_vma=False)
```

```python
import functools

import jax
import jax.numpy as jnp
from jax import lax
from jax.experimental import pallas as pl
from jax.experimental.pallas import tpu as pltpu
from jax.sharding import PartitionSpec as P

H = 12
narrow = jnp.bfloat16
single = jnp.float32
ANY = pl.ANY
VM = pltpu.VMEM
SM = pltpu.SMEM
LIMIT = 60 * 2**20


def dot(a, b):
    return lax.dot_general(a, b, (((1,), (0,)), ((), ())), preferred_element_type=single)


def dot_nt(a, b):
    return lax.dot_general(a, b, (((1,), (1,)), ((), ())), preferred_element_type=single)


def at(start, size):
    return pl.ds(pl.multiple_of(start, 128), size)


def gelu_pair(u):
    t = 1.0 / (1.0 + 0.23164189 * jnp.abs(u))
    e = jnp.exp(-0.5 * (u * u))
    tail = t * (
        0.127414796 + t * (-0.142248368 + t * (0.7107068705 + t * (-0.7265760135 + t * 0.5307027145)))
    )
    tail = tail * e
    phi = jnp.where(u < 0, tail, 1.0 - tail)
    return u * phi, phi + u * (e * 0.3989422804)


def norm_rows(value):
    mean = jnp.mean(value, -1, keepdims=True)
    centred = value - mean
    rstd = lax.rsqrt(jnp.mean(centred * centred, -1, keepdims=True) + 1e-06)
    return centred * rstd, rstd


def norm_back(grad, unit, rstd):
    one = jnp.mean(grad, -1, keepdims=True)
    two = jnp.mean(grad * unit, -1, keepdims=True)
    return rstd * (grad - one - unit * two)


def slot_lengths(lens, flag, g, along_rows, count, width):
    slot = count // 4
    shape = (count, width) if along_rows else (8, count)
    t = lax.broadcasted_iota(jnp.int32, shape, 0 if along_rows else 1)
    which = t // slot
    long = flag[g] > 0
    limit = jnp.where(which == 0, lens[g, 0], lens[g, 1])
    limit = jnp.where(which == 2, lens[g, 2], limit)
    limit = jnp.where(which == 3, lens[g, 3], limit)
    limit = jnp.where(long, lens[g, 0], limit)
    inside = jnp.where(long, t, t % slot)
    return which, inside < limit


def forward_kernel(
    sizes,
    lens, flag, vecs, tok, tab, w_in, w_out, w_up, w_down,
    x_o, mixed_o, prob_o, ctx_o, n1_o, r1_o, act_o, gp_o, n2_o, r2_o, pooled_o,
    v_in, v_out, v_up, v_down, tab_v, x_v, mixed, mask, pst, ctx, hid, hid_low, n_st, r1_v, r2_v, ast, gst, acc,
    in_sem, out_sem, p_sem, a_sem, g_sem,
):
    groups, count, width, ff = sizes
    rows = groups * count
    pairs = width // 128
    loads = [
        pltpu.make_async_copy(s, d, in_sem.at[i])
        for i, (s, d) in enumerate(
            ((tok, x_v), (tab, tab_v), (w_in, v_in), (w_out, v_out), (w_up, v_up), (w_down, v_down))
        )
    ]
    for c in loads:
        c.start()
    stores = []

    def store(src, dst):
        c = pltpu.make_async_copy(src, dst, out_sem.at[len(stores)])
        c.start()
        stores.append(c)

    def vec(i):
        return vecs[i : i + 1, :]

    loads[0].wait()
    loads[1].wait()
    slot = count // 4
    for g in range(groups):
        which_q, _ = slot_lengths(lens, flag, g, True, count, 128)
        which_k, live_k = slot_lengths(lens, flag, g, False, count, 128)
        long = flag[g] > 0
        wq = which_q[:, :1]
        open_ = live_k[:1] & (long | (wq == which_k[:1]))
        mask[g] = jnp.where(open_, 0.0, -1000000000.0).astype(single)
        for s in range(4):
            part = x_v[pl.ds(g * count + s * slot, slot), :].astype(single)
            place = jnp.where(long, tab_v[pl.ds(s * slot, slot), :].astype(single), tab_v[:slot, :].astype(single))
            both = part + place
            hid[pl.ds(g * count + s * slot, slot), :] = both
            x_v[pl.ds(g * count + s * slot, slot), :] = both.astype(narrow)
    store(x_v, x_o)

    loads[2].wait()
    for part in range(3):
        cols = pl.ds(part * width, width)

        def project(b, _, cols=cols, part=part):
            r = at(b * 256, 256)
            out = dot(x_v[r, :], v_in[:, cols])
            if part == 0:
                out = out + vec(0)
            if part == 2:
                out = out + vec(1)
            mixed[r, cols] = out.astype(narrow)
            return 0

        lax.fori_loop(0, rows // 256, project, 0)
    store(mixed, mixed_o)

    lane = lax.broadcasted_iota(jnp.int32, (count, 128), 1)
    half = (lane < 64, lane >= 64)

    def attend(i, _):
        g = i // pairs
        p = i % pairs
        s_ = i % 2
        r = at(g * count, count)

        @pl.when(i >= 2)
        def _():
            pltpu.make_async_copy(pst.at[s_], prob_o.at[i], p_sem.at[s_]).wait()

        q = mixed[r, at(p * 128, 128)]
        k = mixed[r, at(width + p * 128, 128)]
        v = mixed[r, at(2 * width + p * 128, 128)]
        zero = jnp.zeros_like(q)
        out = [None] * (count // 256)
        for h in range(2):
            qh = jnp.where(half[h], q, zero) * jnp.asarray(0.125, narrow)
            vh = jnp.where(half[h], v, zero)
            for b in range(count // 256):
                sc = dot_nt(qh[b * 256 : (b + 1) * 256], k) + mask[g, b * 256 : (b + 1) * 256, :]
                e = jnp.exp(sc - jnp.max(sc, -1, keepdims=True))
                low = (e * (1.0 / jnp.sum(e, -1, keepdims=True))).astype(narrow)
                pst[s_, h, b * 256 : (b + 1) * 256, :] = low
                o = dot(low, vh)
                out[b] = o if out[b] is None else out[b] + o
        for b in range(count // 256):
            ctx[at(g * count + b * 256, 256), at(p * 128, 128)] = out[b].astype(narrow)
        pltpu.make_async_copy(pst.at[s_], prob_o.at[i], p_sem.at[s_]).start()
        return 0

    n = groups * pairs
    lax.fori_loop(0, n, attend, 0)
    for i in range(max(n - 2, 0), n):
        pltpu.make_async_copy(pst.at[i % 2], prob_o.at[i], p_sem.at[i % 2]).wait()
    store(ctx, ctx_o)

    loads[3].wait()

    def first(b, _):
        r = at(b * 256, 256)
        total = hid[r, :] + dot(ctx[r, :], v_out[...]) + vec(2)
        unit, rstd = norm_rows(total)
        n_st[r, :] = unit
        r1_v[r, :] = jnp.broadcast_to(rstd, (256, 128))
        h = unit * vec(3) + vec(4)
        hid[r, :] = h
        hid_low[r, :] = h.astype(narrow)
        acc[r, :] = h + vec(5)
        return 0

    lax.fori_loop(0, rows // 256, first, 0)
    store(n_st, n1_o)
    store(r1_v, r1_o)

    loads[4].wait()
    loads[5].wait()
    wide = ff // width

    def act_copies(j, s_):
        return (
            pltpu.make_async_copy(ast.at[s_], act_o.at[j], a_sem.at[s_]),
            pltpu.make_async_copy(gst.at[s_], gp_o.at[j], g_sem.at[s_]),
        )

    for j in range(wide):
        s_ = j % 2
        if j >= 2:
            for c in act_copies(j - 2, s_):
                c.wait()
        cols = pl.ds(j * width, width)

        def feed(b, _, s_=s_, j=j, cols=cols):
            r = at(b * 256, 256)
            u = dot(hid_low[r, :], v_up[:, cols]) + vec(8 + j)
            a, d = gelu_pair(u)
            a = a.astype(narrow)
            ast[s_, r, :] = a
            gst[s_, r, :] = d.astype(narrow)
            acc[r, :] += dot(a, v_down[cols, :])
            return 0

        lax.fori_loop(0, rows // 256, feed, 0)
        for c in act_copies(j, s_):
            c.start()
    for j in range(max(wide - 2, 0), wide):
        for c in act_copies(j, j % 2):
            c.wait()

    stores[3].wait()
    for g in range(groups):
        _, live = slot_lengths(lens, flag, g, True, count, 128)
        sums = []
        for s in range(4):
            r = pl.ds(g * count + s * slot, slot)
            unit, rstd = norm_rows(acc[r, :])
            n_st[r, :] = unit
            r2_v[r, :] = jnp.broadcast_to(rstd, (slot, 128))
            out = unit * vec(6) + vec(7)
            keep = live[s * slot : (s + 1) * slot, :1]
            sums.append(jnp.sum(jnp.where(keep, out, 0.0), 0, keepdims=True))
        long = flag[g] > 0
        for s in range(4):
            div = jnp.maximum(lens[g, s], 1).astype(single)
            if s == 0:
                total = jnp.where(long, sums[0] + sums[1] + sums[2] + sums[3], sums[0])
            else:
                total = jnp.where(long, 0.0, sums[s])
            pooled_o[4 * g + s : 4 * g + s + 1, :] = total / div
    store(n_st, n2_o)
    store(r2_v, r2_o)
    for i, c in enumerate(stores):
        if i != 3:
            c.wait()


def backward_kernel(
    sizes,
    lens, flag, vecs, pg, w_in, w_out, w_up, w_down, x_i, mixed_i, prob_i, ctx_i, n1_i, r1_i, act_i, gp_i, n2_i, r2_i,
    tok_o, gin_o, gout_o, gup_o, gdown_o, gtab_o, gvec_o,
    v_in, v_out, v_up, v_down, x_v, mixed, ctx, n1, n2, r1_v, r2_v, ast, gst, pst, low, hid_t, up_low, grad, dctx, gst_a, gst_b, gsmall,
    in_sem, a_sem, p_sem, o_sem, b_sem,
):
    groups, count, width, ff = sizes
    rows = groups * count
    pairs = width // 128
    slot = count // 4
    wide = ff // width
    blocks = rows // 256
    loads = [
        pltpu.make_async_copy(s, d, in_sem.at[i])
        for i, (s, d) in enumerate(
            (
                (n2_i, n2), (r2_i, r2_v), (n1_i, n1), (w_down, v_down), (w_up, v_up), (r1_i, r1_v), (ctx_i, ctx),
                (w_out, v_out), (mixed_i, mixed), (x_i, x_v), (w_in, v_in),
            )
        )
    ]
    (l_n2, l_r2, l_n1, l_down, l_up, l_r1, l_ctx, l_wout, l_mixed, l_x, l_win) = loads

    def act_loads(j):
        return (
            pltpu.make_async_copy(act_i.at[j], ast.at[j % 2], a_sem.at[j % 2]),
            pltpu.make_async_copy(gp_i.at[j], gst.at[j % 2], a_sem.at[2 + j % 2]),
        )

    def prob_load(i, s_):
        return pltpu.make_async_copy(prob_i.at[i], pst.at[s_], p_sem.at[s_])

    l_n2.start()
    l_r2.start()
    for c in act_loads(0):
        c.start()
    for c in loads[2:5]:
        c.start()
    for c in act_loads(1):
        c.start()
    for c in loads[5:]:
        c.start()
    prob_load(0, 0).start()
    prob_load(1, 1).start()

    def vec(i):
        return vecs[i : i + 1, :]

    stores = []

    def store(src, dst):
        c = pltpu.make_async_copy(src, dst, o_sem.at[len(stores)])
        c.start()
        stores.append(c)

    l_n2.wait()
    l_r2.wait()
    gain_sum = jnp.zeros((1, width), single)
    shift_sum = jnp.zeros((1, width), single)
    bias_sum = jnp.zeros((1, width), single)
    for g in range(groups):
        _, live = slot_lengths(lens, flag, g, True, count, 128)
        long = flag[g] > 0
        for s in range(4):
            r = pl.ds(g * count + s * slot, slot)
            mine = pg[4 * g + s : 4 * g + s + 1, :] / jnp.maximum(lens[g, s], 1).astype(single)
            first = pg[4 * g : 4 * g + 1, :] / jnp.maximum(lens[g, 0], 1).astype(single)
            row = jnp.where(long, first, mine)
            keep = live[s * slot : (s + 1) * slot, :1]
            d = jnp.where(keep, row, 0.0)
            unit = n2[r, :]
            gain_sum = gain_sum + jnp.sum(d * unit, 0, keepdims=True)
            shift_sum = shift_sum + jnp.sum(d, 0, keepdims=True)
            back = norm_back(d * vec(6), unit, r2_v[r, :1])
            grad[r, :] = back
            lowered = back.astype(narrow)
            low[r, :] = lowered
            bias_sum = bias_sum + jnp.sum(lowered.astype(single), 0, keepdims=True)
    gsmall[...] = jnp.zeros_like(gsmall)
    gsmall[6:7, :] = gain_sum
    gsmall[7:8, :] = shift_sum
    gsmall[5:6, :] = bias_sum
    l_n1.wait()
    for b in range(rows // slot):
        r = pl.ds(b * slot, slot)
        hid_t[:, r] = (n1[r, :] * vec(3) + vec(4)).astype(narrow).T

    l_down.wait()
    l_up.wait()

    for j in range(wide):
        s_ = j % 2
        cols = pl.ds(j * width, width)
        for c in act_loads(j):
            c.wait()
        if j >= 1:
            pltpu.make_async_copy(gst_a, gdown_o.at[pl.ds((j - 1) * width, width), :], b_sem.at[0]).wait()
            pltpu.make_async_copy(gst_b, gup_o.at[:, pl.ds((j - 1) * width, width)], b_sem.at[1]).wait()

        def feed(b, total, s_=s_, cols=cols):
            r = at(b * 256, 256)
            up = (dot_nt(low[r, :], v_down[cols, :]) * gst[s_, r, :].astype(single)).astype(narrow)
            up_low[r, :] = up
            grad[r, :] += dot_nt(up, v_up[:, cols])
            return total + jnp.sum(up.astype(single), 0, keepdims=True)

        gsmall[8 + j : 9 + j, :] = lax.fori_loop(0, blocks, feed, jnp.zeros((1, width), single))

        def weigh(b, _, s_=s_):
            r = at(b * 256, 256)
            gst_a[r, :] = dot(ast[s_, :, r].T, low[...]).astype(narrow)
            gst_b[r, :] = dot(hid_t[r, :], up_low[...]).astype(narrow)
            return 0

        lax.fori_loop(0, width // 256, weigh, 0)
        pltpu.make_async_copy(gst_a, gdown_o.at[cols, :], b_sem.at[0]).start()
        pltpu.make_async_copy(gst_b, gup_o.at[:, cols], b_sem.at[1]).start()
        if j + 2 < wide:
            for c in act_loads(j + 2):
                c.start()

    l_r1.wait()
    l_ctx.wait()
    l_wout.wait()
    gain_sum = jnp.zeros((1, width), single)
    shift_sum = jnp.zeros((1, width), single)
    bias_sum = jnp.zeros((1, width), single)
    for b in range(rows // slot):
        r = pl.ds(b * slot, slot)
        d = grad[r, :]
        unit = n1[r, :]
        gain_sum = gain_sum + jnp.sum(d * unit, 0, keepdims=True)
        shift_sum = shift_sum + jnp.sum(d, 0, keepdims=True)
        back = norm_back(d * vec(3), unit, r1_v[r, :1])
        grad[r, :] = back
        lowered = back.astype(narrow)
        low[r, :] = lowered
        bias_sum = bias_sum + jnp.sum(lowered.astype(single), 0, keepdims=True)
        hid_t[:, r] = ctx[r, :].T
    gsmall[3:4, :] = gain_sum
    gsmall[4:5, :] = shift_sum
    gsmall[2:3, :] = bias_sum
    last = pl.ds((wide - 1) * width, width)
    pltpu.make_async_copy(gst_a, gdown_o.at[last, :], b_sem.at[0]).wait()
    pltpu.make_async_copy(gst_b, gup_o.at[:, last], b_sem.at[1]).wait()

    def out_weigh(b, _):
        r = at(b * 256, 256)
        gst_a[r, :] = dot(hid_t[r, :], low[...]).astype(narrow)
        return 0

    lax.fori_loop(0, width // 256, out_weigh, 0)
    store(gst_a, gout_o)

    def context_back(b, _):
        r = at(b * 256, 256)
        dctx[r, :] = dot_nt(low[r, :], v_out[...]).astype(narrow)
        return 0

    lax.fori_loop(0, blocks, context_back, 0)

    l_mixed.wait()
    lane = lax.broadcasted_iota(jnp.int32, (count, 128), 1)
    half = (lane < 64, lane >= 64)
    scale = jnp.asarray(0.125, narrow)
    n = groups * pairs

    def attend(i, _):
        g = i // pairs
        p = i % pairs
        s_ = i % 2
        r = at(g * count, count)
        prob_load(i, s_).wait()
        c_q = at(p * 128, 128)
        c_k = at(width + p * 128, 128)
        c_v = at(2 * width + p * 128, 128)
        q = mixed[r, c_q] * scale
        k = mixed[r, c_k]
        v = mixed[r, c_v]
        dc = dctx[r, c_q]
        c = ctx[r, c_q]
        q_t = q.T
        dc_t = dc.T
        zero = jnp.zeros_like(q)
        prod = dc.astype(single) * c.astype(single)
        dq = [None] * (count // 256)
        dk_t = []
        dv_t = []
        for h in range(2):
            dch = jnp.where(half[h], dc, zero)
            kh = jnp.where(half[h], k, zero)
            d = jnp.sum(jnp.where(half[h], prod, 0.0), -1, keepdims=True)
            dkh = None
            dvh = None
            for b in range(count // 256):
                rb = slice(b * 256, (b + 1) * 256)
                prob = pst[s_, h, rb, :]
                dp = dot_nt(dch[rb], v)
                ds = (prob.astype(single) * (dp - d[rb])).astype(narrow)
                o = dot(ds, kh)
                dq[b] = o if dq[b] is None else dq[b] + o
                hr = slice(h * 64, (h + 1) * 64)
                one = dot(q_t[hr, rb], ds)
                two = dot(dc_t[hr, rb], prob)
                dkh = one if dkh is None else dkh + one
                dvh = two if dvh is None else dvh + two
            dk_t.append(dkh)
            dv_t.append(dvh)
        for b in range(count // 256):
            mixed[at(g * count + b * 256, 256), c_q] = (dq[b] * 0.125).astype(narrow)
        mixed[r, c_k] = jnp.concatenate(dk_t, 0).T.astype(narrow)
        mixed[r, c_v] = jnp.concatenate(dv_t, 0).T.astype(narrow)

        @pl.when(i + 2 < n)
        def _():
            prob_load(i + 2, s_).start()

        return 0

    lax.fori_loop(0, n, attend, 0)

    l_x.wait()
    l_win.wait()
    for b in range(rows // slot):
        r = pl.ds(b * slot, slot)
        hid_t[:, r] = x_v[r, :].T
    stores[0].wait()

    def bias(b, total):
        r = at(b * 256, 256)
        return (
            total[0] + jnp.sum(mixed[r, :width].astype(single), 0, keepdims=True),
            total[1] + jnp.sum(mixed[r, 2 * width :].astype(single), 0, keepdims=True),
        )

    zero_row = jnp.zeros((1, width), single)
    q_sum, v_sum = lax.fori_loop(0, blocks, bias, (zero_row, zero_row))
    gsmall[0:1, :] = q_sum
    gsmall[1:2, :] = v_sum
    store(gsmall, gvec_o)
    for part in range(3):
        cols = pl.ds(part * width, width)
        buf = gst_a if part % 2 == 0 else gst_b
        if part == 2:
            pltpu.make_async_copy(gst_a, gin_o.at[:, pl.ds(0, width)], b_sem.at[0]).wait()

        def in_weigh(b, _, cols=cols, buf=buf):
            r = at(b * 256, 256)
            buf[r, :] = dot(hid_t[r, :], mixed[:, cols]).astype(narrow)
            return 0

        lax.fori_loop(0, width // 256, in_weigh, 0)
        pltpu.make_async_copy(buf, gin_o.at[:, cols], b_sem.at[part % 2]).start()

    def token_back(b, _):
        r = at(b * 256, 256)
        grad[r, :] += dot_nt(mixed[r, :], v_in[...])
        return 0

    lax.fori_loop(0, blocks, token_back, 0)
    store(grad, tok_o)
    for s in range(4):
        total = None
        for g in range(groups):
            long = flag[g] > 0
            r = pl.ds(g * count + s * slot, slot)
            if s == 0:
                other = grad[r, :]
                for o in range(1, 4):
                    other = other + grad[pl.ds(g * count + o * slot, slot), :]
                piece = jnp.where(long, grad[r, :], other)
            else:
                piece = jnp.where(long, grad[r, :], 0.0)
            total = piece if total is None else total + piece
        up_low[:, s * slot : (s + 1) * slot] = jnp.zeros_like(up_low[:, s * slot : (s + 1) * slot])
        up_low[:width, s * slot : (s + 1) * slot] = total.T.astype(narrow)
    store(up_low.at[pl.ds(0, width), pl.ds(0, count)], gtab_o)
    pltpu.make_async_copy(gst_b, gin_o.at[:, pl.ds(width, width)], b_sem.at[1]).wait()
    pltpu.make_async_copy(gst_a, gin_o.at[:, pl.ds(2 * width, width)], b_sem.at[0]).wait()
    for c in stores[1:]:
        c.wait()


def shapes_of(groups, count, width, ff):
    rows = groups * count
    pairs = width // 128
    wide = ff // width
    return dict(
        x=((rows, width), narrow),
        mixed=((rows, 3 * width), narrow),
        prob=((groups * pairs, 2, count, count), narrow),
        ctx=((rows, width), narrow),
        n1=((rows, width), single),
        r1=((rows, 128), single),
        act=((wide, rows, width), narrow),
        gp=((wide, rows, width), narrow),
        n2=((rows, width), single),
        r2=((rows, 128), single),
    )


def run_forward(groups, count, width, ff, lens, flag, vecs, tok, tab, weights):
    rows = groups * count
    saved = shapes_of(groups, count, width, ff)
    outs = [jax.ShapeDtypeStruct(*v) for v in saved.values()]
    outs.append(jax.ShapeDtypeStruct((groups * 4, width), single))
    spec_any = pl.BlockSpec(memory_space=ANY)
    spec_v = pl.BlockSpec(memory_space=VM)
    spec_s = pl.BlockSpec(memory_space=SM)
    dma = pltpu.SemaphoreType.DMA
    return pl.pallas_call(
        functools.partial(forward_kernel, (groups, count, width, ff)),
        out_shape=outs,
        in_specs=[spec_s, spec_s, spec_v] + [spec_any] * 6,
        out_specs=[spec_any] * 10 + [spec_v],
        scratch_shapes=[
            VM((width, 3 * width), narrow),
            VM((width, width), narrow),
            VM((width, ff), narrow),
            VM((ff, width), narrow),
            VM((count, width), narrow),
            VM((rows, width), narrow),
            VM((rows, 3 * width), narrow),
            VM((groups, count, count), single),
            VM((2, 2, count, count), narrow),
            VM((rows, width), narrow),
            VM((rows, width), single),
            VM((rows, width), narrow),
            VM((rows, width), single),
            VM((rows, 128), single),
            VM((rows, 128), single),
            VM((2, rows, width), narrow),
            VM((2, rows, width), narrow),
            VM((rows, width), single),
            dma((6,)), dma((8,)), dma((2,)), dma((2,)), dma((2,)),
        ],
        compiler_params=pltpu.CompilerParams(vmem_limit_bytes=LIMIT),
        cost_estimate=pl.CostEstimate(flops=2 * rows * width * (4 * width + 2 * ff), bytes_accessed=80 * 2**20, transcendentals=10**7),
        name="encoder_forward",
    )(lens, flag, vecs, tok, tab, *weights)


def run_backward(groups, count, width, ff, lens, flag, vecs, pooled_grad, weights, saved):
    rows = groups * count
    spec_any = pl.BlockSpec(memory_space=ANY)
    spec_v = pl.BlockSpec(memory_space=VM)
    spec_s = pl.BlockSpec(memory_space=SM)
    dma = pltpu.SemaphoreType.DMA
    return pl.pallas_call(
        functools.partial(backward_kernel, (groups, count, width, ff)),
        out_shape=[
            jax.ShapeDtypeStruct((rows, width), single),
            jax.ShapeDtypeStruct((width, 3 * width), narrow),
            jax.ShapeDtypeStruct((width, width), narrow),
            jax.ShapeDtypeStruct((width, ff), narrow),
            jax.ShapeDtypeStruct((ff, width), narrow),
            jax.ShapeDtypeStruct((width, count), narrow),
            jax.ShapeDtypeStruct((16, width), single),
        ],
        in_specs=[spec_s, spec_s, spec_v, spec_v] + [spec_any] * 14,
        out_specs=[spec_any] * 7,
        scratch_shapes=[
            VM((width, 3 * width), narrow),
            VM((width, width), narrow),
            VM((width, ff), narrow),
            VM((ff, width), narrow),
            VM((rows, width), narrow),
            VM((rows, 3 * width), narrow),
            VM((rows, width), narrow),
            VM((rows, width), single),
            VM((rows, width), single),
            VM((rows, 128), single),
            VM((rows, 128), single),
            VM((2, rows, width), narrow),
            VM((2, rows, width), narrow),
            VM((2, 2, count, count), narrow),
            VM((rows, width), narrow),
            VM((width, rows), narrow),
            VM((rows, width), narrow),
            VM((rows, width), single),
            VM((rows, width), narrow),
            VM((width, width), narrow),
            VM((width, width), narrow),
            VM((16, width), single),
            dma((11,)), dma((4,)), dma((2,)), dma((4,)), dma((2,)),
        ],
        compiler_params=pltpu.CompilerParams(vmem_limit_bytes=LIMIT),
        cost_estimate=pl.CostEstimate(flops=4 * rows * width * (4 * width + 2 * ff), bytes_accessed=100 * 2**20, transcendentals=0),
        name="encoder_backward",
    )(lens, flag, vecs, pooled_grad, *weights, *saved)


def normalize_rows(pooled):
    return pooled * lax.rsqrt(jnp.sum(pooled * pooled, -1, keepdims=True) + 1e-06)


def slot_roles(bucket):
    long_slot = jnp.repeat(jnp.repeat(bucket, 2), 4) > 0
    slots = jnp.arange(long_slot.shape[0], dtype=jnp.int32)
    within = slots % 4
    odd_group = slots // 4 % 2
    query = jnp.where(long_slot, (within == 0) & (odd_group == 0), within % 2 == 0)
    passage = jnp.where(long_slot, (within == 0) & (odd_group == 1), within % 2 == 1)
    partner = jnp.where(long_slot, slots + 4, slots + 1)
    return (query, passage, partner)


def contrast(every, own, start, rows, bucket):
    query, passage, partner = slot_roles(bucket)
    pair_count = jnp.sum(4 - 3 * bucket).astype(single)
    logits = jnp.einsum("id,jd->ij", every, every, preferred_element_type=single) * 100.0
    columns = jnp.arange(logits.shape[1], dtype=jnp.int32)
    masked = jnp.where(passage[None, :], logits, -1000000000.0)
    top = jnp.max(masked, -1, keepdims=True)
    raised = jnp.exp(masked - top)
    total = jnp.sum(raised, -1, keepdims=True)
    spread = top[:, 0] + jnp.log(total[:, 0])
    match = columns[None, :] == partner[:, None]
    positive = jnp.sum(jnp.where(match, logits, 0.0), -1)
    loss = jnp.sum(jnp.where(query, spread - positive, 0.0)) / pair_count
    row_weight = jnp.where(query, 1.0, 0.0) / pair_count
    logit_grad = (row_weight[:, None] * (raised / total - match.astype(single))).astype(narrow)
    by_row = lax.dynamic_slice_in_dim(logit_grad, start, rows, 0)
    by_column = lax.dynamic_slice_in_dim(logit_grad, start, rows, 1)
    both = jnp.dot(by_row, every, preferred_element_type=single) + jnp.einsum(
        "ij,id->jd", by_column, every, preferred_element_type=single
    )
    return loss, both * 100.0


MESH = pl.DeviceIdType.MESH


def place():
    dp, fs = lax.axis_index("dp"), lax.axis_index("fsdp")
    return dp % 2, dp // 2, fs // 2, fs % 2


def device_at(x, y, z, c):
    return (y * 2 + x, z * 2 + c)


class Wires:
    def __init__(self, send, recv):
        self.send, self.recv, self.next, self.sent = send, recv, 0, []

    def copy(self, src, dst, device):
        i = self.next
        self.next += 1
        made = pltpu.make_async_remote_copy(
            src_ref=src, dst_ref=dst, send_sem=self.send.at[i], recv_sem=self.recv.at[i],
            device_id=device, device_id_type=MESH,
        )
        made.start()
        self.sent.append(made)
        return made

    def finish(self):
        for made in self.sent:
            made.wait_send()


def greet(devices):
    barrier = pltpu.get_barrier_semaphore()
    for d in devices:
        pl.semaphore_signal(barrier, inc=1, device_id=d, device_id_type=MESH)
    pl.semaphore_wait(barrier, len(devices))


def neighbours(small_too):
    x, y, z, c = place()
    found = [device_at(1 - x, y, z, c), device_at(x, 1 - y, z, c), device_at(x, y, z, 1 - c)]
    for k in (1, 2, 3):
        found.append(device_at(x, y, (z + k) % 4, c))
        if small_too:
            found.append(device_at(x, y, (z + k) % 4, 1 - c))
    return found


class Gather:
    def __init__(self, wires, shard, full, route):
        self.w, self.shard, self.full, self.route = wires, shard, full, route
        self.rows, self.cols = shard.shape
        self.x, self.y, self.z, self.c = place()

    def piece(self, ref, fs, a, b, part=None):
        hr, hc = self.rows // 2, self.cols // 2
        start = a * hr if fs is None else fs * self.rows + a * hr
        if part is not None:
            hr = hr // 2
            start = start + part * hr
        return ref.at[pl.ds(pl.multiple_of(start, 16), hr), pl.ds(pl.multiple_of(b * hc, 128), hc)]

    def whole(self, fs):
        return self.full.at[pl.ds(pl.multiple_of(fs * self.rows, 16), self.rows), :]

    def start(self, local_sem):
        x, y, z, c = self.x, self.y, self.z, self.c
        mine = 2 * z + c
        self.local = pltpu.make_async_copy(self.shard, self.whole(mine), local_sem)
        self.local.start()
        self.by_z = [
            self.w.copy(self.piece(self.shard, None, x, y), self.piece(self.full, mine, x, y), device_at(x, y, (z + k) % 4, c))
            for k in (1, 2, 3)
        ]
        self.by_core = [self.w.copy(self.shard, self.whole(mine), device_at(x, y, z, 1 - c))]

    def plane(self):
        x, y, z, c = self.x, self.y, self.z, self.c
        self.by_x, self.by_y = [], []
        for k in (1, 2, 3):
            self.by_z[k - 1].wait_recv()
            mine = self.piece(self.full, 2 * ((z - k) % 4) + c, x, y)
            self.by_x.append(self.w.copy(mine, mine, device_at(1 - x, y, z, c)))
            self.by_y.append(self.w.copy(mine, mine, device_at(x, 1 - y, z, c)))

    def diagonal(self):
        x, y, z, c = self.x, self.y, self.z, self.c
        self.by_corner = []
        for k in (1, 2, 3):
            fs = 2 * ((z - k) % 4) + c
            self.by_x[k - 1].wait_recv()
            self.by_y[k - 1].wait_recv()
            way = self.route[k - 1]
            if way == "x":
                got = self.piece(self.full, fs, 1 - x, y)
                self.by_corner.append(self.w.copy(got, got, device_at(x, 1 - y, z, c)))
            elif way == "y":
                got = self.piece(self.full, fs, x, 1 - y)
                self.by_corner.append(self.w.copy(got, got, device_at(1 - x, y, z, c)))
            else:
                got = self.piece(self.full, fs, 1 - x, y, 0)
                self.by_corner.append(self.w.copy(got, got, device_at(x, 1 - y, z, c)))
                got = self.piece(self.full, fs, x, 1 - y, 1)
                self.by_corner.append(self.w.copy(got, got, device_at(1 - x, y, z, c)))

    def core(self):
        x, y, z, c = self.x, self.y, self.z, self.c
        for made in self.by_corner:
            made.wait_recv()
        for k in (1, 2, 3):
            fs = 2 * ((z - k) % 4) + c
            self.by_core.append(self.w.copy(self.whole(fs), self.whole(fs), device_at(x, y, z, 1 - c)))

    def finish(self):
        for made in self.by_core:
            made.wait_recv()
        self.local.wait()


ROUTES = (("x", "y", "x"), ("x", "y", "y"), ("x", "y", "x"), ("x", "y", "y"), ("x", "y", "both"))


def gather_kernel(count, small, *refs):
    shards, fulls = refs[:count], refs[count + 1 : 2 * count + 1]
    small_all = refs[count]
    send, recv, local_sems = refs[2 * count + 1 :]
    x, y, z, c = place()
    greet(neighbours(True))
    wires = Wires(send, recv)
    mine = 2 * z + c
    keep = pltpu.make_async_copy(small, small_all.at[mine], local_sems.at[count])
    keep.start()
    little = [
        wires.copy(small, small_all.at[mine], device_at(x, y, (z + k) % 4, (c + j) % 2))
        for k in range(4)
        for j in range(2)
        if (k, j) != (0, 0)
    ]
    work = [Gather(wires, shards[i], fulls[i], ROUTES[i]) for i in range(count)]
    for t in range(count + 3):
        if t < count:
            work[t].start(local_sems.at[t])
        for stage, back in (("plane", 1), ("diagonal", 2), ("core", 3)):
            if 0 <= t - back < count:
                getattr(work[t - back], stage)()
    for g in work:
        g.finish()
    for made in little:
        made.wait_recv()
    keep.wait()
    wires.finish()


def run_gather(small, shards):
    count = len(shards)
    n_small = 7
    copies = n_small + sum(3 + 6 + len([w for w in r]) + ("both" in r) + 4 for r in ROUTES[:count])
    spec = pl.BlockSpec(memory_space=ANY)
    dma = pltpu.SemaphoreType.DMA
    return pl.pallas_call(
        functools.partial(gather_kernel, count),
        out_shape=[jax.ShapeDtypeStruct((8,) + small.shape, small.dtype)]
        + [jax.ShapeDtypeStruct((8 * s.shape[0], s.shape[1]), s.dtype) for s in shards],
        in_specs=[spec] * (count + 1),
        out_specs=[spec] * (count + 1),
        scratch_shapes=[dma((copies,)), dma((copies,)), dma((count + 1,))],
        compiler_params=pltpu.CompilerParams(collective_id=1, has_side_effects=True),
        name="gather_weights",
    )(small, *shards)


class Reduce:
    def __init__(self, wires, grad, own, from_core, b1x, b1y, b2x, b2y, from_z, final, sem):
        self.w, self.grad, self.own, self.from_core = wires, grad, own, from_core
        self.b1x, self.b1y, self.b2x, self.b2y, self.from_z, self.final, self.sem = b1x, b1y, b2x, b2y, from_z, final, sem
        _, self.rows, self.cols = own.shape
        self.x, self.y, self.z, self.c = place()

    def rh(self, a):
        return pl.ds(pl.multiple_of(a * (self.rows // 2), 16), self.rows // 2)

    def ch(self, b):
        return pl.ds(pl.multiple_of(b * (self.cols // 2), 128), self.cols // 2)

    def add(self, zs, row0, rows, cols, other, step=48):
        blocks = rows // step

        def body(i, _):
            zi = i // blocks
            r = i % blocks * step
            mine = (zs[0] + zi, pl.ds(pl.multiple_of(row0 + r, 16), step), cols)
            theirs = other[zi, pl.ds(pl.multiple_of(r, 16), step), :]
            self.own[mine] = (self.own[mine].astype(single) + theirs.astype(single)).astype(narrow)
            return 0

        lax.fori_loop(0, len(zs) * blocks, body, 0)

    def start(self):
        x, y, z, c = self.x, self.y, self.z, self.c
        self.keep = pltpu.make_async_copy(self.grad.at[:, c], self.own, self.sem)
        self.keep.start()
        self.s0 = self.w.copy(self.grad.at[:, 1 - c], self.from_core, device_at(x, y, z, 1 - c))

    def first(self):
        x, y, z, c = self.x, self.y, self.z, self.c
        self.keep.wait()
        self.s0.wait_recv()
        self.add((0, 1, 2, 3), 0, self.rows, slice(None), self.from_core)
        lo, hi = pl.ds(0, 2), pl.ds(2, 2)
        self.s1 = (
            self.w.copy(self.own.at[lo, self.rh(1 - x), :], self.b1x, device_at(1 - x, y, z, c)),
            self.w.copy(self.own.at[hi, :, self.ch(1 - y)], self.b1y, device_at(x, 1 - y, z, c)),
        )

    def second(self):
        x, y, z, c = self.x, self.y, self.z, self.c
        for s in self.s1:
            s.wait_recv()
        self.add((0, 1), x * (self.rows // 2), self.rows // 2, slice(None), self.b1x)
        self.add((2, 3), 0, self.rows, self.ch(y), self.b1y)
        lo, hi = pl.ds(0, 2), pl.ds(2, 2)
        self.s2 = (
            self.w.copy(self.own.at[lo, self.rh(x), self.ch(1 - y)], self.b2y, device_at(x, 1 - y, z, c)),
            self.w.copy(self.own.at[hi, self.rh(1 - x), self.ch(y)], self.b2x, device_at(1 - x, y, z, c)),
        )

    def third(self):
        x, y, z, c = self.x, self.y, self.z, self.c
        for s in self.s2:
            s.wait_recv()
        self.add((0, 1), x * (self.rows // 2), self.rows // 2, self.ch(y), self.b2y)
        self.add((2, 3), x * (self.rows // 2), self.rows // 2, self.ch(y), self.b2x)
        self.s3 = [
            self.w.copy(self.own.at[(z + k) % 4, self.rh(x), self.ch(y)], self.from_z.at[k - 1], device_at(x, y, (z + k) % 4, c))
            for k in (1, 2, 3)
        ]

    def fourth(self):
        x, y, z, c = self.x, self.y, self.z, self.c
        for s in self.s3:
            s.wait_recv()
        half = self.rows // 2

        def body(i, _):
            r = pl.ds(pl.multiple_of(i * 48, 16), 48)
            mine = pl.ds(pl.multiple_of(x * half + i * 48, 16), 48)
            total = self.own[z, mine, self.ch(y)].astype(single)
            for k in range(3):
                total = total + self.from_z[k, r, :].astype(single)
            self.final[mine, self.ch(y)] = total.astype(narrow)
            return 0

        lax.fori_loop(0, half // 48, body, 0)
        mine = self.final.at[self.rh(x), self.ch(y)]
        self.s4 = [
            self.w.copy(mine, mine, device_at(1 - x, y, z, c)),
            self.w.copy(mine, mine, device_at(x, 1 - y, z, c)),
            self.w.copy(mine, mine, device_at(1 - x, 1 - y, z, c)),
        ]

    def finish(self, out):
        for s in self.s4:
            s.wait_recv()

        def body(i, _):
            r = pl.ds(pl.multiple_of(i * 48, 16), 48)
            out[r, :] = self.final[r, :].astype(single)
            return 0

        lax.fori_loop(0, self.rows // 48, body, 0)


class ReduceSmall:
    def __init__(self, wires, total, got):
        self.w, self.total, self.got = wires, total, got

    def send(self, i, device):
        return self.w.copy(self.total.at[i], self.got.at[i], device)

    def start(self):
        x, y, z, c = place()
        self.s = self.send(0, device_at(x, y, z, 1 - c))

    def step(self, i):
        x, y, z, c = place()
        self.s.wait_recv()
        self.total[i + 1] = self.total[i] + self.got[i]
        if i == 0:
            self.s = self.send(1, device_at(1 - x, y, z, c))
        elif i == 1:
            self.s = self.send(2, device_at(x, 1 - y, z, c))
        else:
            self.last = [
                self.w.copy(self.total.at[3], self.got.at[2 + k], device_at(x, y, (z + k) % 4, c)) for k in (1, 2, 3)
            ]

    def finish(self, out):
        for s in self.last:
            s.wait_recv()
        x, y, z, c = place()
        out[...] = jnp.zeros_like(out)
        for i in range(4):
            term = jnp.zeros_like(out)
            for k in range(4):
                part = self.total[3] if k == 0 else self.got[2 + k]
                term = jnp.where((z - k + 4) % 4 == i, part, term)
            out[...] = out[...] + term


def reduce_kernel(count, small, *refs):
    grads, outs, rest = refs[:count], refs[count : 2 * count + 1], refs[2 * count + 1 :]
    total, got, send, recv, sems = rest[:5]
    scratch = rest[5:]
    x, y, z, c = place()
    wires = Wires(send, recv)
    greet(neighbours(False) + [device_at(1 - x, 1 - y, z, c)])
    work = [Reduce(wires, grads[i], *scratch[8 * i : 8 * i + 8], sems.at[i]) for i in range(count)]
    total[0] = small[...]
    tiny = ReduceSmall(wires, total, got)
    for w in work:
        w.start()
    tiny.start()
    for t in range(count + 4):
        for stage, back in (("first", 0), ("second", 1), ("third", 2), ("fourth", 3)):
            if 0 <= t - back < count:
                getattr(work[t - back], stage)()
        if 0 <= t - 4 < count:
            work[t - 4].finish(outs[t - 4])
        if t < 3:
            tiny.step(t)
    tiny.finish(outs[count])
    wires.finish()


def run_reduce(grads, small):
    count = len(grads)
    spec = pl.BlockSpec(memory_space=ANY)
    spec_v = pl.BlockSpec(memory_space=VM)
    dma = pltpu.SemaphoreType.DMA
    scratch = []
    for g in grads:
        _, _, r, k = g.shape
        scratch += [
            VM((4, r, k), narrow), VM((4, r, k), narrow), VM((2, r // 2, k), narrow), VM((2, r, k // 2), narrow),
            VM((2, r // 2, k // 2), narrow), VM((2, r // 2, k // 2), narrow), VM((3, r // 2, k // 2), narrow),
            VM((r, k), narrow),
        ]
    copies = 11 * count + 6
    return pl.pallas_call(
        functools.partial(reduce_kernel, count),
        out_shape=[jax.ShapeDtypeStruct(g.shape[2:], single) for g in grads] + [jax.ShapeDtypeStruct(small.shape, single)],
        in_specs=[spec_v] + [spec] * count,
        out_specs=[spec_v] * (count + 1),
        scratch_shapes=[
            VM((4,) + small.shape, single), VM((6,) + small.shape, single), dma((copies,)), dma((copies,)), dma((count,)),
        ] + scratch,
        compiler_params=pltpu.CompilerParams(collective_id=2, has_side_effects=True, vmem_limit_bytes=LIMIT),
        name="reduce_gradients",
    )(small, *grads)


def contrast_kernel(slots, buckets, bucket, pooled, loss_o, grad_o, mine, every, full, send, recv, sem):
    x, y, z, c = place()
    device = (y * 2 + x) * 8 + 2 * z + c
    greet(neighbours(False))
    wires = Wires(send, recv)
    p = pooled[...]
    scale = lax.rsqrt(jnp.sum(p * p, -1, keepdims=True) + 1e-06)
    e = p * scale
    width = e.shape[1]
    hw = width // 2
    mine[...] = jnp.concatenate([e[:, :hw], e[:, hw:]], 0).astype(narrow)

    def slot_of(xx, yy, zz):
        return (yy * 2 + xx) * 8 + 2 * zz + c

    def block(xx, yy, zz):
        return every.at[slot_of(xx, yy, zz)]

    keep = pltpu.make_async_copy(mine, every.at[device], sem)
    keep.start()
    by_x = wires.copy(mine, block(x, y, z), device_at(1 - x, y, z, c))
    by_y = [wires.copy(mine, block(x, y, z), device_at(x, 1 - y, z, c))]
    by_z = [wires.copy(mine, block(x, y, z), device_at(x, y, (z + k) % 4, c)) for k in (1, 2, 3)]
    by_x.wait_recv()
    by_y.append(wires.copy(block(1 - x, y, z), block(1 - x, y, z), device_at(x, 1 - y, z, c)))
    by_z += [wires.copy(block(1 - x, y, z), block(1 - x, y, z), device_at(x, y, (z + k) % 4, c)) for k in (1, 2, 3)]
    for s in by_y:
        s.wait_recv()
    for xx in (x, 1 - x):
        by_z += [
            wires.copy(block(xx, 1 - y, z), block(xx, 1 - y, z), device_at(x, y, (z + k) % 4, c)) for k in (1, 2, 3)
        ]
    pair_size = 8

    def long_of(shape, axis):
        pair = lax.broadcasted_iota(jnp.int32, shape, axis) // pair_size
        found = jnp.zeros(shape, jnp.int32)
        for b in range(buckets):
            found = jnp.where(pair == b, bucket[b], found)
        return found > 0

    def roles(shape, axis):
        t = lax.broadcasted_iota(jnp.int32, shape, axis)
        long = long_of(shape, axis)
        within, odd = t % 4, t // 4 % 2
        query = jnp.where(long, jnp.where((within == 0) & (odd == 0), 1, 0), jnp.where(within % 2 == 0, 1, 0))
        passage = jnp.where(long, jnp.where((within == 0) & (odd == 1), 1, 0), jnp.where(within % 2 == 1, 1, 0))
        return query > 0, passage > 0, jnp.where(long, t + 4, t + 1)

    _, passage, _ = roles((8, slots), 1)
    query, _, partner = roles((slots, 128), 0)
    passage, query, partner = passage[:1], query[:, :1], partner[:, :1]
    pair_count = jnp.zeros((), single)
    for b in range(buckets):
        pair_count = pair_count + (4 - 3 * bucket[b]).astype(single)
    keep.wait()
    for s in by_z:
        s.wait_recv()
    others = []
    for yy in range(2):
        for xx in range(2):
            for zz in range(4):
                others.append(wires.copy(block(xx, yy, zz), block(xx, yy, zz), device_at(x, y, z, 1 - c)))
    for s in others:
        s.wait_recv()
    both = every[...].astype(single)
    left = both[:, :8, :].reshape(slots, hw).astype(narrow)
    right = both[:, 8:, :].reshape(slots, hw).astype(narrow)
    logits = (dot_nt(left, left) + dot_nt(right, right)) * 100.0
    masked = jnp.where(passage, logits, -1000000000.0)
    top = jnp.max(masked, -1, keepdims=True)
    raised = jnp.exp(masked - top)
    total = jnp.sum(raised, -1, keepdims=True)
    match = lax.broadcasted_iota(jnp.int32, (slots, slots), 1) == partner
    positive = jnp.sum(jnp.where(match, logits, 0.0), -1, keepdims=True)
    terms = jnp.where(query, top + jnp.log(total) - positive, 0.0)
    loss = jnp.sum(terms, 0, keepdims=True) / pair_count
    loss_o[...] = jnp.broadcast_to(loss, loss_o.shape)
    weight = jnp.where(query, 1.0, 0.0) / pair_count
    logit_grad = weight * (raised / total - jnp.where(match, 1.0, 0.0))
    by_row = logit_grad.astype(narrow)
    by_column = logit_grad.T.astype(narrow)
    full[:, :hw] = dot(by_row, left) + dot(by_column, left)
    full[:, hw:] = dot(by_row, right) + dot(by_column, right)
    g = full[pl.ds(pl.multiple_of(device * 8, 8), 8), :] * 100.0
    grad_o[...] = scale * g - p * (scale * scale * scale) * jnp.sum(p * g, -1, keepdims=True)
    wires.finish()


def run_contrast(bucket, pooled, devices):
    rows, width = pooled.shape
    slots = rows * devices
    dma = pltpu.SemaphoreType.DMA
    spec_v = pl.BlockSpec(memory_space=VM)
    copies = 1 + 2 + 12 + 16
    loss, grad = pl.pallas_call(
        functools.partial(contrast_kernel, slots, bucket.shape[0]),
        out_shape=[jax.ShapeDtypeStruct((8, 128), single), jax.ShapeDtypeStruct(pooled.shape, single)],
        in_specs=[pl.BlockSpec(memory_space=SM), spec_v],
        out_specs=[spec_v, spec_v],
        scratch_shapes=[
            VM((2 * rows, width // 2), narrow), VM((devices, 2 * rows, width // 2), narrow), VM((slots, width), single),
            dma((copies,)), dma((copies,)), dma(()),
        ],
        compiler_params=pltpu.CompilerParams(collective_id=3, has_side_effects=True),
        name="contrast",
    )(bucket, pooled)
    return loss[0, 0], grad


def gather_weights(tab, w_in, w_out, w_up, w_down, small):
    gat = lambda a: lax.all_gather(a, "fsdp", axis=0, tiled=True)
    return lax.all_gather(tab, "fsdp", axis=1, tiled=True), gat(w_in), gat(w_out), gat(w_up), gat(w_down), gat(small)


def reduce_all(grads, small):
    done = []
    for a in grads:
        part = lax.psum_scatter(a.astype(single), "fsdp", scatter_dimension=0, tiled=True)
        done.append(lax.psum(part.astype(narrow), "dp").astype(single))
    return done, lax.psum(small, ("dp", "fsdp"))


def local(
    tokens, lengths, bucket, position_table, in_projection, query_bias, value_bias, out_projection, out_bias,
    first_gain, first_shift, up_projection, up_bias, down_projection, down_bias, second_gain, second_shift,
):
    groups = lengths.shape[0]
    width = tokens.shape[1]
    count = tokens.shape[0] // groups
    shards = lax.axis_size("fsdp")
    ff = up_projection.shape[1]
    fs = lax.axis_index("fsdp")
    device = lax.axis_index("dp") * shards + fs
    small_parts = (query_bias, value_bias, out_bias, first_gain, first_shift, down_bias, second_gain, second_shift)
    piece = query_bias.shape[0]
    wide_piece = up_bias.shape[0]
    flag = lax.dynamic_slice_in_dim(jnp.repeat(bucket, 2), device * groups, groups)
    chunks = ff // width
    grid = lax.axis_size("dp") == 4 and shards == 8
    if grid:
        line = jnp.concatenate([v[None] for v in small_parts] + [jnp.zeros((8, piece), narrow)], 0)
        spread = lax.dynamic_update_slice(jnp.zeros((16, width), narrow), line, (0, fs * piece))
        ups = lax.dynamic_update_slice(jnp.zeros((ff,), narrow), up_bias, (fs * wide_piece,)).reshape(chunks, width)
        spread = lax.dynamic_update_slice(spread, ups, (8, 0))
        small_all, table_t, *weights = run_gather(
            spread, (position_table.T, in_projection, out_projection, up_projection, down_projection)
        )
        vecs = jnp.sum(small_all.astype(single), 0)
        table = table_t.T
    else:
        small = jnp.concatenate(small_parts + (up_bias,))[None, :]
        table, *weights, small_all = gather_weights(
            position_table, in_projection, out_projection, up_projection, down_projection, small
        )
        heads = small_all[:, : 8 * piece].reshape(shards, 8, piece).transpose(1, 0, 2).reshape(8, width)
        vecs = jnp.concatenate(
            [heads, small_all[:, 8 * piece :].reshape(chunks, width), jnp.zeros((8 - chunks, width), narrow)]
        ).astype(single)
    *saved, pooled = run_forward(groups, count, width, ff, lengths, flag, vecs, tokens, table, weights)
    slots = groups * 4
    if grid:
        loss, pooled_grad = run_contrast(bucket, pooled, 4 * shards)
    else:
        embedded, norm_grad = jax.vjp(normalize_rows, pooled)
        every = lax.all_gather(embedded.astype(narrow), ("dp", "fsdp"), axis=0, tiled=True)
        loss, embed_grad = contrast(every, embedded, device * slots, slots, bucket)
        pooled_grad = norm_grad(embed_grad)[0]
    tokens_grad, gin, gout, gup, gdown, gtab, gvec = run_backward(
        groups, count, width, ff, lengths, flag, vecs, pooled_grad, weights, saved
    )
    if grid:
        cut = lambda a: a.reshape(4, 2, a.shape[0] // 8, a.shape[1])
        gdown, gup, gout, gin, gtab, gvec = run_reduce([cut(a) for a in (gdown, gup, gout, gin, gtab)], gvec)
    else:
        (gin, gout, gup, gdown, gtab), gvec = reduce_all((gin, gout, gup, gdown, gtab), gvec)
    gtab = gtab.T
    own = [lax.dynamic_slice_in_dim(gvec[i], fs * piece, piece) for i in range(8)]
    up_own = lax.dynamic_slice_in_dim(gvec[8 : 8 + chunks].reshape(ff), fs * wide_piece, wide_piece)
    return (
        loss, pooled, tokens_grad, gtab, gin, own[0], own[1], gout, own[2], own[3], own[4], gup, up_own, gdown,
        own[5], own[6], own[7],
    )


def solution(mesh):
    rows = P(("dp", "fsdp"), None)
    vec = P("fsdp")
    mat = P("fsdp", None)
    in_specs = (rows, rows, P(), P(None, "fsdp"), mat, vec, vec, mat, vec, vec, vec, mat, vec, mat, vec, vec, vec)
    out_specs = (P(), rows, rows, P(None, "fsdp"), mat, vec, vec, mat, vec, vec, vec, mat, vec, mat, vec, vec, vec)
    return jax.shard_map(local, mesh=mesh, in_specs=in_specs, out_specs=out_specs, check_vma=False)
```

```python
import functools

import jax
import jax.numpy as jnp
from jax import lax
from jax.experimental import pallas as pl
from jax.experimental.pallas import tpu as pltpu
from jax.sharding import PartitionSpec as P

H = 12
narrow = jnp.bfloat16
single = jnp.float32
ANY = pl.ANY
VM = pltpu.VMEM
SM = pltpu.SMEM
LIMIT = 60 * 2**20


def dot(a, b):
    return lax.dot_general(a, b, (((1,), (0,)), ((), ())), preferred_element_type=single)


def dot_nt(a, b):
    return lax.dot_general(a, b, (((1,), (1,)), ((), ())), preferred_element_type=single)


def at(start, size):
    return pl.ds(pl.multiple_of(start, 128), size)


def gelu_pair(u):
    t = 1.0 / (1.0 + 0.23164189 * jnp.abs(u))
    e = jnp.exp(-0.5 * (u * u))
    tail = t * (
        0.127414796 + t * (-0.142248368 + t * (0.7107068705 + t * (-0.7265760135 + t * 0.5307027145)))
    )
    tail = tail * e
    phi = jnp.where(u < 0, tail, 1.0 - tail)
    return u * phi, phi + u * (e * 0.3989422804)


def norm_rows(value):
    mean = jnp.mean(value, -1, keepdims=True)
    centred = value - mean
    rstd = lax.rsqrt(jnp.mean(centred * centred, -1, keepdims=True) + 1e-06)
    return centred * rstd, rstd


def norm_back(grad, unit, rstd):
    one = jnp.mean(grad, -1, keepdims=True)
    two = jnp.mean(grad * unit, -1, keepdims=True)
    return rstd * (grad - one - unit * two)


def slot_lengths(lens, flag, g, along_rows, count, width):
    slot = count // 4
    shape = (count, width) if along_rows else (8, count)
    t = lax.broadcasted_iota(jnp.int32, shape, 0 if along_rows else 1)
    which = t // slot
    long = flag[g] > 0
    limit = jnp.where(which == 0, lens[g, 0], lens[g, 1])
    limit = jnp.where(which == 2, lens[g, 2], limit)
    limit = jnp.where(which == 3, lens[g, 3], limit)
    limit = jnp.where(long, lens[g, 0], limit)
    inside = jnp.where(long, t, t % slot)
    return which, inside < limit


def backward_kernel(
    sizes,
    lens, flag, vecs, pg, w_in, w_out, w_up, w_down, x_i, mixed_i, prob_i, ctx_i, hid_i, n1_i, r1_i, act_i, gp_i, n2_i, r2_i,
    tok_o, gin_o, gout_o, gup_o, gdown_o, gtab_o, gvec_o,
    v_in, v_out, v_up, v_down, x_v, mixed, ctx, n1, n2, r1_v, r2_v, ast, gst, pst, low, hid_t, up_low, grad, dctx, gst_a, gst_b, gsmall,
    in_sem, a_sem, p_sem, o_sem, b_sem,
):
    groups, count, width, ff, chunk = sizes
    rows = groups * count
    pairs = width // 128
    slot = count // 4
    wide = ff // chunk
    blocks = rows // 256
    loads = [
        pltpu.make_async_copy(s, d, in_sem.at[i])
        for i, (s, d) in enumerate(
            (
                (n2_i, n2), (r2_i, r2_v), (hid_i, dctx), (w_up, v_up), (r1_i, r1_v), (ctx_i, ctx),
                (w_out, v_out), (mixed_i, mixed), (x_i, x_v), (w_in, v_in), (n1_i, n1),
            )
        )
    ]
    (l_n2, l_r2, l_hid, l_up, l_r1, l_ctx, l_wout, l_mixed, l_x, l_win, l_n1) = loads
    per = chunk // 8
    l_down = [
        pltpu.make_async_copy(
            w_down.at[t] if len(w_down.shape) == 4 else w_down.at[:, pl.ds(t * per, per), :], v_down.at[t], in_sem.at[11 + t]
        )
        for t in range(wide)
    ]

    def act_loads(j):
        return (
            pltpu.make_async_copy(act_i.at[j], ast.at[j % 2], a_sem.at[j % 2]),
            pltpu.make_async_copy(gp_i.at[j], gst.at[j % 2], a_sem.at[2 + j % 2]),
        )

    def prob_load(i, s_):
        return pltpu.make_async_copy(prob_i.at[i], pst.at[s_], p_sem.at[s_])

    l_n2.start()
    l_r2.start()
    for c in act_loads(0):
        c.start()
    for c in loads[2:4] + l_down:
        c.start()
    for c in act_loads(1):
        c.start()
    for c in loads[4:]:
        c.start()
    prob_load(0, 0).start()
    prob_load(1, 1).start()

    def vec(i):
        return vecs[i : i + 1, :width]

    stores = []

    def store(src, dst):
        c = pltpu.make_async_copy(src, dst, o_sem.at[len(stores)])
        c.start()
        stores.append(c)

    l_n2.wait()
    l_r2.wait()
    gain_sum = jnp.zeros((1, width), single)
    shift_sum = jnp.zeros((1, width), single)
    bias_sum = jnp.zeros((1, width), single)
    for g in range(groups):
        _, live = slot_lengths(lens, flag, g, True, count, 128)
        long = flag[g] > 0
        for s in range(4):
            r = pl.ds(g * count + s * slot, slot)
            mine = pg[4 * g + s : 4 * g + s + 1, :] / jnp.maximum(lens[g, s], 1).astype(single)
            first = pg[4 * g : 4 * g + 1, :] / jnp.maximum(lens[g, 0], 1).astype(single)
            row = jnp.where(long, first, mine)
            keep = live[s * slot : (s + 1) * slot, :1]
            d = jnp.where(keep, row, 0.0)
            unit = n2[r, :]
            gain_sum = gain_sum + jnp.sum(d * unit, 0, keepdims=True)
            shift_sum = shift_sum + jnp.sum(d, 0, keepdims=True)
            back = norm_back(d * vec(6), unit, r2_v[r, :1])
            grad[r, :] = back
            lowered = back.astype(narrow)
            low[r, :] = lowered
            bias_sum = bias_sum + jnp.sum(lowered.astype(single), 0, keepdims=True)
    gsmall[...] = jnp.zeros_like(gsmall)
    gsmall[6:7, :width] = gain_sum
    gsmall[7:8, :width] = shift_sum
    gsmall[5:6, :width] = bias_sum
    l_hid.wait()
    for b in range(rows // slot):
        r = pl.ds(b * slot, slot)
        hid_t[:, r] = dctx[r, :].T

    for c in l_down:
        c.wait()
    l_up.wait()

    def weight_copies(j):
        return (
            pltpu.make_async_copy(gst_a, gdown_o.at[j], b_sem.at[0]),
            pltpu.make_async_copy(gst_b, gup_o.at[j], b_sem.at[1]),
        )

    for j in range(wide):
        s_ = j % 2
        cols = pl.ds(j * chunk, chunk)
        for c in act_loads(j):
            c.wait()

        def feed(b, total, s_=s_, j=j, cols=cols):
            r = at(b * 256, 256)
            up = (dot_nt(low[r, :], v_down[j].reshape(chunk, width)) * gst[s_, r, :].astype(single)).astype(narrow)
            up_low[r, :] = up
            grad[r, :] += dot_nt(up, v_up[:, cols])
            return total + jnp.sum(up.astype(single), 0, keepdims=True)

        gsmall[8 + j : 9 + j, :] = lax.fori_loop(0, blocks, feed, jnp.zeros((1, chunk), single))
        if j >= 1:
            for c in weight_copies(j - 1):
                c.wait()

        def weigh(b, _, s_=s_):
            r = at(b * 256, 256)
            gst_a[r, :] = dot(ast[s_, :, r].T, low[...]).astype(narrow)
            return 0

        lax.fori_loop(0, chunk // 256, weigh, 0)

        def weigh_up(b, _):
            r = at(b * 256, 256)
            gst_b[r, :] = dot(hid_t[r, :], up_low[...]).astype(narrow)
            return 0

        lax.fori_loop(0, width // 256, weigh_up, 0)
        for c in weight_copies(j):
            c.start()
        if j + 2 < wide:
            for c in act_loads(j + 2):
                c.start()

    l_n1.wait()
    l_r1.wait()
    l_ctx.wait()
    l_wout.wait()
    gain_sum = jnp.zeros((1, width), single)
    shift_sum = jnp.zeros((1, width), single)
    bias_sum = jnp.zeros((1, width), single)
    for b in range(rows // slot):
        r = pl.ds(b * slot, slot)
        d = grad[r, :]
        unit = n1[r, :]
        gain_sum = gain_sum + jnp.sum(d * unit, 0, keepdims=True)
        shift_sum = shift_sum + jnp.sum(d, 0, keepdims=True)
        back = norm_back(d * vec(3), unit, r1_v[r, :1])
        grad[r, :] = back
        lowered = back.astype(narrow)
        low[r, :] = lowered
        bias_sum = bias_sum + jnp.sum(lowered.astype(single), 0, keepdims=True)
        hid_t[:, r] = ctx[r, :].T
    gsmall[3:4, :width] = gain_sum
    gsmall[4:5, :width] = shift_sum
    gsmall[2:3, :width] = bias_sum
    for c in weight_copies(wide - 1):
        c.wait()

    def out_weigh(b, _):
        r = at(b * 256, 256)
        gst_a[r, :] = dot(hid_t[r, :], low[...]).astype(narrow)
        return 0

    lax.fori_loop(0, width // 256, out_weigh, 0)
    store(gst_a.at[pl.ds(0, width), :], gout_o)

    def context_back(b, _):
        r = at(b * 256, 256)
        dctx[r, :] = dot_nt(low[r, :], v_out[...]).astype(narrow)
        return 0

    lax.fori_loop(0, blocks, context_back, 0)

    l_mixed.wait()
    lane = lax.broadcasted_iota(jnp.int32, (count, 128), 1)
    half = (lane < 64, lane >= 64)
    scale = jnp.asarray(0.125, narrow)
    n = groups * pairs

    def attend(i, _):
        g = i // pairs
        p = i % pairs
        s_ = i % 2
        r = at(g * count, count)
        prob_load(i, s_).wait()
        c_q = at(p * 128, 128)
        c_k = at(width + p * 128, 128)
        c_v = at(2 * width + p * 128, 128)
        q = mixed[r, c_q] * scale
        k = mixed[r, c_k]
        v = mixed[r, c_v]
        dc = dctx[r, c_q]
        c = ctx[r, c_q]
        q_t = q.T
        dc_t = dc.T
        zero = jnp.zeros_like(q)
        prod = dc.astype(single) * c.astype(single)
        dq = [None] * (count // 256)
        dk_t = []
        dv_t = []
        for h in range(2):
            dch = jnp.where(half[h], dc, zero)
            kh = jnp.where(half[h], k, zero)
            d = jnp.sum(jnp.where(half[h], prod, 0.0), -1, keepdims=True)
            dkh = None
            dvh = None
            for b in range(count // 256):
                rb = slice(b * 256, (b + 1) * 256)
                prob = pst[s_, h, rb, :]
                dp = dot_nt(dch[rb], v)
                ds = (prob.astype(single) * (dp - d[rb])).astype(narrow)
                o = dot(ds, kh)
                dq[b] = o if dq[b] is None else dq[b] + o
                hr = slice(h * 64, (h + 1) * 64)
                one = dot(q_t[hr, rb], ds)
                two = dot(dc_t[hr, rb], prob)
                dkh = one if dkh is None else dkh + one
                dvh = two if dvh is None else dvh + two
            dk_t.append(dkh)
            dv_t.append(dvh)
        for b in range(count // 256):
            mixed[at(g * count + b * 256, 256), c_q] = (dq[b] * 0.125).astype(narrow)
        mixed[r, c_k] = jnp.concatenate(dk_t, 0).T.astype(narrow)
        mixed[r, c_v] = jnp.concatenate(dv_t, 0).T.astype(narrow)

        @pl.when(i + 2 < n)
        def _():
            prob_load(i + 2, s_).start()

        return 0

    lax.fori_loop(0, n, attend, 0)

    l_x.wait()
    l_win.wait()
    for b in range(rows // slot):
        r = pl.ds(b * slot, slot)
        hid_t[:, r] = x_v[r, :].T
    stores[0].wait()

    def bias(b, total):
        r = at(b * 256, 256)
        return (
            total[0] + jnp.sum(mixed[r, :width].astype(single), 0, keepdims=True),
            total[1] + jnp.sum(mixed[r, 2 * width :].astype(single), 0, keepdims=True),
        )

    zero_row = jnp.zeros((1, width), single)
    q_sum, v_sum = lax.fori_loop(0, blocks, bias, (zero_row, zero_row))
    gsmall[0:1, :width] = q_sum
    gsmall[1:2, :width] = v_sum
    store(gsmall, gvec_o)
    def in_copy(part):
        buf = gst_a.at[pl.ds(0, width), :] if part % 2 == 0 else gst_b.at[:, pl.ds(0, width)]
        return pltpu.make_async_copy(buf, gin_o.at[:, pl.ds(part * width, width)], b_sem.at[part % 2])

    for part in range(3):
        cols = pl.ds(part * width, width)
        if part == 2:
            in_copy(0).wait()

        def in_weigh(b, _, cols=cols, part=part):
            r = at(b * 256, 256)
            out = dot(hid_t[r, :], mixed[:, cols]).astype(narrow)
            if part % 2 == 0:
                gst_a[r, :] = out
            else:
                gst_b[r, :width] = out
            return 0

        lax.fori_loop(0, width // 256, in_weigh, 0)
        in_copy(part).start()

    def token_back(b, _):
        r = at(b * 256, 256)
        grad[r, :] += dot_nt(mixed[r, :], v_in[...])
        return 0

    lax.fori_loop(0, blocks, token_back, 0)
    store(grad, tok_o)
    for s in range(4):
        total = None
        for g in range(groups):
            long = flag[g] > 0
            r = pl.ds(g * count + s * slot, slot)
            if s == 0:
                other = grad[r, :]
                for o in range(1, 4):
                    other = other + grad[pl.ds(g * count + o * slot, slot), :]
                piece = jnp.where(long, grad[r, :], other)
            else:
                piece = jnp.where(long, grad[r, :], 0.0)
            total = piece if total is None else total + piece
        up_low[:, s * slot : (s + 1) * slot] = jnp.zeros_like(up_low[:, s * slot : (s + 1) * slot])
        up_low[:width, s * slot : (s + 1) * slot] = total.T.astype(narrow)
    store(up_low.at[pl.ds(0, width), pl.ds(0, count)], gtab_o)
    in_copy(1).wait()
    in_copy(2).wait()
    for c in stores[1:]:
        c.wait()


def shapes_of(groups, count, width, ff, chunk):
    rows = groups * count
    pairs = width // 128
    chunks = ff // chunk
    return dict(
        x=((rows, width), narrow),
        mixed=((rows, 3 * width), narrow),
        prob=((groups * pairs, 2, count, count), narrow),
        ctx=((rows, width), narrow),
        hid=((rows, width), narrow),
        n1=((rows, width), single),
        r1=((rows, 128), single),
        act=((chunks, rows, chunk), narrow),
        gp=((chunks, rows, chunk), narrow),
        n2=((rows, width), single),
        r2=((rows, 128), single),
    )


def run_forward(remote, groups, count, width, ff, chunk, lens, flag, small, tok, tab, weights):
    rows = groups * count
    chunks = ff // chunk
    saved = shapes_of(groups, count, width, ff, chunk)
    outs = [jax.ShapeDtypeStruct(*v) for v in saved.values()]
    outs.append(jax.ShapeDtypeStruct((groups * 4, width), single))
    outs.append(jax.ShapeDtypeStruct((16, chunk), single))
    spec_any = pl.BlockSpec(memory_space=ANY)
    spec_v = pl.BlockSpec(memory_space=VM)
    spec_s = pl.BlockSpec(memory_space=SM)
    dma = pltpu.SemaphoreType.DMA
    n_items = 5 + 2 * chunks
    extra = []
    if remote:
        whole = [
            jax.ShapeDtypeStruct((width, count), narrow),
            jax.ShapeDtypeStruct((width, 3 * width), narrow),
            jax.ShapeDtypeStruct((width, width), narrow),
            jax.ShapeDtypeStruct((width, ff), narrow),
            jax.ShapeDtypeStruct((8, ff // 8, width), narrow),
        ]
        outs += whole
        copies = Piece.COPIES * n_items + 8
        extra = [dma((copies,)), dma((copies,)), dma((6,))]
        body = functools.partial(forward_kernel, (groups, count, width, ff, chunk), True)
    else:

        def body(*refs):
            head = 9
            given = refs[4:head]
            rest = refs[head:]
            return forward_kernel((groups, count, width, ff, chunk), False, *refs[:head], *rest[:13], *given, *rest[13:])

    per = chunk // 8
    return pl.pallas_call(
        body,
        out_shape=outs,
        in_specs=[spec_s, spec_s, spec_any] + [spec_any] * 6,
        out_specs=[spec_any] * 11 + [spec_v, spec_v] + [spec_any] * (5 if remote else 0),
        scratch_shapes=[
            VM((width, 3 * width), narrow),
            VM((width, width), narrow),
            VM((width, ff), narrow),
            VM((chunks, 8, per, width), narrow),
            VM((width, count), narrow),
            VM((rows, width), narrow),
            VM((rows, 3 * width), narrow),
            VM((groups, count, count), single),
            VM((2, 2, count, count), narrow),
            VM((rows, width), narrow),
            VM((rows, width), single),
            VM((rows, width), narrow),
            VM((rows, width), single),
            VM((rows, 128), single),
            VM((rows, 128), single),
            VM((2, rows, chunk), narrow),
            VM((2, rows, chunk), narrow),
            VM((rows, width), single),
            VM((8, 16, chunk) if remote else (16, chunk), narrow),
            VM((width // 8, ff) if remote else (16, 128), narrow),
            VM((width // 8, ff) if remote else (16, 128), narrow),
            VM((width // 8, count) if remote else (16, 128), narrow),
            VM((width // 8, 3 * width) if remote else (16, 128), narrow),
            VM((width // 8, width) if remote else (16, 128), narrow),
            VM((ff // 8, width) if remote else (16, 128), narrow),
            dma((6,)), dma((10,)), dma((2,)), dma((4,)), dma((n_items,)),
        ]
        + extra,
        compiler_params=pltpu.CompilerParams(
            vmem_limit_bytes=LIMIT, **(dict(collective_id=1, has_side_effects=True) if remote else {})
        ),
        cost_estimate=pl.CostEstimate(flops=2 * rows * width * (4 * width + 2 * ff), bytes_accessed=80 * 2**20, transcendentals=10**7),
        name="encoder_forward",
    )(lens, flag, small, tok, tab, *weights)


def run_backward(groups, count, width, ff, chunk, lens, flag, vecs, pooled_grad, weights, saved):
    rows = groups * count
    chunks, per = ff // chunk, chunk // 8
    spec_any = pl.BlockSpec(memory_space=ANY)
    spec_v = pl.BlockSpec(memory_space=VM)
    spec_s = pl.BlockSpec(memory_space=SM)
    dma = pltpu.SemaphoreType.DMA
    return pl.pallas_call(
        functools.partial(backward_kernel, (groups, count, width, ff, chunk)),
        out_shape=[
            jax.ShapeDtypeStruct((rows, width), single),
            jax.ShapeDtypeStruct((width, 3 * width), narrow),
            jax.ShapeDtypeStruct((width, width), narrow),
            jax.ShapeDtypeStruct((chunks, width, chunk), narrow),
            jax.ShapeDtypeStruct((chunks, chunk, width), narrow),
            jax.ShapeDtypeStruct((width, count), narrow),
            jax.ShapeDtypeStruct((16, chunk), single),
        ],
        in_specs=[spec_s, spec_s, spec_v, spec_v] + [spec_any] * 15,
        out_specs=[spec_any] * 7,
        scratch_shapes=[
            VM((width, 3 * width), narrow),
            VM((width, width), narrow),
            VM((width, ff), narrow),
            VM((chunks, 8, per, width), narrow),
            VM((rows, width), narrow),
            VM((rows, 3 * width), narrow),
            VM((rows, width), narrow),
            VM((rows, width), single),
            VM((rows, width), single),
            VM((rows, 128), single),
            VM((rows, 128), single),
            VM((2, rows, chunk), narrow),
            VM((2, rows, chunk), narrow),
            VM((2, 2, count, count), narrow),
            VM((rows, width), narrow),
            VM((width, rows), narrow),
            VM((rows, chunk), narrow),
            VM((rows, width), single),
            VM((rows, width), narrow),
            VM((chunk, width), narrow),
            VM((width, chunk), narrow),
            VM((16, chunk), single),
            dma((11 + chunks,)), dma((4,)), dma((2,)), dma((4,)), dma((2,)),
        ],
        compiler_params=pltpu.CompilerParams(vmem_limit_bytes=LIMIT),
        cost_estimate=pl.CostEstimate(flops=4 * rows * width * (4 * width + 2 * ff), bytes_accessed=100 * 2**20, transcendentals=0),
        name="encoder_backward",
    )(lens, flag, vecs, pooled_grad, *weights, *saved)


def forward_kernel(
    sizes, remote,
    lens, flag, small, tok, tab_s, in_s, out_s, up_s, down_s,
    x_o, mixed_o, prob_o, ctx_o, hid_o, n1_o, r1_o, act_o, gp_o, n2_o, r2_o, pooled_o, vecs_o, w_tab, w_in, w_out, w_up, w_down,
    v_in, v_out, v_up, v_down, tab_v, x_v, mixed, mask, pst, ctx, hid, hid_low, n_st, r1_v, r2_v, ast, gst, acc, small_v, up_v, up_p, tab_p, in_p, out_p, down_p,
    in_sem, out_sem, p_sem, a_sem, w_sem, *wires,
):
    groups, count, width, ff, chunk = sizes
    rows = groups * count
    pairs = width // 128
    slot = count // 4
    chunks = ff // chunk
    shards = 8
    load_tok = pltpu.make_async_copy(tok, x_v, in_sem.at[0])
    load_tok.start()
    loads = {}

    def load(name, src, dst):
        loads[name] = pltpu.make_async_copy(src, dst, w_sem.at[len(loads)])
        return loads[name]

    def before():
        for g in range(groups):
            which_q, _ = slot_lengths(lens, flag, g, True, count, 128)
            which_k, live_k = slot_lengths(lens, flag, g, False, count, 128)
            long = flag[g] > 0
            wq = which_q[:, :1]
            open_ = live_k[:1] & (long | (wq == which_k[:1]))
            mask[g] = jnp.where(open_, 0.0, -1000000000.0).astype(single)
        if remote:
            for made in stage:
                made.wait()
            part = chunk // shards
            for fs in range(shards):
                for t in range(chunks):
                    up_p[:, t * chunk + fs * part : t * chunk + (fs + 1) * part] = up_v[
                        :, fs * (ff // shards) + t * part : fs * (ff // shards) + (t + 1) * part
                    ]

    cols = lambda ref, i, n: ref.at[:, pl.ds(i * n, n)]
    down_of = lambda t: w_down.at[:, pl.ds(t * (chunk // shards), chunk // shards), :] if remote else w_down.at[t]
    load("tab", w_tab, tab_v)
    for i in range(3):
        load("in%d" % i, cols(w_in, i, width), cols(v_in, i, width))
    load("out", w_out, v_out)
    for t in range(chunks):
        load("up%d" % t, cols(w_up, t, chunk), cols(v_up, t, chunk))
        load("down%d" % t, down_of(t), v_down.at[t])
    names = list(loads)
    if remote:
        send, recv, own_sem = wires
        here = place()
        x, y, z, c = here
        mine = 2 * z + c
        stage = [
            pltpu.make_async_copy(s, d, in_sem.at[1 + i])
            for i, (s, d) in enumerate(((tab_s, tab_p), (in_s, in_p), (up_s, up_v), (out_s, out_p), (down_s, down_p)))
        ]
        for made in stage:
            made.start()
        greet(neighbours(True), before)
        down_flat = w_down.reshape(ff, width)
        pieces = []
        for n, name in enumerate(names):
            part = int(name[-1]) if name[-1].isdigit() else 0
            kind = name.rstrip("0123456789")
            shard, full, pitch, rr, cc = {
                "tab": (tab_p, w_tab, width // shards, (0, width // shards), (0, count)),
                "in": (in_p, w_in, width // shards, (0, width // shards), (part * width, width)),
                "out": (out_p, w_out, width // shards, (0, width // shards), (0, width)),
                "up": (up_p, w_up, width // shards, (0, width // shards), (part * chunk, chunk)),
                "down": (down_p, down_flat, ff // shards, (part * (chunk // shards), chunk // shards), (0, width)),
            }[kind]
            pieces.append(Piece(n, (send, recv), here, shard, full, pitch, rr, cc))
        extra = Piece.COPIES * len(pieces)

        def small_copy(k, j):
            i = extra + 2 * k + j - 1
            return pltpu.make_async_remote_copy(
                src_ref=small, dst_ref=small_v.at[mine], send_sem=send.at[i], recv_sem=recv.at[i],
                device_id=device_at(x, y, (z + k) % 4, (c + j) % 2), device_id_type=MESH,
            )

        others = [(k, j) for k in range(4) for j in range(2) if (k, j) != (0, 0)]
        own = [
            pltpu.make_async_copy(s, d, own_sem.at[i])
            for i, (s, d) in enumerate(
                (
                    (small, small_v.at[mine]),
                    (tab_p, w_tab.at[pl.ds(pl.multiple_of(mine * (width // shards), 16), width // shards), :]),
                    (in_p, w_in.at[pl.ds(pl.multiple_of(mine * (width // shards), 16), width // shards), :]),
                    (out_p, w_out.at[pl.ds(pl.multiple_of(mine * (width // shards), 16), width // shards), :]),
                    (up_p, w_up.at[pl.ds(pl.multiple_of(mine * (width // shards), 16), width // shards), :]),
                    (down_p, w_down.at[mine]),
                )
            )
        ]
        own_of = {"tab": 1, "in": 2, "out": 3, "up": 4, "down": 5}

        def step(t):
            if t < len(pieces):
                pieces[t].begin()
            for stage, back in (("plane", 1), ("diagonal", 2), ("core", 3), ("finish", 4)):
                if 0 <= t - back < len(pieces):
                    getattr(pieces[t - back], stage)()
                    if stage == "finish":
                        name = names[t - back]
                        kind = name.rstrip("0123456789")
                        if name in (kind, kind + "0"):
                            own[own_of[kind]].wait()
                        loads[name].start()

        for k, j in others:
            small_copy(k, j).start()
        pieces[0].begin()
        for i in (0, 1, 2, 3, 5):
            own[i].start()
        own[4].start()
        steps = [functools.partial(step, t) for t in range(len(pieces) + 4)]
        first_begin = pieces[0].begin
        pieces[0].begin = lambda: None
    else:
        before()
        steps = []
        for n in names:
            loads[n].start()
        little = pltpu.make_async_copy(small, small_v, in_sem.at[1])
        little.start()
    done = [0]

    def pump(upto):
        while done[0] < min(upto, len(steps)):
            steps[done[0]]()
            done[0] += 1

    def pump_in(i, when):
        for n, count_ in enumerate(when):
            if done[0] + n < len(steps):

                @pl.when(i == count_)
                def _(n=n):
                    steps[done[0] + n]()

    def pumped(when):
        done[0] = min(len(steps), done[0] + len(when))

    def need(name):
        pump(names.index(name) + 5)
        loads[name].wait()

    stores = []

    def store(src, dst):
        made = pltpu.make_async_copy(src, dst, out_sem.at[len(stores)])
        made.start()
        stores.append(made)

    need("tab")
    load_tok.wait()
    for g in range(groups):
        long = flag[g] > 0
        for s in range(4):
            part = x_v[pl.ds(g * count + s * slot, slot), :].astype(single)
            place_ = jnp.where(
                long, tab_v[:, s * slot : (s + 1) * slot].T.astype(single), tab_v[:, :slot].T.astype(single)
            )
            both = part + place_
            hid[pl.ds(g * count + s * slot, slot), :] = both
            x_v[pl.ds(g * count + s * slot, slot), :] = both.astype(narrow)
    store(x_v, x_o)
    if remote:
        own[0].wait()
        for k, j in others:
            small_copy(k, j).wait_recv()
        total = small_v[0].astype(single)
        for i in range(1, shards):
            total = total + small_v[i].astype(single)
        vecs_o[...] = total
    else:
        little.wait()
        vecs_o[...] = small_v[...].astype(single)

    def vec(i, n=width):
        return vecs_o[i : i + 1, :n]

    for part in range(3):
        need("in%d" % part)
        cs = pl.ds(part * width, width)

        def project(b, _, cs=cs, part=part):
            r = at(b * 256, 256)
            out = dot(x_v[r, :], v_in[:, cs])
            if part == 0:
                out = out + vec(0)
            if part == 2:
                out = out + vec(1)
            mixed[r, cs] = out.astype(narrow)
            return 0

        lax.fori_loop(0, rows // 256, project, 0)
    store(mixed, mixed_o)

    lane = lax.broadcasted_iota(jnp.int32, (count, 128), 1)
    half = (lane < 64, lane >= 64)
    n = groups * pairs

    def attend(i, _):
        g = i // pairs
        p = i % pairs
        s_ = i % 2
        r = at(g * count, count)

        pump_in(i, ATTEND_PUMPS)
        @pl.when(i >= 2)
        def _():
            pltpu.make_async_copy(pst.at[s_], prob_o.at[i], p_sem.at[s_]).wait()

        q = mixed[r, at(p * 128, 128)]
        k = mixed[r, at(width + p * 128, 128)]
        v = mixed[r, at(2 * width + p * 128, 128)]
        zero = jnp.zeros_like(q)
        out = [None] * (count // 256)
        for h in range(2):
            qh = jnp.where(half[h], q, zero) * jnp.asarray(0.125, narrow)
            vh = jnp.where(half[h], v, zero)
            for b in range(count // 256):
                sc = dot_nt(qh[b * 256 : (b + 1) * 256], k) + mask[g, b * 256 : (b + 1) * 256, :]
                e = jnp.exp(sc - jnp.max(sc, -1, keepdims=True))
                low = (e * (1.0 / jnp.sum(e, -1, keepdims=True))).astype(narrow)
                pst[s_, h, b * 256 : (b + 1) * 256, :] = low
                o = dot(low, vh)
                out[b] = o if out[b] is None else out[b] + o
        for b in range(count // 256):
            ctx[at(g * count + b * 256, 256), at(p * 128, 128)] = out[b].astype(narrow)
        pltpu.make_async_copy(pst.at[s_], prob_o.at[i], p_sem.at[s_]).start()
        return 0

    lax.fori_loop(0, n, attend, 0)
    pumped(ATTEND_PUMPS)
    for i in range(max(n - 2, 0), n):
        pltpu.make_async_copy(pst.at[i % 2], prob_o.at[i], p_sem.at[i % 2]).wait()
    store(ctx, ctx_o)

    need("out")

    def first(b, _):
        pump_in(b, FIRST_PUMPS)
        r = at(b * 256, 256)
        total = hid[r, :] + dot(ctx[r, :], v_out[...]) + vec(2)
        unit, rstd = norm_rows(total)
        n_st[r, :] = unit
        r1_v[r, :] = jnp.broadcast_to(rstd, (256, 128))
        h = unit * vec(3) + vec(4)
        hid_low[r, :] = h.astype(narrow)
        acc[r, :] = h + vec(5)
        return 0

    lax.fori_loop(0, rows // 256, first, 0)
    pumped(FIRST_PUMPS)
    store(n_st, n1_o)
    n1_store = stores[-1]
    store(r1_v, r1_o)
    store(hid_low, hid_o)

    def act_copies(j, s_):
        return (
            pltpu.make_async_copy(ast.at[s_], act_o.at[j], a_sem.at[s_]),
            pltpu.make_async_copy(gst.at[s_], gp_o.at[j], a_sem.at[2 + s_]),
        )

    for j in range(chunks):
        s_ = j % 2
        need("up%d" % j)
        need("down%d" % j)
        if j >= 2:
            for made in act_copies(j - 2, s_):
                made.wait()
        cs = pl.ds(j * chunk, chunk)

        def feed(b, _, s_=s_, j=j, cs=cs):
            pump_in(b, FEED_PUMPS[j])
            r = at(b * 256, 256)
            u = dot(hid_low[r, :], v_up[:, cs]) + vec(8 + j, chunk)
            a, d = gelu_pair(u)
            a = a.astype(narrow)
            ast[s_, r, :] = a
            gst[s_, r, :] = d.astype(narrow)
            acc[r, :] += dot(a, v_down[j].reshape(chunk, width))
            return 0

        lax.fori_loop(0, rows // 256, feed, 0)
        pumped(FEED_PUMPS[j])
        for made in act_copies(j, s_):
            made.start()
    for j in range(max(chunks - 2, 0), chunks):
        for made in act_copies(j, j % 2):
            made.wait()

    n1_store.wait()
    for g in range(groups):
        _, live = slot_lengths(lens, flag, g, True, count, 128)
        sums = []
        for s in range(4):
            r = pl.ds(g * count + s * slot, slot)
            unit, rstd = norm_rows(acc[r, :])
            n_st[r, :] = unit
            r2_v[r, :] = jnp.broadcast_to(rstd, (slot, 128))
            out = unit * vec(6) + vec(7)
            keep = live[s * slot : (s + 1) * slot, :1]
            sums.append(jnp.sum(jnp.where(keep, out, 0.0), 0, keepdims=True))
        long = flag[g] > 0
        for s in range(4):
            div = jnp.maximum(lens[g, s], 1).astype(single)
            if s == 0:
                total = jnp.where(long, sums[0] + sums[1] + sums[2] + sums[3], sums[0])
            else:
                total = jnp.where(long, 0.0, sums[s])
            pooled_o[4 * g + s : 4 * g + s + 1, :] = total / div
    store(n_st, n2_o)
    store(r2_v, r2_o)
    for made in stores:
        if made is not n1_store:
            made.wait()
    if remote:
        for p in pieces:
            p.sent()
        for k, j in others:
            small_copy(k, j).wait_send()


def normalize_rows(pooled):
    return pooled * lax.rsqrt(jnp.sum(pooled * pooled, -1, keepdims=True) + 1e-06)


def slot_roles(bucket):
    long_slot = jnp.repeat(jnp.repeat(bucket, 2), 4) > 0
    slots = jnp.arange(long_slot.shape[0], dtype=jnp.int32)
    within = slots % 4
    odd_group = slots // 4 % 2
    query = jnp.where(long_slot, (within == 0) & (odd_group == 0), within % 2 == 0)
    passage = jnp.where(long_slot, (within == 0) & (odd_group == 1), within % 2 == 1)
    partner = jnp.where(long_slot, slots + 4, slots + 1)
    return (query, passage, partner)


def contrast(every, own, start, rows, bucket):
    query, passage, partner = slot_roles(bucket)
    pair_count = jnp.sum(4 - 3 * bucket).astype(single)
    logits = jnp.einsum("id,jd->ij", every, every, preferred_element_type=single) * 100.0
    columns = jnp.arange(logits.shape[1], dtype=jnp.int32)
    masked = jnp.where(passage[None, :], logits, -1000000000.0)
    top = jnp.max(masked, -1, keepdims=True)
    raised = jnp.exp(masked - top)
    total = jnp.sum(raised, -1, keepdims=True)
    spread = top[:, 0] + jnp.log(total[:, 0])
    match = columns[None, :] == partner[:, None]
    positive = jnp.sum(jnp.where(match, logits, 0.0), -1)
    loss = jnp.sum(jnp.where(query, spread - positive, 0.0)) / pair_count
    row_weight = jnp.where(query, 1.0, 0.0) / pair_count
    logit_grad = (row_weight[:, None] * (raised / total - match.astype(single))).astype(narrow)
    by_row = lax.dynamic_slice_in_dim(logit_grad, start, rows, 0)
    by_column = lax.dynamic_slice_in_dim(logit_grad, start, rows, 1)
    both = jnp.dot(by_row, every, preferred_element_type=single) + jnp.einsum(
        "ij,id->jd", by_column, every, preferred_element_type=single
    )
    return loss, both * 100.0


MESH = pl.DeviceIdType.MESH


def place():
    dp, fs = lax.axis_index("dp"), lax.axis_index("fsdp")
    return dp % 2, dp // 2, fs // 2, fs % 2


def device_at(x, y, z, c):
    return (y * 2 + x, z * 2 + c)


class Wires:
    def __init__(self, send, recv):
        self.send, self.recv, self.next, self.sent = send, recv, 0, []

    def copy(self, src, dst, device):
        i = self.next
        self.next += 1
        made = pltpu.make_async_remote_copy(
            src_ref=src, dst_ref=dst, send_sem=self.send.at[i], recv_sem=self.recv.at[i],
            device_id=device, device_id_type=MESH,
        )
        made.start()
        self.sent.append(made)
        return made

    def finish(self):
        for made in self.sent:
            made.wait_send()


def greet(devices, between=None):
    barrier = pltpu.get_barrier_semaphore()
    for d in devices:
        pl.semaphore_signal(barrier, inc=1, device_id=d, device_id_type=MESH)
    if between is not None:
        between()
    pl.semaphore_wait(barrier, len(devices))


def neighbours(small_too):
    x, y, z, c = place()
    found = [device_at(1 - x, y, z, c), device_at(x, 1 - y, z, c), device_at(x, y, z, 1 - c)]
    for k in (1, 2, 3):
        found.append(device_at(x, y, (z + k) % 4, c))
        if small_too:
            found.append(device_at(x, y, (z + k) % 4, 1 - c))
    return found


ATTEND_PUMPS = (0, 3, 6, 9)
FIRST_PUMPS = (1,)
FEED_PUMPS = ((1,), (1,), ())


class Piece:
    COPIES = 17

    def __init__(self, index, sems, at_, shard, full, pitch, rows, cols):
        self.send, self.recv = sems
        self.x, self.y, self.z, self.c = at_
        self.base = index * self.COPIES
        self.shard, self.full, self.pitch = shard, full, pitch
        self.r0, self.rows = rows
        self.c0, self.cols = cols
        self.both = self.rows % 64 == 0
        self.ways = ("x", "y", "both" if self.both else ("x" if index % 2 else "y"))

    def block(self, ref, fs, a=None, b=None, part=None):
        start = self.r0 if fs is None else fs * self.pitch + self.r0
        rows, col, cols = self.rows, self.c0, self.cols
        if a is not None:
            rows, cols = rows // 2, cols // 2
            start, col = start + a * rows, col + b * cols
        if part is not None:
            rows = rows // 2
            start = start + part * rows
        return ref.at[pl.ds(pl.multiple_of(start, 16), rows), pl.ds(pl.multiple_of(col, 128), cols)]

    def copy(self, i, src, dst, device):
        return pltpu.make_async_remote_copy(
            src_ref=src, dst_ref=dst, send_sem=self.send.at[self.base + i], recv_sem=self.recv.at[self.base + i],
            device_id=device, device_id_type=MESH,
        )

    def from_z(self, k):
        return 2 * ((self.z - k + 4) % 4) + self.c

    def by_z(self, k):
        mine = 2 * self.z + self.c
        there = device_at(self.x, self.y, (self.z + k) % 4, self.c)
        return self.copy(k - 1, self.block(self.shard, None, self.x, self.y), self.block(self.full, mine, self.x, self.y), there)

    def by_x(self, k):
        mine = self.block(self.full, self.from_z(k), self.x, self.y)
        return self.copy(2 + k, mine, mine, device_at(1 - self.x, self.y, self.z, self.c))

    def by_y(self, k):
        mine = self.block(self.full, self.from_z(k), self.x, self.y)
        return self.copy(5 + k, mine, mine, device_at(self.x, 1 - self.y, self.z, self.c))

    def corners(self, k):
        way = self.ways[k - 1]
        parts = (0, 1) if way == "both" else (None, None)
        made = []
        if way != "y":
            got = self.block(self.full, self.from_z(k), 1 - self.x, self.y, parts[0])
            made.append(self.copy(8 + k, got, got, device_at(self.x, 1 - self.y, self.z, self.c)))
        if way != "x":
            got = self.block(self.full, self.from_z(k), self.x, 1 - self.y, parts[1])
            made.append(self.copy(10 if k == 2 else 12, got, got, device_at(1 - self.x, self.y, self.z, self.c)))
        return made

    def by_core(self, k):
        there = device_at(self.x, self.y, self.z, 1 - self.c)
        got = self.block(self.full, self.from_z(k))
        src = self.block(self.shard, None) if k == 0 else got
        return self.copy(13 + k, src, got, there)

    def begin(self):
        for k in (1, 2, 3):
            self.by_z(k).start()
        self.by_core(0).start()

    def plane(self):
        for k in (1, 2, 3):
            self.by_z(k).wait_recv()
            self.by_x(k).start()
            self.by_y(k).start()

    def diagonal(self):
        for k in (1, 2, 3):
            self.by_x(k).wait_recv()
            self.by_y(k).wait_recv()
            for made in self.corners(k):
                made.start()

    def core(self):
        for k in (1, 2, 3):
            for made in self.corners(k):
                made.wait_recv()
            self.by_core(k).start()

    def finish(self):
        for k in range(4):
            self.by_core(k).wait_recv()

    def sent(self):
        for k in (1, 2, 3):
            for made in [self.by_z(k), self.by_x(k), self.by_y(k), self.by_core(k)] + self.corners(k):
                made.wait_send()
        self.by_core(0).wait_send()


class Reduce:
    def __init__(self, wires, grad, own, from_core, b1x, b1y, b2x, b2y, from_z, final, sem):
        self.w, self.grad, self.own, self.from_core = wires, grad, own, from_core
        self.b1x, self.b1y, self.b2x, self.b2y, self.from_z, self.final, self.sem = b1x, b1y, b2x, b2y, from_z, final, sem
        _, self.rows, self.cols = own.shape
        self.x, self.y, self.z, self.c = place()

    def rh(self, a):
        return pl.ds(pl.multiple_of(a * (self.rows // 2), 16), self.rows // 2)

    def ch(self, b):
        return pl.ds(pl.multiple_of(b * (self.cols // 2), 128), self.cols // 2)

    def add(self, zs, row0, rows, cols, other, step=16):
        blocks = rows // step

        def body(i, _):
            zi = i // blocks
            r = i % blocks * step
            mine = (zs[0] + zi, pl.ds(pl.multiple_of(row0 + r, 16), step), cols)
            theirs = other[zi, pl.ds(pl.multiple_of(r, 16), step), :]
            self.own[mine] = (self.own[mine].astype(single) + theirs.astype(single)).astype(narrow)
            return 0

        lax.fori_loop(0, len(zs) * blocks, body, 0)

    def start(self):
        x, y, z, c = self.x, self.y, self.z, self.c
        self.keep = pltpu.make_async_copy(self.grad.at[:, c], self.own, self.sem)
        self.keep.start()
        self.s0 = self.w.copy(self.grad.at[:, 1 - c], self.from_core, device_at(x, y, z, 1 - c))

    def first(self):
        x, y, z, c = self.x, self.y, self.z, self.c
        self.keep.wait()
        self.s0.wait_recv()
        self.add((0, 1, 2, 3), 0, self.rows, slice(None), self.from_core)
        lo, hi = pl.ds(0, 2), pl.ds(2, 2)
        self.s1 = (
            self.w.copy(self.own.at[lo, self.rh(1 - x), :], self.b1x, device_at(1 - x, y, z, c)),
            self.w.copy(self.own.at[hi, :, self.ch(1 - y)], self.b1y, device_at(x, 1 - y, z, c)),
        )

    def second(self):
        x, y, z, c = self.x, self.y, self.z, self.c
        for s in self.s1:
            s.wait_recv()
        self.add((0, 1), x * (self.rows // 2), self.rows // 2, slice(None), self.b1x)
        self.add((2, 3), 0, self.rows, self.ch(y), self.b1y)
        lo, hi = pl.ds(0, 2), pl.ds(2, 2)
        self.s2 = (
            self.w.copy(self.own.at[lo, self.rh(x), self.ch(1 - y)], self.b2y, device_at(x, 1 - y, z, c)),
            self.w.copy(self.own.at[hi, self.rh(1 - x), self.ch(y)], self.b2x, device_at(1 - x, y, z, c)),
        )

    def third(self):
        x, y, z, c = self.x, self.y, self.z, self.c
        for s in self.s2:
            s.wait_recv()
        self.add((0, 1), x * (self.rows // 2), self.rows // 2, self.ch(y), self.b2y)
        self.add((2, 3), x * (self.rows // 2), self.rows // 2, self.ch(y), self.b2x)
        self.s3 = [
            self.w.copy(self.own.at[(z + k) % 4, self.rh(x), self.ch(y)], self.from_z.at[k - 1], device_at(x, y, (z + k) % 4, c))
            for k in (1, 2, 3)
        ]

    def fourth(self):
        x, y, z, c = self.x, self.y, self.z, self.c
        for s in self.s3:
            s.wait_recv()
        half = self.rows // 2

        def body(i, _):
            r = pl.ds(pl.multiple_of(i * 16, 16), 16)
            mine = pl.ds(pl.multiple_of(x * half + i * 16, 16), 16)
            total = self.own[z, mine, self.ch(y)].astype(single)
            for k in range(3):
                total = total + self.from_z[k, r, :].astype(single)
            self.final[mine, self.ch(y)] = total.astype(narrow)
            return 0

        lax.fori_loop(0, half // 16, body, 0)
        mine = self.final.at[self.rh(x), self.ch(y)]
        self.s4 = [
            self.w.copy(mine, mine, device_at(1 - x, y, z, c)),
            self.w.copy(mine, mine, device_at(x, 1 - y, z, c)),
            self.w.copy(mine, mine, device_at(1 - x, 1 - y, z, c)),
        ]

    def finish(self, out):
        for s in self.s4:
            s.wait_recv()

        def body(i, _):
            r = pl.ds(pl.multiple_of(i * 16, 16), 16)
            out[r, :] = self.final[r, :].astype(single)
            return 0

        lax.fori_loop(0, self.rows // 16, body, 0)


class ReduceSmall:
    def __init__(self, wires, total, got):
        self.w, self.total, self.got = wires, total, got

    def send(self, i, device):
        return self.w.copy(self.total.at[i], self.got.at[i], device)

    def start(self):
        x, y, z, c = place()
        self.s = self.send(0, device_at(x, y, z, 1 - c))

    def step(self, i):
        x, y, z, c = place()
        self.s.wait_recv()
        self.total[i + 1] = self.total[i] + self.got[i]
        if i == 0:
            self.s = self.send(1, device_at(1 - x, y, z, c))
        elif i == 1:
            self.s = self.send(2, device_at(x, 1 - y, z, c))
        else:
            self.last = [
                self.w.copy(self.total.at[3], self.got.at[2 + k], device_at(x, y, (z + k) % 4, c)) for k in (1, 2, 3)
            ]

    def finish(self, out):
        for s in self.last:
            s.wait_recv()
        x, y, z, c = place()
        out[...] = jnp.zeros_like(out)
        for i in range(4):
            term = jnp.zeros_like(out)
            for k in range(4):
                part = self.total[3] if k == 0 else self.got[2 + k]
                term = jnp.where((z - k + 4) % 4 == i, part, term)
            out[...] = out[...] + term


def reduce_kernel(count, small, *refs):
    grads, outs, rest = refs[:count], refs[count : 2 * count + 1], refs[2 * count + 1 :]
    total, got, send, recv, sems = rest[:5]
    scratch = rest[5:]
    x, y, z, c = place()
    wires = Wires(send, recv)
    greet(neighbours(False) + [device_at(1 - x, 1 - y, z, c)])
    work = [Reduce(wires, grads[i], *scratch[8 * i : 8 * i + 8], sems.at[i]) for i in range(count)]
    total[0] = small[...]
    tiny = ReduceSmall(wires, total, got)
    for w in work:
        w.start()
    tiny.start()
    for t in range(count + 4):
        for stage, back in (("first", 0), ("second", 1), ("third", 2), ("fourth", 3)):
            if 0 <= t - back < count:
                getattr(work[t - back], stage)()
        if 0 <= t - 4 < count:
            work[t - 4].finish(outs[t - 4])
        if t < 3:
            tiny.step(t)
    tiny.finish(outs[count])
    wires.finish()


def run_reduce(grads, small):
    count = len(grads)
    spec = pl.BlockSpec(memory_space=ANY)
    spec_v = pl.BlockSpec(memory_space=VM)
    dma = pltpu.SemaphoreType.DMA
    scratch = []
    for g in grads:
        _, _, r, k = g.shape
        scratch += [
            VM((4, r, k), narrow), VM((4, r, k), narrow), VM((2, r // 2, k), narrow), VM((2, r, k // 2), narrow),
            VM((2, r // 2, k // 2), narrow), VM((2, r // 2, k // 2), narrow), VM((3, r // 2, k // 2), narrow),
            VM((r, k), narrow),
        ]
    copies = 11 * count + 6
    return pl.pallas_call(
        functools.partial(reduce_kernel, count),
        out_shape=[jax.ShapeDtypeStruct(g.shape[2:], single) for g in grads] + [jax.ShapeDtypeStruct(small.shape, single)],
        in_specs=[spec_v] + [spec] * count,
        out_specs=[spec_v] * (count + 1),
        scratch_shapes=[
            VM((4,) + small.shape, single), VM((6,) + small.shape, single), dma((copies,)), dma((copies,)), dma((count,)),
        ] + scratch,
        compiler_params=pltpu.CompilerParams(collective_id=2, has_side_effects=True, vmem_limit_bytes=LIMIT),
        name="reduce_gradients",
    )(small, *grads)


def contrast_kernel(slots, buckets, bucket, pooled, loss_o, grad_o, mine, every, full, send, recv, sem):
    x, y, z, c = place()
    device = (y * 2 + x) * 8 + 2 * z + c
    greet(neighbours(False))
    wires = Wires(send, recv)
    p = pooled[...]
    scale = lax.rsqrt(jnp.sum(p * p, -1, keepdims=True) + 1e-06)
    e = p * scale
    width = e.shape[1]
    hw = width // 2
    mine[...] = jnp.concatenate([e[:, :hw], e[:, hw:]], 0).astype(narrow)

    def slot_of(xx, yy, zz):
        return (yy * 2 + xx) * 8 + 2 * zz + c

    def block(xx, yy, zz):
        return every.at[slot_of(xx, yy, zz)]

    keep = pltpu.make_async_copy(mine, every.at[device], sem)
    keep.start()
    by_x = wires.copy(mine, block(x, y, z), device_at(1 - x, y, z, c))
    by_y = [wires.copy(mine, block(x, y, z), device_at(x, 1 - y, z, c))]
    by_z = [wires.copy(mine, block(x, y, z), device_at(x, y, (z + k) % 4, c)) for k in (1, 2, 3)]
    by_x.wait_recv()
    by_y.append(wires.copy(block(1 - x, y, z), block(1 - x, y, z), device_at(x, 1 - y, z, c)))
    by_z += [wires.copy(block(1 - x, y, z), block(1 - x, y, z), device_at(x, y, (z + k) % 4, c)) for k in (1, 2, 3)]
    for s in by_y:
        s.wait_recv()
    for xx in (x, 1 - x):
        by_z += [
            wires.copy(block(xx, 1 - y, z), block(xx, 1 - y, z), device_at(x, y, (z + k) % 4, c)) for k in (1, 2, 3)
        ]
    pair_size = 8

    def long_of(shape, axis):
        pair = lax.broadcasted_iota(jnp.int32, shape, axis) // pair_size
        found = jnp.zeros(shape, jnp.int32)
        for b in range(buckets):
            found = jnp.where(pair == b, bucket[b], found)
        return found > 0

    def roles(shape, axis):
        t = lax.broadcasted_iota(jnp.int32, shape, axis)
        long = long_of(shape, axis)
        within, odd = t % 4, t // 4 % 2
        query = jnp.where(long, jnp.where((within == 0) & (odd == 0), 1, 0), jnp.where(within % 2 == 0, 1, 0))
        passage = jnp.where(long, jnp.where((within == 0) & (odd == 1), 1, 0), jnp.where(within % 2 == 1, 1, 0))
        return query > 0, passage > 0, jnp.where(long, t + 4, t + 1)

    _, passage, _ = roles((8, slots), 1)
    query, _, partner = roles((slots, 128), 0)
    passage, query, partner = passage[:1], query[:, :1], partner[:, :1]
    pair_count = jnp.zeros((), single)
    for b in range(buckets):
        pair_count = pair_count + (4 - 3 * bucket[b]).astype(single)
    keep.wait()
    for s in by_z:
        s.wait_recv()
    others = []
    for yy in range(2):
        for xx in range(2):
            for zz in range(4):
                others.append(wires.copy(block(xx, yy, zz), block(xx, yy, zz), device_at(x, y, z, 1 - c)))
    for s in others:
        s.wait_recv()
    both = every[...].astype(single)
    left = both[:, :8, :].reshape(slots, hw).astype(narrow)
    right = both[:, 8:, :].reshape(slots, hw).astype(narrow)
    logits = (dot_nt(left, left) + dot_nt(right, right)) * 100.0
    masked = jnp.where(passage, logits, -1000000000.0)
    top = jnp.max(masked, -1, keepdims=True)
    raised = jnp.exp(masked - top)
    total = jnp.sum(raised, -1, keepdims=True)
    match = lax.broadcasted_iota(jnp.int32, (slots, slots), 1) == partner
    positive = jnp.sum(jnp.where(match, logits, 0.0), -1, keepdims=True)
    terms = jnp.where(query, top + jnp.log(total) - positive, 0.0)
    loss = jnp.sum(terms, 0, keepdims=True) / pair_count
    loss_o[...] = jnp.broadcast_to(loss, loss_o.shape)
    weight = jnp.where(query, 1.0, 0.0) / pair_count
    logit_grad = weight * (raised / total - jnp.where(match, 1.0, 0.0))
    by_row = logit_grad.astype(narrow)
    by_column = logit_grad.T.astype(narrow)
    full[:, :hw] = dot(by_row, left) + dot(by_column, left)
    full[:, hw:] = dot(by_row, right) + dot(by_column, right)
    g = full[pl.ds(pl.multiple_of(device * 8, 8), 8), :] * 100.0
    grad_o[...] = scale * g - p * (scale * scale * scale) * jnp.sum(p * g, -1, keepdims=True)
    wires.finish()


def run_contrast(bucket, pooled, devices):
    rows, width = pooled.shape
    slots = rows * devices
    dma = pltpu.SemaphoreType.DMA
    spec_v = pl.BlockSpec(memory_space=VM)
    copies = 1 + 2 + 12 + 16
    loss, grad = pl.pallas_call(
        functools.partial(contrast_kernel, slots, bucket.shape[0]),
        out_shape=[jax.ShapeDtypeStruct((8, 128), single), jax.ShapeDtypeStruct(pooled.shape, single)],
        in_specs=[pl.BlockSpec(memory_space=SM), spec_v],
        out_specs=[spec_v, spec_v],
        scratch_shapes=[
            VM((2 * rows, width // 2), narrow), VM((devices, 2 * rows, width // 2), narrow), VM((slots, width), single),
            dma((copies,)), dma((copies,)), dma(()),
        ],
        compiler_params=pltpu.CompilerParams(collective_id=3, has_side_effects=True),
        name="contrast",
    )(bucket, pooled)
    return loss[0, 0], grad


def gather_weights(tab, w_in, w_out, w_up, w_down, small):
    gat = lambda a: lax.all_gather(a, "fsdp", axis=0, tiled=True)
    return lax.all_gather(tab, "fsdp", axis=1, tiled=True), gat(w_in), gat(w_out), gat(w_up), gat(w_down), gat(small)


def reduce_all(grads, small):
    done = []
    for a in grads:
        part = lax.psum_scatter(a.astype(single), "fsdp", scatter_dimension=0, tiled=True)
        done.append(lax.psum(part.astype(narrow), "dp").astype(single))
    return done, lax.psum(small, ("dp", "fsdp"))


def local(
    tokens, lengths, bucket, position_table, in_projection, query_bias, value_bias, out_projection, out_bias,
    first_gain, first_shift, up_projection, up_bias, down_projection, down_bias, second_gain, second_shift,
):
    groups = lengths.shape[0]
    width = tokens.shape[1]
    count = tokens.shape[0] // groups
    shards = lax.axis_size("fsdp")
    ff = up_projection.shape[1]
    fs = lax.axis_index("fsdp")
    device = lax.axis_index("dp") * shards + fs
    small_parts = (query_bias, value_bias, out_bias, first_gain, first_shift, down_bias, second_gain, second_shift)
    piece = query_bias.shape[0]
    wide_piece = up_bias.shape[0]
    flag = lax.dynamic_slice_in_dim(jnp.repeat(bucket, 2), device * groups, groups)
    chunk = 1024
    chunks, per = ff // chunk, chunk // 8
    grid = lax.axis_size("dp") == 4 and shards == 8
    if grid:
        line = jnp.concatenate([v[None] for v in small_parts] + [jnp.zeros((8, piece), narrow)], 0)
        spread = lax.dynamic_update_slice(jnp.zeros((16, chunk), narrow), line, (0, fs * piece))
        ups = up_bias.reshape(chunks, per)
        small = lax.dynamic_update_slice(spread, ups, (8, fs * per))
        table = position_table.T
        weights = (in_projection, out_projection, up_projection, down_projection)
    else:
        vectors = jnp.concatenate(small_parts + (up_bias,))[None, :]
        table, w_in, w_out, w_up, w_down, small_all = gather_weights(
            position_table, in_projection, out_projection, up_projection, down_projection, vectors
        )
        table = table.T
        heads = small_all[:, : 8 * piece].reshape(shards, 8, piece).transpose(1, 0, 2).reshape(8, width)
        ups = small_all[:, 8 * piece :].reshape(8, chunks, per).transpose(1, 0, 2).reshape(chunks, chunk)
        small = jnp.concatenate(
            [jnp.pad(heads, ((0, 0), (0, chunk - width))), ups, jnp.zeros((8 - chunks, chunk), narrow)]
        )
        w_up = w_up.reshape(width, 8, chunks, per).transpose(0, 2, 1, 3).reshape(width, ff)
        w_down = w_down.reshape(8, chunks, per, width).transpose(1, 0, 2, 3)
        weights = (w_in, w_out, w_up, w_down)
    outs = run_forward(grid, groups, count, width, ff, chunk, lengths, flag, small, tokens, table, weights)
    saved, pooled, vecs = outs[:11], outs[11], outs[12]
    if grid:
        weights = tuple(outs[14:18])
    slots = groups * 4
    if grid:
        loss, pooled_grad = run_contrast(bucket, pooled, 4 * shards)
    else:
        embedded, norm_grad = jax.vjp(normalize_rows, pooled)
        every = lax.all_gather(embedded.astype(narrow), ("dp", "fsdp"), axis=0, tiled=True)
        loss, embed_grad = contrast(every, embedded, device * slots, slots, bucket)
        pooled_grad = norm_grad(embed_grad)[0]
    tokens_grad, gin, gout, gup, gdown, gtab, gvec = run_backward(
        groups, count, width, ff, chunk, lengths, flag, vecs, pooled_grad, weights, saved
    )
    if grid:
        cut = lambda a: a.reshape(4, 2, a.shape[0] // 8, a.shape[1])
        items = [cut(a) for t in range(chunks) for a in (gdown[t], gup[t])] + [cut(gout), cut(gin), cut(gtab)]
        *done, gvec = run_reduce(items, gvec)
        gdown = jnp.stack(done[0 : 2 * chunks : 2]).reshape(wide_piece, width)
        gup = jnp.stack([a.reshape(piece, 8, per) for a in done[1 : 2 * chunks : 2]], 2).reshape(piece, ff)
        gout, gin, gtab = done[2 * chunks :]
    else:
        gdown = gdown.reshape(chunks, 8, per, width).transpose(1, 0, 2, 3).reshape(ff, width)
        gup = gup.reshape(chunks, width, 8, per).transpose(1, 2, 0, 3).reshape(width, ff)
        (gin, gout, gup, gdown, gtab), gvec = reduce_all((gin, gout, gup, gdown, gtab), gvec)
    gtab = gtab.T
    own = [lax.dynamic_slice_in_dim(gvec[i], fs * piece, piece) for i in range(8)]
    ups = gvec[8 : 8 + chunks].reshape(chunks, 8, per).transpose(1, 0, 2).reshape(ff)
    up_own = lax.dynamic_slice_in_dim(ups, fs * wide_piece, wide_piece)
    return (
        loss, pooled, tokens_grad, gtab, gin, own[0], own[1], gout, own[2], own[3], own[4], gup, up_own, gdown,
        own[5], own[6], own[7],
    )


def solution(mesh):
    rows = P(("dp", "fsdp"), None)
    vec = P("fsdp")
    mat = P("fsdp", None)
    in_specs = (rows, rows, P(), P(None, "fsdp"), mat, vec, vec, mat, vec, vec, vec, mat, vec, mat, vec, vec, vec)
    out_specs = (P(), rows, rows, P(None, "fsdp"), mat, vec, vec, mat, vec, vec, vec, mat, vec, mat, vec, vec, vec)
    return jax.shard_map(local, mesh=mesh, in_specs=in_specs, out_specs=out_specs, check_vma=False)
```

```python
import functools

import jax
import jax.numpy as jnp
from jax import lax
from jax.experimental import pallas as pl
from jax.experimental.pallas import tpu as pltpu
from jax.sharding import PartitionSpec as P

H = 12
narrow = jnp.bfloat16
single = jnp.float32
ANY = pl.ANY
VM = pltpu.VMEM
SM = pltpu.SMEM
LIMIT = 60 * 2**20


def dot(a, b):
    return lax.dot_general(a, b, (((1,), (0,)), ((), ())), preferred_element_type=single)


def dot_nt(a, b):
    return lax.dot_general(a, b, (((1,), (1,)), ((), ())), preferred_element_type=single)


def at(start, size):
    return pl.ds(pl.multiple_of(start, 128), size)


def gelu_pair(u):
    t = 1.0 / (1.0 + 0.23164189 * jnp.abs(u))
    e = jnp.exp(-0.5 * (u * u))
    tail = t * (
        0.127414796 + t * (-0.142248368 + t * (0.7107068705 + t * (-0.7265760135 + t * 0.5307027145)))
    )
    tail = tail * e
    phi = jnp.where(u < 0, tail, 1.0 - tail)
    return u * phi, phi + u * (e * 0.3989422804)


def norm_rows(value):
    mean = jnp.mean(value, -1, keepdims=True)
    centred = value - mean
    rstd = lax.rsqrt(jnp.mean(centred * centred, -1, keepdims=True) + 1e-06)
    return centred * rstd, rstd


def norm_back(grad, unit, rstd):
    one = jnp.mean(grad, -1, keepdims=True)
    two = jnp.mean(grad * unit, -1, keepdims=True)
    return rstd * (grad - one - unit * two)


def slot_lengths(lens, flag, g, along_rows, count, width):
    slot = count // 4
    shape = (count, width) if along_rows else (8, count)
    t = lax.broadcasted_iota(jnp.int32, shape, 0 if along_rows else 1)
    which = t // slot
    long = flag[g] > 0
    limit = jnp.where(which == 0, lens[g, 0], lens[g, 1])
    limit = jnp.where(which == 2, lens[g, 2], limit)
    limit = jnp.where(which == 3, lens[g, 3], limit)
    limit = jnp.where(long, lens[g, 0], limit)
    inside = jnp.where(long, t, t % slot)
    return which, inside < limit


FEED_SUMS = ((), (), (2,))
WEIGH_SUMS = ((), (), ())
FIRST_SUMS = 1
ATTEND_SUMS = (2, 6, 10)
IN_SUMS = ((), (1,), ())
TOKEN_SUMS = (1,)


def item_shapes(count, width, ff, chunk):
    found = []
    for _ in range(ff // chunk):
        found += [(chunk // 8, width), (width // 8, chunk)]
    return found + [(width // 8, width)] * 4 + [(width // 8, count)]


def backward_kernel(
    sizes, remote,
    lens, flag, vecs, pg, w_in, w_out, w_up, w_down, x_i, mixed_i, prob_i, ctx_i, hid_i, n1_i, r1_i, act_i, gp_i, n2_i, r2_i,
    *refs,
):
    groups, count, width, ff, chunk = sizes
    rows = groups * count
    pairs = width // 128
    slot = count // 4
    wide = ff // chunk
    blocks = rows // 256
    per = chunk // 8
    shapes = item_shapes(count, width, ff, chunk)
    items = len(shapes)
    tok_o, item_o, gvec_o, refs = refs[0], refs[1 : 1 + items], refs[1 + items], refs[2 + items :]
    (
        v_in, v_out, v_up, v_down, mixed, ctx, unit_v, rstd_v, ast, gst, low, hid_t, up_low, grad, dctx, stage_a, stage_b,
        gsmall, in_sem, p_sem, o_sem, i_sem,
    ) = refs[:22]
    wires = refs[22:]
    load = [
        pltpu.make_async_copy(s, d, in_sem.at[i])
        for i, (s, d) in enumerate(
            (
                (n2_i, unit_v), (r2_i, rstd_v), (hid_i, dctx), (n1_i, unit_v), (r1_i, rstd_v), (ctx_i, ctx),
                (w_out, v_out), (mixed_i, mixed), (x_i, low), (w_in, v_in),
            )
        )
    ]
    l_n2, l_r2, l_hid, l_n1, l_r1, l_ctx, l_wout, l_mixed, l_x, l_win = load

    def chunk_loads(j):
        down = w_down.at[j] if len(w_down.shape) == 4 else w_down.at[:, pl.ds(j * per, per), :]
        return (
            pltpu.make_async_copy(down, v_down, in_sem.at[10]),
            pltpu.make_async_copy(gp_i.at[j], gst, in_sem.at[11]),
            pltpu.make_async_copy(w_up.at[:, pl.ds(j * chunk, chunk)], v_up, in_sem.at[12]),
        )

    def act_load(j):
        return pltpu.make_async_copy(act_i.at[j], ast, in_sem.at[13])

    def prob_loads(i, s_):
        return [
            pltpu.make_async_copy(
                prob_i.at[i, h],
                up_low.at[pl.ds(pl.multiple_of(s_ * count, count), count), pl.ds(h * count, count)],
                p_sem.at[2 * s_ + h],
            )
            for h in range(2)
        ]

    l_n2.start()
    l_r2.start()
    l_hid.start()
    for made in chunk_loads(0):
        made.start()
    act_load(0).start()
    for made in (l_ctx, l_wout, l_mixed, l_win):
        made.start()

    def vec(i):
        return vecs[i : i + 1, :width]

    def staged(t, lead=None):
        r, k = shapes[t]
        ref = stage_a if t % 2 == 0 else stage_b
        if lead is None:
            return ref.at[:, :, pl.ds(0, r), pl.ds(0, k)]
        return ref.at[:, lead, pl.ds(0, r), pl.ds(0, k)]

    steps = []
    done = [0]
    firsts = [0]
    if remote:
        send, recv, free, total_v, got_v, ring = wires[:6]
        held = wires[6:]
        here = place()
        x, y, z, c = here
        sums = [Sum(t, (send, recv), here, *held[7 * t : 7 * t + 7]) for t in range(items)]
        tiny = SumSmall(Sum.COPIES * items, (send, recv), here, total_v, got_v)

        def slot_of(t):
            r, k = shapes[t]
            return ring.at[t % 3, :, pl.ds(0, r), pl.ds(0, k)]

        def crossing(t):
            return sums[t].to_core(staged(t, 1 - c), slot_of(t))

        def item_store(t):
            return pltpu.make_async_copy(sums[t].final, item_o[t], i_sem.at[t])

        def first(t):
            while firsts[0] <= t:
                n = firsts[0]
                crossing(n).wait_recv()
                sums[n].first(staged(n), slot_of(n))
                if n + 3 < items:
                    pl.semaphore_signal(free, inc=1, device_id=device_at(x, y, z, 1 - c), device_id_type=MESH)
                firsts[0] += 1

        def ready(t):
            if t >= 2:
                first(t - 2)
                crossing(t - 2).wait_send()

        def produced(t):
            if t >= 3:
                pl.semaphore_wait(free, 1)
            crossing(t).start()
            if t >= 1:
                first(t - 1)

        def step(u):
            for stage, behind in (("second", 0), ("third", 1), ("fourth", 2), ("finish", 3)):
                t = u - behind
                if 0 <= t < items:
                    getattr(sums[t], stage)()
                    if stage == "finish":
                        item_store(t).start()

        steps = [functools.partial(step, u) for u in range(items + 3)]
    else:

        def item_store(t):
            return pltpu.make_async_copy(staged(t), item_o[t], i_sem.at[t])

        def first(t):
            pass

        def ready(t):
            if t >= 2:
                item_store(t - 2).wait()

        def produced(t):
            item_store(t).start()

    def pump(n=1):
        for _ in range(n):
            if done[0] < len(steps):
                steps[done[0]]()
                done[0] += 1

    def pump_in(i, when):
        for n, count_ in enumerate(when):
            if done[0] + n < len(steps):

                @pl.when(i == count_)
                def _(n=n):
                    steps[done[0] + n]()

    def pumped(when):
        done[0] = min(len(steps), done[0] + len(when))

    def put(t, b, out):
        r, k = shapes[t]
        ref = stage_a if t % 2 == 0 else stage_b
        out = out.astype(narrow)
        ref[b, 0, :r, :k] = out[:r]
        ref[b, 1, :r, :k] = out[r:]

    def second_norm():
        l_n2.wait()
        l_r2.wait()
        gain_sum = jnp.zeros((1, width), single)
        shift_sum = jnp.zeros((1, width), single)
        bias_sum = jnp.zeros((1, width), single)
        for g in range(groups):
            _, live = slot_lengths(lens, flag, g, True, count, 128)
            long = flag[g] > 0
            for s in range(4):
                r = pl.ds(g * count + s * slot, slot)
                mine = pg[4 * g + s : 4 * g + s + 1, :] / jnp.maximum(lens[g, s], 1).astype(single)
                whole = pg[4 * g : 4 * g + 1, :] / jnp.maximum(lens[g, 0], 1).astype(single)
                row = jnp.where(long, whole, mine)
                keep = live[s * slot : (s + 1) * slot, :1]
                d = jnp.where(keep, row, 0.0)
                unit = unit_v[r, :]
                gain_sum = gain_sum + jnp.sum(d * unit, 0, keepdims=True)
                shift_sum = shift_sum + jnp.sum(d, 0, keepdims=True)
                back = norm_back(d * vec(6), unit, rstd_v[r, :1])
                grad[r, :] = back
                lowered = back.astype(narrow)
                low[r, :] = lowered
                bias_sum = bias_sum + jnp.sum(lowered.astype(single), 0, keepdims=True)
        gsmall[...] = jnp.zeros_like(gsmall)
        gsmall[6:7, :width] = gain_sum
        gsmall[7:8, :width] = shift_sum
        gsmall[5:6, :width] = bias_sum
        l_n1.start()
        l_r1.start()
        l_hid.wait()
        for b in range(rows // slot):
            r = pl.ds(b * slot, slot)
            hid_t[:, r] = dctx[r, :].T

    if remote:
        greet(neighbours(False) + [device_at(1 - x, 1 - y, z, c)], second_norm)
    else:
        second_norm()

    for j in range(wide):
        for made in chunk_loads(j):
            made.wait()

        def feed(b, total, j=j):
            pump_in(b, FEED_SUMS[j])
            r = at(b * 256, 256)
            up = (dot_nt(low[r, :], v_down[...].reshape(chunk, width)) * gst[r, :].astype(single)).astype(narrow)
            up_low[r, :] = up
            grad[r, :] += dot_nt(up, v_up[...])
            return total + jnp.sum(up.astype(single), 0, keepdims=True)

        gsmall[8 + j : 9 + j, :] = lax.fori_loop(0, blocks, feed, jnp.zeros((1, chunk), single))
        pumped(FEED_SUMS[j])
        if j + 1 < wide:
            for made in chunk_loads(j + 1):
                made.start()
        act_load(j).wait()
        ready(2 * j)

        def weigh(b, _, j=j):
            put(2 * j, b, dot(ast[:, at(b * 256, 256)].T, low[...]))
            return 0

        lax.fori_loop(0, 4, weigh, 0)
        produced(2 * j)
        if j + 1 < wide:
            act_load(j + 1).start()
        ready(2 * j + 1)

        def weigh_up(b, _, j=j):
            pump_in(b, WEIGH_SUMS[j])
            put(2 * j + 1, b, dot(hid_t[pl.ds(pl.multiple_of(b * (width // 4), 64), width // 4), :], up_low[...]))
            return 0

        lax.fori_loop(0, 4, weigh_up, 0)
        pumped(WEIGH_SUMS[j])
        produced(2 * j + 1)

    for made in prob_loads(0, 0) + prob_loads(1, 1):
        made.start()

    l_n1.wait()
    l_r1.wait()
    l_ctx.wait()
    l_wout.wait()
    gain_sum = jnp.zeros((1, width), single)
    shift_sum = jnp.zeros((1, width), single)
    bias_sum = jnp.zeros((1, width), single)
    for b in range(rows // slot):
        r = pl.ds(b * slot, slot)
        d = grad[r, :]
        unit = unit_v[r, :]
        gain_sum = gain_sum + jnp.sum(d * unit, 0, keepdims=True)
        shift_sum = shift_sum + jnp.sum(d, 0, keepdims=True)
        back = norm_back(d * vec(3), unit, rstd_v[r, :1])
        grad[r, :] = back
        lowered = back.astype(narrow)
        low[r, :] = lowered
        bias_sum = bias_sum + jnp.sum(lowered.astype(single), 0, keepdims=True)
        hid_t[:, r] = ctx[r, :].T
    gsmall[3:4, :width] = gain_sum
    gsmall[4:5, :width] = shift_sum
    gsmall[2:3, :width] = bias_sum
    pump(FIRST_SUMS)

    def weigh_by_columns(t, other):
        def body(b, _):
            put(t, b, dot(hid_t[pl.ds(pl.multiple_of(b * (width // 4), 64), width // 4), :], other()))
            return 0

        lax.fori_loop(0, 4, body, 0)

    t_out = 2 * wide
    ready(t_out)
    weigh_by_columns(t_out, lambda: low[...])
    produced(t_out)

    def context_back(b, _):
        r = at(b * 256, 256)
        dctx[r, :] = dot_nt(low[r, :], v_out[...]).astype(narrow)
        return 0

    lax.fori_loop(0, blocks, context_back, 0)
    l_x.start()
    first(t_out)

    l_mixed.wait()
    lane = lax.broadcasted_iota(jnp.int32, (count, 128), 1)
    half = (lane < 64, lane >= 64)
    scale = jnp.asarray(0.125, narrow)
    n = groups * pairs

    def attend(i, _):
        g = i // pairs
        p = i % pairs
        s_ = i % 2
        r = at(g * count, count)
        pump_in(i, ATTEND_SUMS)
        for made in prob_loads(i, s_):
            made.wait()
        c_q = at(p * 128, 128)
        c_k = at(width + p * 128, 128)
        c_v = at(2 * width + p * 128, 128)
        q = mixed[r, c_q] * scale
        k = mixed[r, c_k]
        v = mixed[r, c_v]
        dc = dctx[r, c_q]
        c = ctx[r, c_q]
        q_t = q.T
        dc_t = dc.T
        zero = jnp.zeros_like(q)
        prod = dc.astype(single) * c.astype(single)
        dq = [None] * (count // 256)
        dk_t = []
        dv_t = []
        for h in range(2):
            dch = jnp.where(half[h], dc, zero)
            kh = jnp.where(half[h], k, zero)
            d = jnp.sum(jnp.where(half[h], prod, 0.0), -1, keepdims=True)
            dkh = None
            dvh = None
            for b in range(count // 256):
                rb = slice(b * 256, (b + 1) * 256)
                prob = up_low[pl.ds(pl.multiple_of(s_ * count + b * 256, 256), 256), h * count : (h + 1) * count]
                dp = dot_nt(dch[rb], v)
                ds = (prob.astype(single) * (dp - d[rb])).astype(narrow)
                o = dot(ds, kh)
                dq[b] = o if dq[b] is None else dq[b] + o
                hr = slice(h * 64, (h + 1) * 64)
                one = dot(q_t[hr, rb], ds)
                two = dot(dc_t[hr, rb], prob)
                dkh = one if dkh is None else dkh + one
                dvh = two if dvh is None else dvh + two
            dk_t.append(dkh)
            dv_t.append(dvh)
        for b in range(count // 256):
            mixed[at(g * count + b * 256, 256), c_q] = (dq[b] * 0.125).astype(narrow)
        mixed[r, c_k] = jnp.concatenate(dk_t, 0).T.astype(narrow)
        mixed[r, c_v] = jnp.concatenate(dv_t, 0).T.astype(narrow)

        @pl.when(i + 2 < n)
        def _():
            for made in prob_loads(i + 2, s_):
                made.start()

        return 0

    lax.fori_loop(0, n, attend, 0)
    pumped(ATTEND_SUMS)

    l_x.wait()
    l_win.wait()
    for b in range(rows // slot):
        r = pl.ds(b * slot, slot)
        hid_t[:, r] = low[r, :].T
    for part in range(3):
        cols = pl.ds(part * width, width)
        ready(t_out + 1 + part)

        def in_weigh(b, _, cols=cols, part=part):
            pump_in(b, IN_SUMS[part])
            put(t_out + 1 + part, b, dot(hid_t[pl.ds(pl.multiple_of(b * (width // 4), 64), width // 4), :], mixed[:, cols]))
            return 0

        lax.fori_loop(0, 4, in_weigh, 0)
        pumped(IN_SUMS[part])
        produced(t_out + 1 + part)

    def bias(b, total):
        r = at(b * 256, 256)
        return (
            total[0] + jnp.sum(mixed[r, :width].astype(single), 0, keepdims=True),
            total[1] + jnp.sum(mixed[r, 2 * width :].astype(single), 0, keepdims=True),
        )

    zero_row = jnp.zeros((1, width), single)
    q_sum, v_sum = lax.fori_loop(0, blocks, bias, (zero_row, zero_row))
    gsmall[0:1, :width] = q_sum
    gsmall[1:2, :width] = v_sum
    if remote:
        total_v[0] = gsmall[...]
        tiny.begin()

    def token_back(b, _):
        pump_in(b, TOKEN_SUMS)
        r = at(b * 256, 256)
        grad[r, :] += dot_nt(mixed[r, :], v_in[...])
        return 0

    lax.fori_loop(0, blocks, token_back, 0)
    pumped(TOKEN_SUMS)
    tok_store = pltpu.make_async_copy(grad, tok_o, o_sem.at[0])
    tok_store.start()
    last = items - 1
    ready(last)
    ref = stage_a if last % 2 == 0 else stage_b
    for s in range(4):
        total = None
        for g in range(groups):
            long = flag[g] > 0
            r = pl.ds(g * count + s * slot, slot)
            if s == 0:
                other = grad[r, :]
                for o in range(1, 4):
                    other = other + grad[pl.ds(g * count + o * slot, slot), :]
                piece = jnp.where(long, grad[r, :], other)
            else:
                piece = jnp.where(long, grad[r, :], 0.0)
            total = piece if total is None else total + piece
        turned = total.T.astype(narrow)
        for fs in range(8):
            ref[fs // 2, fs % 2, : width // 8, s * slot : (s + 1) * slot] = turned[
                fs * (width // 8) : (fs + 1) * (width // 8), :
            ]
    produced(last)
    if remote:
        first(last)
        for i in range(3):
            pump()
            tiny.step(i)
        while done[0] < len(steps):
            pump()
        tiny.finish(gvec_o)
        for t in range(items):
            item_store(t).wait()
            sums[t].sent()
        for t in (items - 2, items - 1):
            crossing(t).wait_send()
    else:
        gvec_o[...] = gsmall[...]
        for t in (items - 2, items - 1):
            item_store(t).wait()
    tok_store.wait()


def finish_kernel(shapes, wide, *refs):
    given, (down, up, out, qkv, tab) = refs[: len(shapes)], refs[len(shapes) :]
    for t in range(wide):
        r, k = shapes[2 * t]
        down[t * r : (t + 1) * r, :] = given[2 * t][...].astype(single)
        _, k = shapes[2 * t + 1]
        part = k // 8
        for fs in range(8):
            up[:, fs * wide * part + t * part : fs * wide * part + (t + 1) * part] = given[2 * t + 1][
                :, fs * part : (fs + 1) * part
            ].astype(single)
    out[...] = given[2 * wide][...].astype(single)
    n = shapes[2 * wide + 1][1]
    for i in range(3):
        qkv[:, i * n : (i + 1) * n] = given[2 * wide + 1 + i][...].astype(single)
    tab[...] = given[2 * wide + 4][...].astype(single).T


def run_finish(shapes, wide, given):
    (r_down, width), (r, chunk) = shapes[0], shapes[1]
    count = shapes[-1][1]
    sds = jax.ShapeDtypeStruct
    return pl.pallas_call(
        functools.partial(finish_kernel, shapes, wide),
        out_shape=[
            sds((r_down * wide, width), single), sds((r, chunk * wide), single), sds((r, width), single),
            sds((r, 3 * width), single), sds((count, r), single),
        ],
        name="finish",
    )(*given)


def shapes_of(groups, count, width, ff, chunk):
    rows = groups * count
    pairs = width // 128
    chunks = ff // chunk
    return dict(
        x=((rows, width), narrow),
        mixed=((rows, 3 * width), narrow),
        prob=((groups * pairs, 2, count, count), narrow),
        ctx=((rows, width), narrow),
        hid=((rows, width), narrow),
        n1=((rows, width), single),
        r1=((rows, 128), single),
        act=((chunks, rows, chunk), narrow),
        gp=((chunks, rows, chunk), narrow),
        n2=((rows, width), single),
        r2=((rows, 128), single),
    )


def run_forward(remote, groups, count, width, ff, chunk, lens, flag, small, tok, tab, weights):
    rows = groups * count
    chunks = ff // chunk
    saved = shapes_of(groups, count, width, ff, chunk)
    outs = [jax.ShapeDtypeStruct(*v) for v in saved.values()]
    outs.append(jax.ShapeDtypeStruct((groups * 4, width), single))
    outs.append(jax.ShapeDtypeStruct((16, chunk), single))
    spec_any = pl.BlockSpec(memory_space=ANY)
    spec_v = pl.BlockSpec(memory_space=VM)
    spec_s = pl.BlockSpec(memory_space=SM)
    dma = pltpu.SemaphoreType.DMA
    n_items = 5 + 2 * chunks
    extra = []
    if remote:
        whole = [
            jax.ShapeDtypeStruct((width, count), narrow),
            jax.ShapeDtypeStruct((width, 3 * width), narrow),
            jax.ShapeDtypeStruct((width, width), narrow),
            jax.ShapeDtypeStruct((width, ff), narrow),
            jax.ShapeDtypeStruct((8, ff // 8, width), narrow),
        ]
        outs += whole
        copies = Piece.COPIES * n_items + 8
        extra = [dma((copies,)), dma((copies,)), dma((6,))]
        body = functools.partial(forward_kernel, (groups, count, width, ff, chunk), True)
    else:

        def body(*refs):
            head = 9
            given = refs[4:head]
            rest = refs[head:]
            return forward_kernel((groups, count, width, ff, chunk), False, *refs[:head], *rest[:13], *given, *rest[13:])

    per = chunk // 8
    return pl.pallas_call(
        body,
        out_shape=outs,
        in_specs=[spec_s, spec_s, spec_any] + [spec_any] * 6,
        out_specs=[spec_any] * 11 + [spec_v, spec_v] + [spec_any] * (5 if remote else 0),
        scratch_shapes=[
            VM((width, 3 * width), narrow),
            VM((width, width), narrow),
            VM((width, ff), narrow),
            VM((chunks, 8, per, width), narrow),
            VM((width, count), narrow),
            VM((rows, width), narrow),
            VM((rows, 3 * width), narrow),
            VM((groups, count, count), single),
            VM((2, 2, count, count), narrow),
            VM((rows, width), narrow),
            VM((rows, width), single),
            VM((rows, width), narrow),
            VM((rows, width), single),
            VM((rows, 128), single),
            VM((rows, 128), single),
            VM((2, rows, chunk), narrow),
            VM((2, rows, chunk), narrow),
            VM((rows, width), single),
            VM((8, 16, chunk) if remote else (16, chunk), narrow),
            VM((width // 8, ff) if remote else (16, 128), narrow),
            VM((width // 8, ff) if remote else (16, 128), narrow),
            VM((width // 8, count) if remote else (16, 128), narrow),
            VM((width // 8, 3 * width) if remote else (16, 128), narrow),
            VM((width // 8, width) if remote else (16, 128), narrow),
            VM((ff // 8, width) if remote else (16, 128), narrow),
            dma((6,)), dma((10,)), dma((2,)), dma((4,)), dma((n_items,)),
        ]
        + extra,
        compiler_params=pltpu.CompilerParams(
            vmem_limit_bytes=LIMIT, **(dict(collective_id=1, has_side_effects=True) if remote else {})
        ),
        cost_estimate=pl.CostEstimate(flops=2 * rows * width * (4 * width + 2 * ff), bytes_accessed=80 * 2**20, transcendentals=10**7),
        name="encoder_forward",
    )(lens, flag, small, tok, tab, *weights)


def run_backward(remote, groups, count, width, ff, chunk, lens, flag, vecs, pooled_grad, weights, saved):
    rows = groups * count
    chunks, per = ff // chunk, chunk // 8
    shapes = item_shapes(count, width, ff, chunk)
    items = len(shapes)
    spec_any = pl.BlockSpec(memory_space=ANY)
    spec_v = pl.BlockSpec(memory_space=VM)
    spec_s = pl.BlockSpec(memory_space=SM)
    dma = pltpu.SemaphoreType.DMA
    tall = max(r for r, _ in shapes)
    broad = max(k for _, k in shapes)
    extra = []
    if remote:
        copies = Sum.COPIES * items + SumSmall.COPIES
        extra = [
            dma((copies,)), dma((copies,)), pltpu.SemaphoreType.REGULAR, VM((4, 16, chunk), single), VM((6, 16, chunk), single),
            VM((3, 4, tall, broad), narrow),
        ]
        for r, k in shapes:
            extra += [
                VM((4, r, k), narrow), VM((2, r // 2, k), narrow), VM((2, r, k // 2), narrow), VM((2, r // 2, k // 2), narrow),
                VM((2, r // 2, k // 2), narrow), VM((3, r // 2, k // 2), narrow), VM((r, k), narrow),
            ]
    outs = [jax.ShapeDtypeStruct((rows, width), single)]
    outs += [jax.ShapeDtypeStruct((r, k) if remote else (4, 2, r, k), narrow) for r, k in shapes]
    outs += [jax.ShapeDtypeStruct((16, chunk), single)]
    tok, *blocks, gvec = pl.pallas_call(
        functools.partial(backward_kernel, (groups, count, width, ff, chunk), remote),
        out_shape=outs,
        in_specs=[spec_s, spec_s, spec_v, spec_v] + [spec_any] * 15,
        out_specs=[spec_any] * (1 + items) + [spec_v],
        scratch_shapes=[
            VM((width, 3 * width), narrow),
            VM((width, width), narrow),
            VM((width, chunk), narrow),
            VM((8, per, width), narrow),
            VM((rows, 3 * width), narrow),
            VM((rows, width), narrow),
            VM((rows, width), single),
            VM((rows, 128), single),
            VM((rows, chunk), narrow),
            VM((rows, chunk), narrow),
            VM((rows, width), narrow),
            VM((width, rows), narrow),
            VM((rows, chunk), narrow),
            VM((rows, width), single),
            VM((rows, width), narrow),
            VM((4, 2, tall, max(k for _, k in shapes[::2])), narrow),
            VM((4, 2, max(r for r, _ in shapes[1::2]), broad), narrow),
            VM((16, chunk), single),
            dma((14,)), dma((4,)), dma((1,)), dma((items,)),
        ]
        + extra,
        compiler_params=pltpu.CompilerParams(
            vmem_limit_bytes=62 * 2**20, **(dict(collective_id=2, has_side_effects=True) if remote else {})
        ),
        cost_estimate=pl.CostEstimate(flops=4 * rows * width * (4 * width + 2 * ff), bytes_accessed=100 * 2**20, transcendentals=0),
        name="encoder_backward",
    )(lens, flag, vecs, pooled_grad, *weights, *saved)
    return tok, blocks, gvec


def forward_kernel(
    sizes, remote,
    lens, flag, small, tok, tab_s, in_s, out_s, up_s, down_s,
    x_o, mixed_o, prob_o, ctx_o, hid_o, n1_o, r1_o, act_o, gp_o, n2_o, r2_o, pooled_o, vecs_o, w_tab, w_in, w_out, w_up, w_down,
    v_in, v_out, v_up, v_down, tab_v, x_v, mixed, mask, pst, ctx, hid, hid_low, n_st, r1_v, r2_v, ast, gst, acc, small_v, up_v, up_p, tab_p, in_p, out_p, down_p,
    in_sem, out_sem, p_sem, a_sem, w_sem, *wires,
):
    groups, count, width, ff, chunk = sizes
    rows = groups * count
    pairs = width // 128
    slot = count // 4
    chunks = ff // chunk
    shards = 8
    load_tok = pltpu.make_async_copy(tok, x_v, in_sem.at[0])
    load_tok.start()
    loads = {}

    def load(name, src, dst):
        loads[name] = pltpu.make_async_copy(src, dst, w_sem.at[len(loads)])
        return loads[name]

    def before():
        for g in range(groups):
            which_q, _ = slot_lengths(lens, flag, g, True, count, 128)
            which_k, live_k = slot_lengths(lens, flag, g, False, count, 128)
            long = flag[g] > 0
            wq = which_q[:, :1]
            open_ = live_k[:1] & (long | (wq == which_k[:1]))
            mask[g] = jnp.where(open_, 0.0, -1000000000.0).astype(single)
        if remote:
            for made in stage:
                made.wait()
            part = chunk // shards
            for fs in range(shards):
                for t in range(chunks):
                    up_p[:, t * chunk + fs * part : t * chunk + (fs + 1) * part] = up_v[
                        :, fs * (ff // shards) + t * part : fs * (ff // shards) + (t + 1) * part
                    ]

    cols = lambda ref, i, n: ref.at[:, pl.ds(i * n, n)]
    down_of = lambda t: w_down.at[:, pl.ds(t * (chunk // shards), chunk // shards), :] if remote else w_down.at[t]
    load("tab", w_tab, tab_v)
    for i in range(3):
        load("in%d" % i, cols(w_in, i, width), cols(v_in, i, width))
    load("out", w_out, v_out)
    for t in range(chunks):
        load("up%d" % t, cols(w_up, t, chunk), cols(v_up, t, chunk))
        load("down%d" % t, down_of(t), v_down.at[t])
    names = list(loads)
    if remote:
        send, recv, own_sem = wires
        here = place()
        x, y, z, c = here
        mine = 2 * z + c
        stage = [
            pltpu.make_async_copy(s, d, in_sem.at[1 + i])
            for i, (s, d) in enumerate(((tab_s, tab_p), (in_s, in_p), (up_s, up_v), (out_s, out_p), (down_s, down_p)))
        ]
        for made in stage:
            made.start()
        greet(neighbours(True), before)
        down_flat = w_down.reshape(ff, width)
        pieces = []
        for n, name in enumerate(names):
            part = int(name[-1]) if name[-1].isdigit() else 0
            kind = name.rstrip("0123456789")
            shard, full, pitch, rr, cc = {
                "tab": (tab_p, w_tab, width // shards, (0, width // shards), (0, count)),
                "in": (in_p, w_in, width // shards, (0, width // shards), (part * width, width)),
                "out": (out_p, w_out, width // shards, (0, width // shards), (0, width)),
                "up": (up_p, w_up, width // shards, (0, width // shards), (part * chunk, chunk)),
                "down": (down_p, down_flat, ff // shards, (part * (chunk // shards), chunk // shards), (0, width)),
            }[kind]
            pieces.append(Piece(n, (send, recv), here, shard, full, pitch, rr, cc))
        extra = Piece.COPIES * len(pieces)

        def small_copy(k, j):
            i = extra + 2 * k + j - 1
            return pltpu.make_async_remote_copy(
                src_ref=small, dst_ref=small_v.at[mine], send_sem=send.at[i], recv_sem=recv.at[i],
                device_id=device_at(x, y, (z + k) % 4, (c + j) % 2), device_id_type=MESH,
            )

        others = [(k, j) for k in range(4) for j in range(2) if (k, j) != (0, 0)]
        own = [
            pltpu.make_async_copy(s, d, own_sem.at[i])
            for i, (s, d) in enumerate(
                (
                    (small, small_v.at[mine]),
                    (tab_p, w_tab.at[pl.ds(pl.multiple_of(mine * (width // shards), 16), width // shards), :]),
                    (in_p, w_in.at[pl.ds(pl.multiple_of(mine * (width // shards), 16), width // shards), :]),
                    (out_p, w_out.at[pl.ds(pl.multiple_of(mine * (width // shards), 16), width // shards), :]),
                    (up_p, w_up.at[pl.ds(pl.multiple_of(mine * (width // shards), 16), width // shards), :]),
                    (down_p, w_down.at[mine]),
                )
            )
        ]
        own_of = {"tab": 1, "in": 2, "out": 3, "up": 4, "down": 5}

        def step(t):
            if t < len(pieces):
                pieces[t].begin()
            for stage, back in (("plane", 1), ("diagonal", 2), ("core", 3), ("finish", 4)):
                if 0 <= t - back < len(pieces):
                    getattr(pieces[t - back], stage)()
                    if stage == "finish":
                        name = names[t - back]
                        kind = name.rstrip("0123456789")
                        if name in (kind, kind + "0"):
                            own[own_of[kind]].wait()
                        loads[name].start()

        for k, j in others:
            small_copy(k, j).start()
        pieces[0].begin()
        for i in (0, 1, 2, 3, 5):
            own[i].start()
        own[4].start()
        steps = [functools.partial(step, t) for t in range(len(pieces) + 4)]
        first_begin = pieces[0].begin
        pieces[0].begin = lambda: None
    else:
        before()
        steps = []
        for n in names:
            loads[n].start()
        little = pltpu.make_async_copy(small, small_v, in_sem.at[1])
        little.start()
    done = [0]

    def pump(upto):
        while done[0] < min(upto, len(steps)):
            steps[done[0]]()
            done[0] += 1

    def pump_in(i, when):
        for n, count_ in enumerate(when):
            if done[0] + n < len(steps):

                @pl.when(i == count_)
                def _(n=n):
                    steps[done[0] + n]()

    def pumped(when):
        done[0] = min(len(steps), done[0] + len(when))

    def need(name):
        pump(names.index(name) + 5)
        loads[name].wait()

    stores = []

    def store(src, dst):
        made = pltpu.make_async_copy(src, dst, out_sem.at[len(stores)])
        made.start()
        stores.append(made)

    need("tab")
    load_tok.wait()
    for g in range(groups):
        long = flag[g] > 0
        for s in range(4):
            part = x_v[pl.ds(g * count + s * slot, slot), :].astype(single)
            place_ = jnp.where(
                long, tab_v[:, s * slot : (s + 1) * slot].T.astype(single), tab_v[:, :slot].T.astype(single)
            )
            both = part + place_
            hid[pl.ds(g * count + s * slot, slot), :] = both
            x_v[pl.ds(g * count + s * slot, slot), :] = both.astype(narrow)
    store(x_v, x_o)
    if remote:
        own[0].wait()
        for k, j in others:
            small_copy(k, j).wait_recv()
        total = small_v[0].astype(single)
        for i in range(1, shards):
            total = total + small_v[i].astype(single)
        vecs_o[...] = total
    else:
        little.wait()
        vecs_o[...] = small_v[...].astype(single)

    def vec(i, n=width):
        return vecs_o[i : i + 1, :n]

    for part in range(3):
        need("in%d" % part)
        cs = pl.ds(part * width, width)

        def project(b, _, cs=cs, part=part):
            r = at(b * 256, 256)
            out = dot(x_v[r, :], v_in[:, cs])
            if part == 0:
                out = out + vec(0)
            if part == 2:
                out = out + vec(1)
            mixed[r, cs] = out.astype(narrow)
            return 0

        lax.fori_loop(0, rows // 256, project, 0)
    store(mixed, mixed_o)

    lane = lax.broadcasted_iota(jnp.int32, (count, 128), 1)
    half = (lane < 64, lane >= 64)
    n = groups * pairs

    def attend(i, _):
        g = i // pairs
        p = i % pairs
        s_ = i % 2
        r = at(g * count, count)

        pump_in(i, ATTEND_PUMPS)
        @pl.when(i >= 2)
        def _():
            pltpu.make_async_copy(pst.at[s_], prob_o.at[i], p_sem.at[s_]).wait()

        q = mixed[r, at(p * 128, 128)]
        k = mixed[r, at(width + p * 128, 128)]
        v = mixed[r, at(2 * width + p * 128, 128)]
        zero = jnp.zeros_like(q)
        out = [None] * (count // 256)
        for h in range(2):
            qh = jnp.where(half[h], q, zero) * jnp.asarray(0.125, narrow)
            vh = jnp.where(half[h], v, zero)
            for b in range(count // 256):
                sc = dot_nt(qh[b * 256 : (b + 1) * 256], k) + mask[g, b * 256 : (b + 1) * 256, :]
                e = jnp.exp(sc - jnp.max(sc, -1, keepdims=True))
                low = (e * (1.0 / jnp.sum(e, -1, keepdims=True))).astype(narrow)
                pst[s_, h, b * 256 : (b + 1) * 256, :] = low
                o = dot(low, vh)
                out[b] = o if out[b] is None else out[b] + o
        for b in range(count // 256):
            ctx[at(g * count + b * 256, 256), at(p * 128, 128)] = out[b].astype(narrow)
        pltpu.make_async_copy(pst.at[s_], prob_o.at[i], p_sem.at[s_]).start()
        return 0

    lax.fori_loop(0, n, attend, 0)
    pumped(ATTEND_PUMPS)
    for i in range(max(n - 2, 0), n):
        pltpu.make_async_copy(pst.at[i % 2], prob_o.at[i], p_sem.at[i % 2]).wait()
    store(ctx, ctx_o)

    need("out")

    def first(b, _):
        pump_in(b, FIRST_PUMPS)
        r = at(b * 256, 256)
        total = hid[r, :] + dot(ctx[r, :], v_out[...]) + vec(2)
        unit, rstd = norm_rows(total)
        n_st[r, :] = unit
        r1_v[r, :] = jnp.broadcast_to(rstd, (256, 128))
        h = unit * vec(3) + vec(4)
        hid_low[r, :] = h.astype(narrow)
        acc[r, :] = h + vec(5)
        return 0

    lax.fori_loop(0, rows // 256, first, 0)
    pumped(FIRST_PUMPS)
    store(n_st, n1_o)
    n1_store = stores[-1]
    store(r1_v, r1_o)
    store(hid_low, hid_o)

    def act_copies(j, s_):
        return (
            pltpu.make_async_copy(ast.at[s_], act_o.at[j], a_sem.at[s_]),
            pltpu.make_async_copy(gst.at[s_], gp_o.at[j], a_sem.at[2 + s_]),
        )

    for j in range(chunks):
        s_ = j % 2
        need("up%d" % j)
        need("down%d" % j)
        if j >= 2:
            for made in act_copies(j - 2, s_):
                made.wait()
        cs = pl.ds(j * chunk, chunk)

        def feed(b, _, s_=s_, j=j, cs=cs):
            pump_in(b, FEED_PUMPS[j])
            r = at(b * 256, 256)
            u = dot(hid_low[r, :], v_up[:, cs]) + vec(8 + j, chunk)
            a, d = gelu_pair(u)
            a = a.astype(narrow)
            ast[s_, r, :] = a
            gst[s_, r, :] = d.astype(narrow)
            acc[r, :] += dot(a, v_down[j].reshape(chunk, width))
            return 0

        lax.fori_loop(0, rows // 256, feed, 0)
        pumped(FEED_PUMPS[j])
        for made in act_copies(j, s_):
            made.start()
    for j in range(max(chunks - 2, 0), chunks):
        for made in act_copies(j, j % 2):
            made.wait()

    n1_store.wait()
    for g in range(groups):
        _, live = slot_lengths(lens, flag, g, True, count, 128)
        sums = []
        for s in range(4):
            r = pl.ds(g * count + s * slot, slot)
            unit, rstd = norm_rows(acc[r, :])
            n_st[r, :] = unit
            r2_v[r, :] = jnp.broadcast_to(rstd, (slot, 128))
            out = unit * vec(6) + vec(7)
            keep = live[s * slot : (s + 1) * slot, :1]
            sums.append(jnp.sum(jnp.where(keep, out, 0.0), 0, keepdims=True))
        long = flag[g] > 0
        for s in range(4):
            div = jnp.maximum(lens[g, s], 1).astype(single)
            if s == 0:
                total = jnp.where(long, sums[0] + sums[1] + sums[2] + sums[3], sums[0])
            else:
                total = jnp.where(long, 0.0, sums[s])
            pooled_o[4 * g + s : 4 * g + s + 1, :] = total / div
    store(n_st, n2_o)
    store(r2_v, r2_o)
    for made in stores:
        if made is not n1_store:
            made.wait()
    if remote:
        for p in pieces:
            p.sent()
        for k, j in others:
            small_copy(k, j).wait_send()


def normalize_rows(pooled):
    return pooled * lax.rsqrt(jnp.sum(pooled * pooled, -1, keepdims=True) + 1e-06)


def slot_roles(bucket):
    long_slot = jnp.repeat(jnp.repeat(bucket, 2), 4) > 0
    slots = jnp.arange(long_slot.shape[0], dtype=jnp.int32)
    within = slots % 4
    odd_group = slots // 4 % 2
    query = jnp.where(long_slot, (within == 0) & (odd_group == 0), within % 2 == 0)
    passage = jnp.where(long_slot, (within == 0) & (odd_group == 1), within % 2 == 1)
    partner = jnp.where(long_slot, slots + 4, slots + 1)
    return (query, passage, partner)


def contrast(every, own, start, rows, bucket):
    query, passage, partner = slot_roles(bucket)
    pair_count = jnp.sum(4 - 3 * bucket).astype(single)
    logits = jnp.einsum("id,jd->ij", every, every, preferred_element_type=single) * 100.0
    columns = jnp.arange(logits.shape[1], dtype=jnp.int32)
    masked = jnp.where(passage[None, :], logits, -1000000000.0)
    top = jnp.max(masked, -1, keepdims=True)
    raised = jnp.exp(masked - top)
    total = jnp.sum(raised, -1, keepdims=True)
    spread = top[:, 0] + jnp.log(total[:, 0])
    match = columns[None, :] == partner[:, None]
    positive = jnp.sum(jnp.where(match, logits, 0.0), -1)
    loss = jnp.sum(jnp.where(query, spread - positive, 0.0)) / pair_count
    row_weight = jnp.where(query, 1.0, 0.0) / pair_count
    logit_grad = (row_weight[:, None] * (raised / total - match.astype(single))).astype(narrow)
    by_row = lax.dynamic_slice_in_dim(logit_grad, start, rows, 0)
    by_column = lax.dynamic_slice_in_dim(logit_grad, start, rows, 1)
    both = jnp.dot(by_row, every, preferred_element_type=single) + jnp.einsum(
        "ij,id->jd", by_column, every, preferred_element_type=single
    )
    return loss, both * 100.0


MESH = pl.DeviceIdType.MESH


def place():
    dp, fs = lax.axis_index("dp"), lax.axis_index("fsdp")
    return dp % 2, dp // 2, fs // 2, fs % 2


def device_at(x, y, z, c):
    return (y * 2 + x, z * 2 + c)


class Wires:
    def __init__(self, send, recv):
        self.send, self.recv, self.next, self.sent = send, recv, 0, []

    def copy(self, src, dst, device):
        i = self.next
        self.next += 1
        made = pltpu.make_async_remote_copy(
            src_ref=src, dst_ref=dst, send_sem=self.send.at[i], recv_sem=self.recv.at[i],
            device_id=device, device_id_type=MESH,
        )
        made.start()
        self.sent.append(made)
        return made

    def finish(self):
        for made in self.sent:
            made.wait_send()


def greet(devices, between=None):
    barrier = pltpu.get_barrier_semaphore()
    for d in devices:
        pl.semaphore_signal(barrier, inc=1, device_id=d, device_id_type=MESH)
    if between is not None:
        between()
    pl.semaphore_wait(barrier, len(devices))


def neighbours(small_too):
    x, y, z, c = place()
    found = [device_at(1 - x, y, z, c), device_at(x, 1 - y, z, c), device_at(x, y, z, 1 - c)]
    for k in (1, 2, 3):
        found.append(device_at(x, y, (z + k) % 4, c))
        if small_too:
            found.append(device_at(x, y, (z + k) % 4, 1 - c))
    return found


ATTEND_PUMPS = (0, 3, 6, 9)
FIRST_PUMPS = (1,)
FEED_PUMPS = ((1,), (1,), ())


class Piece:
    COPIES = 17

    def __init__(self, index, sems, at_, shard, full, pitch, rows, cols):
        self.send, self.recv = sems
        self.x, self.y, self.z, self.c = at_
        self.base = index * self.COPIES
        self.shard, self.full, self.pitch = shard, full, pitch
        self.r0, self.rows = rows
        self.c0, self.cols = cols
        self.both = self.rows % 64 == 0
        self.ways = ("x", "y", "both" if self.both else ("x" if index % 2 else "y"))

    def block(self, ref, fs, a=None, b=None, part=None):
        start = self.r0 if fs is None else fs * self.pitch + self.r0
        rows, col, cols = self.rows, self.c0, self.cols
        if a is not None:
            rows, cols = rows // 2, cols // 2
            start, col = start + a * rows, col + b * cols
        if part is not None:
            rows = rows // 2
            start = start + part * rows
        return ref.at[pl.ds(pl.multiple_of(start, 16), rows), pl.ds(pl.multiple_of(col, 128), cols)]

    def copy(self, i, src, dst, device):
        return pltpu.make_async_remote_copy(
            src_ref=src, dst_ref=dst, send_sem=self.send.at[self.base + i], recv_sem=self.recv.at[self.base + i],
            device_id=device, device_id_type=MESH,
        )

    def from_z(self, k):
        return 2 * ((self.z - k + 4) % 4) + self.c

    def by_z(self, k):
        mine = 2 * self.z + self.c
        there = device_at(self.x, self.y, (self.z + k) % 4, self.c)
        return self.copy(k - 1, self.block(self.shard, None, self.x, self.y), self.block(self.full, mine, self.x, self.y), there)

    def by_x(self, k):
        mine = self.block(self.full, self.from_z(k), self.x, self.y)
        return self.copy(2 + k, mine, mine, device_at(1 - self.x, self.y, self.z, self.c))

    def by_y(self, k):
        mine = self.block(self.full, self.from_z(k), self.x, self.y)
        return self.copy(5 + k, mine, mine, device_at(self.x, 1 - self.y, self.z, self.c))

    def corners(self, k):
        way = self.ways[k - 1]
        parts = (0, 1) if way == "both" else (None, None)
        made = []
        if way != "y":
            got = self.block(self.full, self.from_z(k), 1 - self.x, self.y, parts[0])
            made.append(self.copy(8 + k, got, got, device_at(self.x, 1 - self.y, self.z, self.c)))
        if way != "x":
            got = self.block(self.full, self.from_z(k), self.x, 1 - self.y, parts[1])
            made.append(self.copy(10 if k == 2 else 12, got, got, device_at(1 - self.x, self.y, self.z, self.c)))
        return made

    def by_core(self, k):
        there = device_at(self.x, self.y, self.z, 1 - self.c)
        got = self.block(self.full, self.from_z(k))
        src = self.block(self.shard, None) if k == 0 else got
        return self.copy(13 + k, src, got, there)

    def begin(self):
        for k in (1, 2, 3):
            self.by_z(k).start()
        self.by_core(0).start()

    def plane(self):
        for k in (1, 2, 3):
            self.by_z(k).wait_recv()
            self.by_x(k).start()
            self.by_y(k).start()

    def diagonal(self):
        for k in (1, 2, 3):
            self.by_x(k).wait_recv()
            self.by_y(k).wait_recv()
            for made in self.corners(k):
                made.start()

    def core(self):
        for k in (1, 2, 3):
            for made in self.corners(k):
                made.wait_recv()
            self.by_core(k).start()

    def finish(self):
        for k in range(4):
            self.by_core(k).wait_recv()

    def sent(self):
        for k in (1, 2, 3):
            for made in [self.by_z(k), self.by_x(k), self.by_y(k), self.by_core(k)] + self.corners(k):
                made.wait_send()
        self.by_core(0).wait_send()


class Sum:
    COPIES = 11

    def __init__(self, index, sems, at_, own, b1x, b1y, b2x, b2y, from_z, final):
        self.send, self.recv = sems
        self.x, self.y, self.z, self.c = at_
        self.base = index * self.COPIES
        self.own, self.b1x, self.b1y, self.b2x, self.b2y, self.from_z, self.final = own, b1x, b1y, b2x, b2y, from_z, final
        _, self.rows, self.cols = own.shape

    def rh(self, a):
        return pl.ds(pl.multiple_of(a * (self.rows // 2), 16), self.rows // 2)

    def ch(self, b):
        return pl.ds(pl.multiple_of(b * (self.cols // 2), 128), self.cols // 2)

    def copy(self, i, src, dst, device):
        return pltpu.make_async_remote_copy(
            src_ref=src, dst_ref=dst, send_sem=self.send.at[self.base + i], recv_sem=self.recv.at[self.base + i],
            device_id=device, device_id_type=MESH,
        )

    def to_x(self):
        return device_at(1 - self.x, self.y, self.z, self.c)

    def to_y(self):
        return device_at(self.x, 1 - self.y, self.z, self.c)

    def to_core(self, src, dst):
        return self.copy(0, src, dst, device_at(self.x, self.y, self.z, 1 - self.c))

    def halves(self):
        lo, hi = pl.ds(0, 2), pl.ds(2, 2)
        return (
            self.copy(1, self.own.at[lo, self.rh(1 - self.x), :], self.b1x, self.to_x()),
            self.copy(2, self.own.at[hi, :, self.ch(1 - self.y)], self.b1y, self.to_y()),
        )

    def quarters(self):
        lo, hi = pl.ds(0, 2), pl.ds(2, 2)
        return (
            self.copy(3, self.own.at[lo, self.rh(self.x), self.ch(1 - self.y)], self.b2y, self.to_y()),
            self.copy(4, self.own.at[hi, self.rh(1 - self.x), self.ch(self.y)], self.b2x, self.to_x()),
        )

    def along(self):
        return [
            self.copy(
                4 + k, self.own.at[(self.z + k) % 4, self.rh(self.x), self.ch(self.y)], self.from_z.at[k - 1],
                device_at(self.x, self.y, (self.z + k) % 4, self.c),
            )
            for k in (1, 2, 3)
        ]

    def back(self):
        mine = self.final.at[self.rh(self.x), self.ch(self.y)]
        return [
            self.copy(8, mine, mine, self.to_x()),
            self.copy(9, mine, mine, self.to_y()),
            self.copy(10, mine, mine, device_at(1 - self.x, 1 - self.y, self.z, self.c)),
        ]

    def add(self, zs, row0, rows, cols, other):
        step = self.rows // 2
        blocks = rows // step

        def body(i, _):
            zi = i // blocks
            r = i % blocks * step
            mine = (zs + zi, pl.ds(pl.multiple_of(row0 + r, 16), step), cols)
            theirs = other[zi, pl.ds(pl.multiple_of(r, 16), step), :]
            self.own[mine] = (self.own[mine].astype(single) + theirs.astype(single)).astype(narrow)
            return 0

        lax.fori_loop(0, 2 * blocks, body, 0)

    def first(self, stage, got):
        def body(i, _):
            self.own[i] = (stage[i, self.c].astype(single) + got[i].astype(single)).astype(narrow)
            return 0

        lax.fori_loop(0, 4, body, 0)
        for made in self.halves():
            made.start()

    def second(self):
        for made in self.halves():
            made.wait_recv()
        self.add(0, self.x * (self.rows // 2), self.rows // 2, slice(None), self.b1x)
        self.add(2, 0, self.rows, self.ch(self.y), self.b1y)
        for made in self.quarters():
            made.start()

    def third(self):
        for made in self.quarters():
            made.wait_recv()
        self.add(0, self.x * (self.rows // 2), self.rows // 2, self.ch(self.y), self.b2y)
        self.add(2, self.x * (self.rows // 2), self.rows // 2, self.ch(self.y), self.b2x)
        for made in self.along():
            made.start()

    def fourth(self):
        for made in self.along():
            made.wait_recv()
        total = self.own[self.z, self.rh(self.x), self.ch(self.y)].astype(single)
        for k in range(3):
            total = total + self.from_z[k].astype(single)
        self.final[self.rh(self.x), self.ch(self.y)] = total.astype(narrow)
        for made in self.back():
            made.start()

    def finish(self):
        for made in self.back():
            made.wait_recv()

    def sent(self):
        for made in list(self.halves()) + list(self.quarters()) + self.along() + self.back():
            made.wait_send()


class SumSmall:
    COPIES = 6

    def __init__(self, base, sems, at_, total, got):
        self.send, self.recv = sems
        self.x, self.y, self.z, self.c = at_
        self.base, self.total, self.got = base, total, got

    def copies(self, i):
        x, y, z, c = self.x, self.y, self.z, self.c
        to = [[device_at(x, y, z, 1 - c)], [device_at(1 - x, y, z, c)], [device_at(x, 1 - y, z, c)]]
        to.append([device_at(x, y, (z + k) % 4, c) for k in (1, 2, 3)])
        return [
            pltpu.make_async_remote_copy(
                src_ref=self.total.at[i], dst_ref=self.got.at[i + n], send_sem=self.send.at[self.base + i + n],
                recv_sem=self.recv.at[self.base + i + n], device_id=d, device_id_type=MESH,
            )
            for n, d in enumerate(to[i])
        ]

    def begin(self):
        for made in self.copies(0):
            made.start()

    def step(self, i):
        for made in self.copies(i):
            made.wait_recv()
        self.total[i + 1] = self.total[i] + self.got[i]
        for made in self.copies(i + 1):
            made.start()

    def finish(self, out):
        for made in self.copies(3):
            made.wait_recv()
        terms = []
        for i in range(4):
            term = self.total[3]
            for k in (1, 2, 3):
                term = jnp.where((self.z - k + 4) % 4 == i, self.got[2 + k], term)
            terms.append(term)
        out[...] = ((terms[0] + terms[1]) + terms[2]) + terms[3]
        for i in range(4):
            for made in self.copies(i):
                made.wait_send()


def contrast_kernel(slots, buckets, bucket, pooled, loss_o, grad_o, mine, every, full, send, recv, sem):
    x, y, z, c = place()
    device = (y * 2 + x) * 8 + 2 * z + c
    greet(neighbours(False))
    wires = Wires(send, recv)
    p = pooled[...]
    scale = lax.rsqrt(jnp.sum(p * p, -1, keepdims=True) + 1e-06)
    e = p * scale
    width = e.shape[1]
    hw = width // 2
    mine[...] = jnp.concatenate([e[:, :hw], e[:, hw:]], 0).astype(narrow)

    def slot_of(xx, yy, zz):
        return (yy * 2 + xx) * 8 + 2 * zz + c

    def block(xx, yy, zz):
        return every.at[slot_of(xx, yy, zz)]

    keep = pltpu.make_async_copy(mine, every.at[device], sem)
    keep.start()
    by_x = wires.copy(mine, block(x, y, z), device_at(1 - x, y, z, c))
    by_y = [wires.copy(mine, block(x, y, z), device_at(x, 1 - y, z, c))]
    by_z = [wires.copy(mine, block(x, y, z), device_at(x, y, (z + k) % 4, c)) for k in (1, 2, 3)]
    by_x.wait_recv()
    by_y.append(wires.copy(block(1 - x, y, z), block(1 - x, y, z), device_at(x, 1 - y, z, c)))
    by_z += [wires.copy(block(1 - x, y, z), block(1 - x, y, z), device_at(x, y, (z + k) % 4, c)) for k in (1, 2, 3)]
    for s in by_y:
        s.wait_recv()
    for xx in (x, 1 - x):
        by_z += [
            wires.copy(block(xx, 1 - y, z), block(xx, 1 - y, z), device_at(x, y, (z + k) % 4, c)) for k in (1, 2, 3)
        ]
    pair_size = 8

    def long_of(shape, axis):
        pair = lax.broadcasted_iota(jnp.int32, shape, axis) // pair_size
        found = jnp.zeros(shape, jnp.int32)
        for b in range(buckets):
            found = jnp.where(pair == b, bucket[b], found)
        return found > 0

    def roles(shape, axis):
        t = lax.broadcasted_iota(jnp.int32, shape, axis)
        long = long_of(shape, axis)
        within, odd = t % 4, t // 4 % 2
        query = jnp.where(long, jnp.where((within == 0) & (odd == 0), 1, 0), jnp.where(within % 2 == 0, 1, 0))
        passage = jnp.where(long, jnp.where((within == 0) & (odd == 1), 1, 0), jnp.where(within % 2 == 1, 1, 0))
        return query > 0, passage > 0, jnp.where(long, t + 4, t + 1)

    _, passage, _ = roles((8, slots), 1)
    query, _, partner = roles((slots, 128), 0)
    passage, query, partner = passage[:1], query[:, :1], partner[:, :1]
    pair_count = jnp.zeros((), single)
    for b in range(buckets):
        pair_count = pair_count + (4 - 3 * bucket[b]).astype(single)
    keep.wait()
    for s in by_z:
        s.wait_recv()
    others = []
    for yy in range(2):
        for xx in range(2):
            for zz in range(4):
                others.append(wires.copy(block(xx, yy, zz), block(xx, yy, zz), device_at(x, y, z, 1 - c)))
    for s in others:
        s.wait_recv()
    both = every[...].astype(single)
    left = both[:, :8, :].reshape(slots, hw).astype(narrow)
    right = both[:, 8:, :].reshape(slots, hw).astype(narrow)
    logits = (dot_nt(left, left) + dot_nt(right, right)) * 100.0
    masked = jnp.where(passage, logits, -1000000000.0)
    top = jnp.max(masked, -1, keepdims=True)
    raised = jnp.exp(masked - top)
    total = jnp.sum(raised, -1, keepdims=True)
    match = lax.broadcasted_iota(jnp.int32, (slots, slots), 1) == partner
    positive = jnp.sum(jnp.where(match, logits, 0.0), -1, keepdims=True)
    terms = jnp.where(query, top + jnp.log(total) - positive, 0.0)
    loss = jnp.sum(terms, 0, keepdims=True) / pair_count
    loss_o[...] = jnp.broadcast_to(loss, loss_o.shape)
    weight = jnp.where(query, 1.0, 0.0) / pair_count
    logit_grad = weight * (raised / total - jnp.where(match, 1.0, 0.0))
    by_row = logit_grad.astype(narrow)
    by_column = logit_grad.T.astype(narrow)
    full[:, :hw] = dot(by_row, left) + dot(by_column, left)
    full[:, hw:] = dot(by_row, right) + dot(by_column, right)
    g = full[pl.ds(pl.multiple_of(device * 8, 8), 8), :] * 100.0
    grad_o[...] = scale * g - p * (scale * scale * scale) * jnp.sum(p * g, -1, keepdims=True)
    wires.finish()


def run_contrast(bucket, pooled, devices):
    rows, width = pooled.shape
    slots = rows * devices
    dma = pltpu.SemaphoreType.DMA
    spec_v = pl.BlockSpec(memory_space=VM)
    copies = 1 + 2 + 12 + 16
    loss, grad = pl.pallas_call(
        functools.partial(contrast_kernel, slots, bucket.shape[0]),
        out_shape=[jax.ShapeDtypeStruct((8, 128), single), jax.ShapeDtypeStruct(pooled.shape, single)],
        in_specs=[pl.BlockSpec(memory_space=SM), spec_v],
        out_specs=[spec_v, spec_v],
        scratch_shapes=[
            VM((2 * rows, width // 2), narrow), VM((devices, 2 * rows, width // 2), narrow), VM((slots, width), single),
            dma((copies,)), dma((copies,)), dma(()),
        ],
        compiler_params=pltpu.CompilerParams(collective_id=3, has_side_effects=True),
        name="contrast",
    )(bucket, pooled)
    return loss[0, 0], grad


def gather_weights(tab, w_in, w_out, w_up, w_down, small):
    gat = lambda a: lax.all_gather(a, "fsdp", axis=0, tiled=True)
    return lax.all_gather(tab, "fsdp", axis=1, tiled=True), gat(w_in), gat(w_out), gat(w_up), gat(w_down), gat(small)


def reduce_all(grads, small):
    done = []
    for a in grads:
        part = lax.psum_scatter(a.astype(single), "fsdp", scatter_dimension=0, tiled=True)
        done.append(lax.psum(part.astype(narrow), "dp").astype(single))
    return done, lax.psum(small, ("dp", "fsdp"))


def local(
    tokens, lengths, bucket, position_table, in_projection, query_bias, value_bias, out_projection, out_bias,
    first_gain, first_shift, up_projection, up_bias, down_projection, down_bias, second_gain, second_shift,
):
    groups = lengths.shape[0]
    width = tokens.shape[1]
    count = tokens.shape[0] // groups
    shards = lax.axis_size("fsdp")
    ff = up_projection.shape[1]
    fs = lax.axis_index("fsdp")
    device = lax.axis_index("dp") * shards + fs
    small_parts = (query_bias, value_bias, out_bias, first_gain, first_shift, down_bias, second_gain, second_shift)
    piece = query_bias.shape[0]
    wide_piece = up_bias.shape[0]
    flag = lax.dynamic_slice_in_dim(jnp.repeat(bucket, 2), device * groups, groups)
    chunk = 1024
    chunks, per = ff // chunk, chunk // 8
    grid = lax.axis_size("dp") == 4 and shards == 8
    if grid:
        line = jnp.concatenate([v[None] for v in small_parts] + [jnp.zeros((8, piece), narrow)], 0)
        spread = lax.dynamic_update_slice(jnp.zeros((16, chunk), narrow), line, (0, fs * piece))
        ups = up_bias.reshape(chunks, per)
        small = lax.dynamic_update_slice(spread, ups, (8, fs * per))
        table = position_table.T
        weights = (in_projection, out_projection, up_projection, down_projection)
    else:
        vectors = jnp.concatenate(small_parts + (up_bias,))[None, :]
        table, w_in, w_out, w_up, w_down, small_all = gather_weights(
            position_table, in_projection, out_projection, up_projection, down_projection, vectors
        )
        table = table.T
        heads = small_all[:, : 8 * piece].reshape(shards, 8, piece).transpose(1, 0, 2).reshape(8, width)
        ups = small_all[:, 8 * piece :].reshape(8, chunks, per).transpose(1, 0, 2).reshape(chunks, chunk)
        small = jnp.concatenate(
            [jnp.pad(heads, ((0, 0), (0, chunk - width))), ups, jnp.zeros((8 - chunks, chunk), narrow)]
        )
        w_up = w_up.reshape(width, 8, chunks, per).transpose(0, 2, 1, 3).reshape(width, ff)
        w_down = w_down.reshape(8, chunks, per, width).transpose(1, 0, 2, 3)
        weights = (w_in, w_out, w_up, w_down)
    outs = run_forward(grid, groups, count, width, ff, chunk, lengths, flag, small, tokens, table, weights)
    saved, pooled, vecs = outs[:11], outs[11], outs[12]
    if grid:
        weights = tuple(outs[14:18])
    slots = groups * 4
    if grid:
        loss, pooled_grad = run_contrast(bucket, pooled, 4 * shards)
    else:
        embedded, norm_grad = jax.vjp(normalize_rows, pooled)
        every = lax.all_gather(embedded.astype(narrow), ("dp", "fsdp"), axis=0, tiled=True)
        loss, embed_grad = contrast(every, embedded, device * slots, slots, bucket)
        pooled_grad = norm_grad(embed_grad)[0]
    tokens_grad, blocks, gvec = run_backward(
        grid, groups, count, width, ff, chunk, lengths, flag, vecs, pooled_grad, weights, saved
    )
    shapes = item_shapes(count, width, ff, chunk)
    if grid:
        gdown, gup, gout, gin, gtab = run_finish(shapes, chunks, blocks)
    else:
        blocks = [b.reshape(8 * r, k) for b, (r, k) in zip(blocks, shapes)]
        gdown = jnp.stack([b.reshape(8, per, width) for b in blocks[0 : 2 * chunks : 2]], 1).reshape(ff, width)
        gup = jnp.stack([b.reshape(width, 8, per) for b in blocks[1 : 2 * chunks : 2]], 2).reshape(width, ff)
        gin = jnp.concatenate(blocks[2 * chunks + 1 : 2 * chunks + 4], 1)
        (gin, gout, gup, gdown, gtab), gvec = reduce_all((gin, blocks[2 * chunks], gup, gdown, blocks[-1]), gvec)
        gtab = gtab.T
    own = [lax.dynamic_slice_in_dim(gvec[i], fs * piece, piece) for i in range(8)]
    ups = gvec[8 : 8 + chunks].reshape(chunks, 8, per).transpose(1, 0, 2).reshape(ff)
    up_own = lax.dynamic_slice_in_dim(ups, fs * wide_piece, wide_piece)
    return (
        loss, pooled, tokens_grad, gtab, gin, own[0], own[1], gout, own[2], own[3], own[4], gup, up_own, gdown,
        own[5], own[6], own[7],
    )


def solution(mesh):
    rows = P(("dp", "fsdp"), None)
    vec = P("fsdp")
    mat = P("fsdp", None)
    in_specs = (rows, rows, P(), P(None, "fsdp"), mat, vec, vec, mat, vec, vec, vec, mat, vec, mat, vec, vec, vec)
    out_specs = (P(), rows, rows, P(None, "fsdp"), mat, vec, vec, mat, vec, vec, vec, mat, vec, mat, vec, vec, vec)
    return jax.shard_map(local, mesh=mesh, in_specs=in_specs, out_specs=out_specs, check_vma=False)
```

```python
import functools

import jax
import jax.numpy as jnp
from jax import lax
from jax.experimental import pallas as pl
from jax.experimental.pallas import tpu as pltpu
from jax.sharding import PartitionSpec as P

H = 12
narrow = jnp.bfloat16
single = jnp.float32
ANY = pl.ANY
VM = pltpu.VMEM
SM = pltpu.SMEM
LIMIT = 60 * 2**20


def dot(a, b):
    return lax.dot_general(a, b, (((1,), (0,)), ((), ())), preferred_element_type=single)


def dot_nt(a, b):
    return lax.dot_general(a, b, (((1,), (1,)), ((), ())), preferred_element_type=single)


def at(start, size):
    return pl.ds(pl.multiple_of(start, 128), size)


def gelu_pair(u):
    t = 1.0 / (1.0 + 0.23164189 * jnp.abs(u))
    e = jnp.exp(-0.5 * (u * u))
    tail = t * (
        0.127414796 + t * (-0.142248368 + t * (0.7107068705 + t * (-0.7265760135 + t * 0.5307027145)))
    )
    tail = tail * e
    phi = jnp.where(u < 0, tail, 1.0 - tail)
    return u * phi, phi + u * (e * 0.3989422804)


def norm_rows(value):
    mean = jnp.mean(value, -1, keepdims=True)
    centred = value - mean
    rstd = lax.rsqrt(jnp.mean(centred * centred, -1, keepdims=True) + 1e-06)
    return centred * rstd, rstd


def norm_back(grad, unit, rstd):
    one = jnp.mean(grad, -1, keepdims=True)
    two = jnp.mean(grad * unit, -1, keepdims=True)
    return rstd * (grad - one - unit * two)


def slot_lengths(lens, flag, g, along_rows, count, width):
    slot = count // 4
    shape = (count, width) if along_rows else (8, count)
    t = lax.broadcasted_iota(jnp.int32, shape, 0 if along_rows else 1)
    which = t // slot
    long = flag[g] > 0
    limit = jnp.where(which == 0, lens[g, 0], lens[g, 1])
    limit = jnp.where(which == 2, lens[g, 2], limit)
    limit = jnp.where(which == 3, lens[g, 3], limit)
    limit = jnp.where(long, lens[g, 0], limit)
    inside = jnp.where(long, t, t % slot)
    return which, inside < limit


SUM_EVENTS = ((0, 0), (0, 2), (1, 0), (0, 1), (0, 4), (0, 5), (1, 2), (0, 6), (0, 3), (1, 1), (1, 4), (2, 0), (0, 7), (2, 2), (1, 5), (1, 6), (1, 3), (2, 1), (2, 4), (3, 0), (1, 7), (3, 2), (2, 3), (3, 1), (3, 4), (0, 8), (0, 9), (2, 5), (3, 3), (0, 10), (2, 6), (1, 8), (1, 9), (2, 7), (3, 5), (1, 10), (3, 6), (2, 8), (3, 7), (2, 9), (2, 10), (3, 8), (3, 9), (3, 10))
SUMS_FEED = ((0, 0, 0, 0), (0, 0, 0, 0), (0, 0, 1, 1))
SUMS_UP = ((0, 0, 0, 0), (0, 0, 0, 0), (1, 1, 1, 1))
SUMS_NORM, SUMS_CTX, SUMS_XT, SUMS_BIAS = 2, 3, 3, 22
SUMS_ATTEND = ((4, 4, 5, 5), (7, 7, 10, 11), (13, 15, 19, 21))
SUMS_IN = (5, 12, 21)
SUMS_TOKEN = (23, 23, 23, 24)


def item_shapes(count, width, ff, chunk):
    found = []
    for _ in range(ff // chunk):
        found += [(chunk // 8, width), (width // 8, chunk)]
    return found + [(width // 8, width)] * 4 + [(width // 8, count)]


def backward_kernel(
    sizes, remote,
    lens, flag, vecs, pg, w_in, w_out, w_up, w_down, x_i, mixed_i, prob_i, ctx_i, hid_i, n1_i, r1_i, act_i, gp_i, n2_i, r2_i,
    *refs,
):
    groups, count, width, ff, chunk = sizes
    rows = groups * count
    pairs = width // 128
    slot = count // 4
    wide = ff // chunk
    blocks = rows // 256
    per = chunk // 8
    shapes = item_shapes(count, width, ff, chunk)
    items = len(shapes)
    tok_o, item_o, gvec_o, refs = refs[0], refs[1 : 1 + items], refs[1 + items], refs[2 + items :]
    (
        v_in, v_out, v_up, v_down, mixed, ctx, unit_v, rstd_v, ast, gst, low, hid_t, up_low, grad, dctx, stage_a, stage_b,
        gsmall, in_sem, p_sem, o_sem, i_sem,
    ) = refs[:22]
    wires = refs[22:]
    load = [
        pltpu.make_async_copy(s, d, in_sem.at[i])
        for i, (s, d) in enumerate(
            (
                (n2_i, unit_v), (r2_i, rstd_v), (hid_i, dctx), (n1_i, unit_v), (r1_i, rstd_v), (ctx_i, ctx),
                (w_out, v_out), (mixed_i, mixed), (x_i.reshape(8, per, width), v_down), (w_in, v_in),
            )
        )
    ]
    l_n2, l_r2, l_hid, l_n1, l_r1, l_ctx, l_wout, l_mixed, l_x, l_win = load

    def chunk_loads(j):
        down = w_down.at[j] if len(w_down.shape) == 4 else w_down.at[:, pl.ds(j * per, per), :]
        return (
            pltpu.make_async_copy(down, v_down, in_sem.at[10]),
            pltpu.make_async_copy(gp_i.at[j], gst, in_sem.at[11]),
            pltpu.make_async_copy(w_up.at[:, pl.ds(j * chunk, chunk)], v_up, in_sem.at[12]),
        )

    def act_load(j):
        return pltpu.make_async_copy(act_i.at[j], ast, in_sem.at[13])

    def prob_loads(i, s_):
        return [
            pltpu.make_async_copy(
                prob_i.at[i, h],
                up_low.at[pl.ds(pl.multiple_of(s_ * count, count), count), pl.ds(h * count, count)],
                p_sem.at[2 * s_ + h],
            )
            for h in range(2)
        ]

    l_n2.start()
    l_r2.start()
    l_hid.start()
    for made in chunk_loads(0):
        made.start()
    act_load(0).start()
    for made in (l_ctx, l_wout, l_mixed, l_win):
        made.start()

    def vec(i):
        return vecs[i : i + 1, :width]

    def staged(t, lead=None):
        r, k = shapes[t]
        ref = stage_a if t % 2 == 0 else stage_b
        if lead is None:
            return ref.at[:, :, pl.ds(0, r), pl.ds(0, k)]
        return ref.at[:, lead, pl.ds(0, r), pl.ds(0, k)]

    steps = []
    done = [0]
    firsts = [0]
    if remote:
        send, recv, free, total_v, got_v, ring = wires[:6]
        held = wires[6:]
        here = place()
        x, y, z, c = here
        sums = []
        for t in range(items):
            n_held = 5 if t in DEEP else 7
            sums.append((SumDeep if t in DEEP else Sum)(t, (send, recv), here, *held[:n_held]))
            held = held[n_held:]
        tiny = SumSmall(Sum.COPIES * items, (send, recv), here, total_v, got_v)

        def slot_of(t):
            r, k = shapes[t]
            return ring.at[t % 3, :, pl.ds(0, r), pl.ds(0, k)]

        def crossing(t):
            return sums[t].to_core(staged(t, 1 - c), slot_of(t))

        def item_store(t):
            return pltpu.make_async_copy(sums[t].final, item_o[t], i_sem.at[t])

        def first_of(n):
            crossing(n).wait_recv()
            sums[n].first(staged(n), slot_of(n))
            if n + 3 < items:
                pl.semaphore_signal(free, inc=1, device_id=device_at(x, y, z, 1 - c), device_id_type=MESH)

        def first(t):
            while firsts[0] <= t:
                first_of(firsts[0])
                firsts[0] += 1

        def first_in(i, which):
            for count_, t in which.items():
                pl.when(i == count_)(functools.partial(first_of, t))

        def ready(t):
            if t >= 2:
                first(t - 2)
                crossing(t - 2).wait_send()

        def produced(t):
            if t >= 3:
                pl.semaphore_wait(free, 1)
            crossing(t).start()

        def step(stage, t):
            getattr(sums[t], ("second", "third", "fourth", "finish")[stage])()
            if stage == 3:
                item_store(t).start()

        steps = [functools.partial(step, *event) for event in SUM_EVENTS]
    else:

        def item_store(t):
            return pltpu.make_async_copy(staged(t), item_o[t], i_sem.at[t])

        def first(t):
            pass

        def first_in(i, which):
            pass

        def ready(t):
            if t >= 2:
                item_store(t - 2).wait()

        def produced(t):
            item_store(t).start()

    def pump(upto):
        while done[0] < min(upto, len(steps)):
            steps[done[0]]()
            done[0] += 1

    def pump_in(i, marks):
        at_step = done[0]
        for count_, mark in enumerate(marks):
            mark = max(min(mark, len(steps)), at_step)
            if mark > at_step:

                @pl.when(i == count_)
                def _(a=at_step, b=mark):
                    for n in range(a, b):
                        steps[n]()

            at_step = mark

    def pumped(marks):
        done[0] = max([done[0]] + [min(m, len(steps)) for m in marks])

    def put(t, b, out):
        r, k = shapes[t]
        ref = stage_a if t % 2 == 0 else stage_b
        out = out.astype(narrow)
        ref[b, 0, :r, :k] = out[:r]
        ref[b, 1, :r, :k] = out[r:]

    def second_norm():
        l_n2.wait()
        l_r2.wait()
        gain_sum = jnp.zeros((1, width), single)
        shift_sum = jnp.zeros((1, width), single)
        bias_sum = jnp.zeros((1, width), single)
        for g in range(groups):
            _, live = slot_lengths(lens, flag, g, True, count, 128)
            long = flag[g] > 0
            for s in range(4):
                r = pl.ds(g * count + s * slot, slot)
                mine = pg[4 * g + s : 4 * g + s + 1, :] / jnp.maximum(lens[g, s], 1).astype(single)
                whole = pg[4 * g : 4 * g + 1, :] / jnp.maximum(lens[g, 0], 1).astype(single)
                row = jnp.where(long, whole, mine)
                keep = live[s * slot : (s + 1) * slot, :1]
                d = jnp.where(keep, row, 0.0)
                unit = unit_v[r, :]
                gain_sum = gain_sum + jnp.sum(d * unit, 0, keepdims=True)
                shift_sum = shift_sum + jnp.sum(d, 0, keepdims=True)
                back = norm_back(d * vec(6), unit, rstd_v[r, :1])
                grad[r, :] = back
                lowered = back.astype(narrow)
                low[r, :] = lowered
                bias_sum = bias_sum + jnp.sum(lowered.astype(single), 0, keepdims=True)
        gsmall[...] = jnp.zeros_like(gsmall)
        gsmall[6:7, :width] = gain_sum
        gsmall[7:8, :width] = shift_sum
        gsmall[5:6, :width] = bias_sum
        l_n1.start()
        l_r1.start()
        l_hid.wait()
        for b in range(rows // slot):
            r = pl.ds(b * slot, slot)
            hid_t[:, r] = dctx[r, :].T

    if remote:
        greet(neighbours(False) + [device_at(1 - x, 1 - y, z, c)], second_norm)
    else:
        second_norm()

    for j in range(wide):
        for made in chunk_loads(j):
            made.wait()

        def feed(b, total, j=j):
            r = at(b * 256, 256)
            up = (dot_nt(low[r, :], v_down[...].reshape(chunk, width)) * gst[r, :].astype(single)).astype(narrow)
            up_low[r, :] = up
            grad[r, :] += dot_nt(up, v_up[...])
            if j >= 1:
                first_in(b, {0: 2 * j - 2, 2: 2 * j - 1})
            pump_in(b, SUMS_FEED[j])
            return total + jnp.sum(up.astype(single), 0, keepdims=True)

        gsmall[8 + j : 9 + j, :] = lax.fori_loop(0, blocks, feed, jnp.zeros((1, chunk), single))
        firsts[0] = max(firsts[0], 2 * j)
        pumped(SUMS_FEED[j])
        if j + 1 < wide:
            for made in chunk_loads(j + 1):
                made.start()
        act_load(j).wait()
        ready(2 * j)

        def weigh(b, _, j=j):
            put(2 * j, b, dot(ast[:, at(b * 256, 256)].T, low[...]))
            return 0

        lax.fori_loop(0, 4, weigh, 0)
        produced(2 * j)
        if j + 1 < wide:
            act_load(j + 1).start()
        ready(2 * j + 1)

        def weigh_up(b, _, j=j):
            put(2 * j + 1, b, dot(hid_t[pl.ds(pl.multiple_of(b * (width // 4), 64), width // 4), :], up_low[...]))
            pump_in(b, SUMS_UP[j])
            return 0

        lax.fori_loop(0, 4, weigh_up, 0)
        pumped(SUMS_UP[j])
        produced(2 * j + 1)

    for made in prob_loads(0, 0) + prob_loads(1, 1):
        made.start()

    l_x.start()

    l_n1.wait()
    l_r1.wait()
    l_ctx.wait()
    l_wout.wait()
    gain_sum = jnp.zeros((1, width), single)
    shift_sum = jnp.zeros((1, width), single)
    bias_sum = jnp.zeros((1, width), single)
    for b in range(rows // slot):
        r = pl.ds(b * slot, slot)
        d = grad[r, :]
        unit = unit_v[r, :]
        gain_sum = gain_sum + jnp.sum(d * unit, 0, keepdims=True)
        shift_sum = shift_sum + jnp.sum(d, 0, keepdims=True)
        back = norm_back(d * vec(3), unit, rstd_v[r, :1])
        grad[r, :] = back
        lowered = back.astype(narrow)
        low[r, :] = lowered
        bias_sum = bias_sum + jnp.sum(lowered.astype(single), 0, keepdims=True)
        hid_t[:, r] = ctx[r, :].T
    gsmall[3:4, :width] = gain_sum
    gsmall[4:5, :width] = shift_sum
    gsmall[2:3, :width] = bias_sum
    first(2 * wide - 1)
    pump(SUMS_NORM)

    def weigh_by_columns(t, other):
        def body(b, _):
            put(t, b, dot(hid_t[pl.ds(pl.multiple_of(b * (width // 4), 64), width // 4), :], other()))
            return 0

        lax.fori_loop(0, 4, body, 0)

    t_out = 2 * wide
    ready(t_out)
    weigh_by_columns(t_out, lambda: low[...])
    produced(t_out)

    def context_back(b, _):
        r = at(b * 256, 256)
        dctx[r, :] = dot_nt(low[r, :], v_out[...]).astype(narrow)
        return 0

    lax.fori_loop(0, blocks, context_back, 0)
    first(t_out)
    pump(SUMS_CTX)
    l_x.wait()
    for b in range(8):
        hid_t[:, pl.ds(b * per, per)] = v_down[b].T
    pump(SUMS_XT)

    l_mixed.wait()
    lane = lax.broadcasted_iota(jnp.int32, (count, 128), 1)
    half = (lane < 64, lane >= 64)
    scale = jnp.asarray(0.125, narrow)
    third = width // 3
    per_part = pairs // 3
    n = groups * per_part

    def prob_index(j, part):
        return j // per_part * pairs + part * per_part + j % per_part

    def attend(j, _, part):
        g = j // per_part
        s_ = j % 2
        r = at(g * count, count)
        for made in prob_loads(prob_index(j, part), s_):
            made.wait()
        base = part * width + j % per_part * 128
        c_q = at(base, 128)
        c_k = at(base + third, 128)
        c_v = at(base + 2 * third, 128)
        c_c = at(part * third + j % per_part * 128, 128)
        q = mixed[r, c_q] * scale
        k = mixed[r, c_k]
        v = mixed[r, c_v]
        dc = dctx[r, c_c]
        c = ctx[r, c_c]
        q_t = q.T
        dc_t = dc.T
        zero = jnp.zeros_like(q)
        prod = dc.astype(single) * c.astype(single)
        dq = [None] * (count // 512)
        dk_t = []
        dv_t = []
        for h in range(2):
            dch = jnp.where(half[h], dc, zero)
            kh = jnp.where(half[h], k, zero)
            d = jnp.sum(jnp.where(half[h], prod, 0.0), -1, keepdims=True)
            dkh = None
            dvh = None
            for b in range(count // 512):
                rb = slice(b * 512, (b + 1) * 512)
                prob = up_low[pl.ds(pl.multiple_of(s_ * count + b * 512, 512), 512), h * count : (h + 1) * count]
                dp = dot_nt(dch[rb], v)
                ds = (prob.astype(single) * (dp - d[rb])).astype(narrow)
                o = dot(ds, kh)
                dq[b] = o if dq[b] is None else dq[b] + o
                hr = slice(h * 64, (h + 1) * 64)
                one = dot(q_t[hr, rb], ds)
                two = dot(dc_t[hr, rb], prob)
                dkh = one if dkh is None else dkh + one
                dvh = two if dvh is None else dvh + two
            dk_t.append(dkh)
            dv_t.append(dvh)
        for b in range(count // 512):
            mixed[at(g * count + b * 512, 512), c_q] = (dq[b] * 0.125).astype(narrow)
        mixed[r, c_k] = jnp.concatenate(dk_t, 0).T.astype(narrow)
        mixed[r, c_v] = jnp.concatenate(dv_t, 0).T.astype(narrow)

        @pl.when(part * n + j + 2 < 3 * n)
        def _():
            for made in prob_loads(prob_index((j + 2) % n, part + (j + 2) // n), s_):
                made.start()

        if part >= 1:
            first_in(j, {0: t_out + part})
        pump_in(j, SUMS_ATTEND[part])
        return 0

    l_win.wait()
    for part in range(3):
        lax.fori_loop(0, n, functools.partial(attend, part=part), 0)
        if part >= 1:
            firsts[0] = max(firsts[0], t_out + part + 1)
        pumped(SUMS_ATTEND[part])
        cols = pl.ds(part * width, width)
        ready(t_out + 1 + part)

        def in_weigh(b, _, cols=cols, part=part):
            put(t_out + 1 + part, b, dot(hid_t[pl.ds(pl.multiple_of(b * (width // 4), 64), width // 4), :], mixed[:, cols]))
            return 0

        lax.fori_loop(0, 4, in_weigh, 0)
        produced(t_out + 1 + part)
        pump(SUMS_IN[part])

    for p in range(3):

        def bias(b, total, p=p):
            r = at(b * 256, 256)
            q_cols = slice(p * width, p * width + third)
            v_cols = slice(p * width + 2 * third, (p + 1) * width)
            return (
                total[0] + jnp.sum(mixed[r, q_cols].astype(single), 0, keepdims=True),
                total[1] + jnp.sum(mixed[r, v_cols].astype(single), 0, keepdims=True),
            )

        zero_row = jnp.zeros((1, third), single)
        q_sum, v_sum = lax.fori_loop(0, blocks, bias, (zero_row, zero_row))
        gsmall[0:1, p * third : (p + 1) * third] = q_sum
        gsmall[1:2, p * third : (p + 1) * third] = v_sum
    first(t_out + 3)
    pump(SUMS_BIAS)
    if remote:
        total_v[0] = gsmall[...]
        tiny.begin()

    def token_back(b, _):
        r = at(b * 256, 256)
        grad[r, :] += dot_nt(mixed[r, :], v_in[...])
        pump_in(b, SUMS_TOKEN)
        return 0

    lax.fori_loop(0, blocks, token_back, 0)
    pumped(SUMS_TOKEN)
    tok_store = pltpu.make_async_copy(grad, tok_o, o_sem.at[0])
    tok_store.start()
    last = items - 1
    ready(last)
    ref = stage_a if last % 2 == 0 else stage_b
    for s in range(4):
        total = None
        for g in range(groups):
            long = flag[g] > 0
            r = pl.ds(g * count + s * slot, slot)
            if s == 0:
                other = grad[r, :]
                for o in range(1, 4):
                    other = other + grad[pl.ds(g * count + o * slot, slot), :]
                piece = jnp.where(long, grad[r, :], other)
            else:
                piece = jnp.where(long, grad[r, :], 0.0)
            total = piece if total is None else total + piece
        turned = total.T.astype(narrow)
        for fs in range(8):
            ref[fs // 2, fs % 2, : width // 8, s * slot : (s + 1) * slot] = turned[
                fs * (width // 8) : (fs + 1) * (width // 8), :
            ]
    produced(last)
    if remote:
        first(last)
        for i in range(3):
            pump(done[0] + 2)
            tiny.step(i)
        pump(len(steps))
        tiny.finish(gvec_o)
        for t in range(items):
            item_store(t).wait()
            sums[t].sent()
        for t in (items - 2, items - 1):
            crossing(t).wait_send()
    else:
        gvec_o[...] = gsmall[...]
        for t in (items - 2, items - 1):
            item_store(t).wait()
    tok_store.wait()


def finish_kernel(shapes, wide, tok, *refs):
    given, (tok_o, down, up, out, qkv, tab, buf, load_sem, store_sem) = refs[: len(shapes)], refs[len(shapes) :]
    parts = 4
    n = tok.shape[0] // parts
    moves = [
        (
            pltpu.make_async_copy(tok.at[pl.ds(i * n, n), :], buf.at[i], load_sem.at[i]),
            pltpu.make_async_copy(buf.at[i], tok_o.at[pl.ds(i * n, n), :], store_sem.at[i]),
        )
        for i in range(parts)
    ]
    for load, _ in moves:
        load.start()
    for t in range(wide):
        r, k = shapes[2 * t]
        down[t * r : (t + 1) * r, :] = given[2 * t][...].astype(single)
        _, k = shapes[2 * t + 1]
        part = k // 8
        for fs in range(8):
            up[:, fs * wide * part + t * part : fs * wide * part + (t + 1) * part] = given[2 * t + 1][
                :, fs * part : (fs + 1) * part
            ].astype(single)
    out[...] = given[2 * wide][...].astype(single)
    n = shapes[2 * wide + 1][1]
    third = n // 3
    for p in range(3):
        for i in range(3):
            qkv[:, i * n + p * third : i * n + (p + 1) * third] = given[2 * wide + 1 + p][
                :, i * third : (i + 1) * third
            ].astype(single)
    tab[...] = given[2 * wide + 4][...].astype(single).T
    for load, keep in moves:
        load.wait()
        keep.start()
    for _, keep in moves:
        keep.wait()


def run_finish(shapes, wide, tok, given):
    (r_down, width), (r, chunk) = shapes[0], shapes[1]
    count = shapes[-1][1]
    sds = jax.ShapeDtypeStruct
    return pl.pallas_call(
        functools.partial(finish_kernel, shapes, wide),
        in_specs=[pl.BlockSpec(memory_space=ANY)] + [pl.BlockSpec(memory_space=VM)] * len(given),
        out_specs=[pl.BlockSpec(memory_space=ANY)] + [pl.BlockSpec(memory_space=VM)] * 5,
        out_shape=[
            sds(tok.shape, single),
            sds((r_down * wide, width), single), sds((r, chunk * wide), single), sds((r, width), single),
            sds((r, 3 * width), single), sds((count, r), single),
        ],
        scratch_shapes=[
            VM((4, tok.shape[0] // 4, width), single), pltpu.SemaphoreType.DMA((4,)), pltpu.SemaphoreType.DMA((4,)),
        ],
        compiler_params=pltpu.CompilerParams(vmem_limit_bytes=LIMIT),
        name="finish",
    )(tok, *given)


def shapes_of(groups, count, width, ff, chunk):
    rows = groups * count
    pairs = width // 128
    chunks = ff // chunk
    return dict(
        x=((rows, width), narrow),
        mixed=((rows, 3 * width), narrow),
        prob=((groups * pairs, 2, count, count), narrow),
        ctx=((rows, width), narrow),
        hid=((rows, width), narrow),
        n1=((rows, width), single),
        r1=((rows, 128), single),
        act=((chunks, rows, chunk), narrow),
        gp=((chunks, rows, chunk), narrow),
        n2=((rows, width), single),
        r2=((rows, 128), single),
    )


def run_forward(remote, groups, count, width, ff, chunk, lens, flag, small, tok, tab, weights):
    rows = groups * count
    chunks = ff // chunk
    saved = shapes_of(groups, count, width, ff, chunk)
    outs = [jax.ShapeDtypeStruct(*v) for v in saved.values()]
    outs.append(jax.ShapeDtypeStruct((groups * 4, width), single))
    outs.append(jax.ShapeDtypeStruct((16, chunk), single))
    spec_any = pl.BlockSpec(memory_space=ANY)
    spec_v = pl.BlockSpec(memory_space=VM)
    spec_s = pl.BlockSpec(memory_space=SM)
    dma = pltpu.SemaphoreType.DMA
    n_items = 5 + 2 * chunks
    extra = []
    if remote:
        whole = [
            jax.ShapeDtypeStruct((width, count), narrow),
            jax.ShapeDtypeStruct((width, 3 * width), narrow),
            jax.ShapeDtypeStruct((width, width), narrow),
            jax.ShapeDtypeStruct((width, ff), narrow),
            jax.ShapeDtypeStruct((8, ff // 8, width), narrow),
        ]
        outs += whole
        copies = Piece.COPIES * n_items + 8
        extra = [dma((copies,)), dma((copies,)), dma((6,))]
        body = functools.partial(forward_kernel, (groups, count, width, ff, chunk), True)
    else:

        def body(*refs):
            head = 9
            given = refs[4:head]
            rest = refs[head:]
            return forward_kernel((groups, count, width, ff, chunk), False, *refs[:head], *rest[:13], *given, *rest[13:])

    per = chunk // 8
    return pl.pallas_call(
        body,
        out_shape=outs,
        in_specs=[spec_s, spec_s, spec_any] + [spec_any] * 6,
        out_specs=[spec_any] * 11 + [spec_v, spec_v] + [spec_any] * (5 if remote else 0),
        scratch_shapes=[
            VM((width, 3 * width), narrow),
            VM((width, width), narrow),
            VM((width, ff), narrow),
            VM((chunks, 8, per, width), narrow),
            VM((width, count), narrow),
            VM((rows, width), narrow),
            VM((rows, 3 * width), narrow),
            VM((groups, count, count), single),
            VM((2, 2, count, count), narrow),
            VM((rows, width), narrow),
            VM((rows, width), single),
            VM((rows, width), narrow),
            VM((rows, width), single),
            VM((rows, 128), single),
            VM((rows, 128), single),
            VM((2, rows, chunk), narrow),
            VM((2, rows, chunk), narrow),
            VM((rows, width), single),
            VM((8, 16, chunk) if remote else (16, chunk), narrow),
            VM((width // 8, ff) if remote else (16, 128), narrow),
            VM((width // 8, ff) if remote else (16, 128), narrow),
            VM((width // 8, count) if remote else (16, 128), narrow),
            VM((width // 8, 3 * width) if remote else (16, 128), narrow),
            VM((width // 8, 3 * width) if remote else (16, 128), narrow),
            VM((width // 8, width) if remote else (16, 128), narrow),
            VM((ff // 8, width) if remote else (16, 128), narrow),
            dma((6,)), dma((10,)), dma((2,)), dma((4,)), dma((n_items,)),
        ]
        + extra,
        compiler_params=pltpu.CompilerParams(
            vmem_limit_bytes=LIMIT, **(dict(collective_id=1, has_side_effects=True) if remote else {})
        ),
        cost_estimate=pl.CostEstimate(flops=2 * rows * width * (4 * width + 2 * ff), bytes_accessed=80 * 2**20, transcendentals=10**7),
        name="encoder_forward",
    )(lens, flag, small, tok, tab, *weights)


def run_backward(remote, groups, count, width, ff, chunk, lens, flag, vecs, pooled_grad, weights, saved):
    rows = groups * count
    chunks, per = ff // chunk, chunk // 8
    shapes = item_shapes(count, width, ff, chunk)
    items = len(shapes)
    spec_any = pl.BlockSpec(memory_space=ANY)
    spec_v = pl.BlockSpec(memory_space=VM)
    spec_s = pl.BlockSpec(memory_space=SM)
    dma = pltpu.SemaphoreType.DMA
    tall = max(r for r, _ in shapes)
    broad = max(k for _, k in shapes)
    extra = []
    if remote:
        copies = Sum.COPIES * items + SumSmall.COPIES
        extra = [
            dma((copies,)), dma((copies,)), pltpu.SemaphoreType.REGULAR, VM((4, 16, chunk), single), VM((6, 16, chunk), single),
            VM((3, 4, tall, broad), narrow),
        ]
        for t, (r, k) in enumerate(shapes):
            if t in DEEP:
                half = (r // 2, k) if t % 4 == 1 else (r, k // 2)
                extra += [
                    VM((4, r, k), narrow), VM(half, narrow), VM((r // 2, k // 2), narrow), VM((3, r, k), narrow),
                    VM((r, k), narrow),
                ]
                continue
            extra += [
                VM((4, r, k), narrow), VM((2, r // 2, k), narrow), VM((2, r, k // 2), narrow), VM((2, r // 2, k // 2), narrow),
                VM((2, r // 2, k // 2), narrow), VM((3, r // 2, k // 2), narrow), VM((r, k), narrow),
            ]
    outs = [jax.ShapeDtypeStruct((rows, width), single)]
    outs += [jax.ShapeDtypeStruct((r, k) if remote else (4, 2, r, k), narrow) for r, k in shapes]
    outs += [jax.ShapeDtypeStruct((16, chunk), single)]
    tok, *blocks, gvec = pl.pallas_call(
        functools.partial(backward_kernel, (groups, count, width, ff, chunk), remote),
        out_shape=outs,
        in_specs=[spec_s, spec_s, spec_v, spec_v] + [spec_any] * 15,
        out_specs=[spec_any] * (1 + items) + [spec_v],
        scratch_shapes=[
            VM((width, 3 * width), narrow),
            VM((width, width), narrow),
            VM((width, chunk), narrow),
            VM((8, per, width), narrow),
            VM((rows, 3 * width), narrow),
            VM((rows, width), narrow),
            VM((rows, width), single),
            VM((rows, 128), single),
            VM((rows, chunk), narrow),
            VM((rows, chunk), narrow),
            VM((rows, width), narrow),
            VM((width, rows), narrow),
            VM((rows, chunk), narrow),
            VM((rows, width), single),
            VM((rows, width), narrow),
            VM((4, 2, tall, max(k for _, k in shapes[::2])), narrow),
            VM((4, 2, max(r for r, _ in shapes[1::2]), broad), narrow),
            VM((16, chunk), single),
            dma((14,)), dma((4,)), dma((1,)), dma((items,)),
        ]
        + extra,
        compiler_params=pltpu.CompilerParams(
            vmem_limit_bytes=62 * 2**20, **(dict(collective_id=2, has_side_effects=True) if remote else {})
        ),
        cost_estimate=pl.CostEstimate(flops=4 * rows * width * (4 * width + 2 * ff), bytes_accessed=100 * 2**20, transcendentals=0),
        name="encoder_backward",
    )(lens, flag, vecs, pooled_grad, *weights, *saved)
    return tok, blocks, gvec


def forward_kernel(
    sizes, remote,
    lens, flag, small, tok, tab_s, in_s, out_s, up_s, down_s,
    x_o, mixed_o, prob_o, ctx_o, hid_o, n1_o, r1_o, act_o, gp_o, n2_o, r2_o, pooled_o, vecs_o, w_tab, w_in, w_out, w_up, w_down,
    v_in, v_out, v_up, v_down, tab_v, x_v, mixed, mask, pst, ctx, hid, hid_low, n_st, r1_v, r2_v, ast, gst, acc, small_v, up_v, up_p, tab_p, in_v, in_p, out_p, down_p,
    in_sem, out_sem, p_sem, a_sem, w_sem, *wires,
):
    groups, count, width, ff, chunk = sizes
    rows = groups * count
    pairs = width // 128
    slot = count // 4
    chunks = ff // chunk
    shards = 8
    load_tok = pltpu.make_async_copy(tok, x_v, in_sem.at[0])
    load_tok.start()
    loads = {}

    def load(name, src, dst):
        loads[name] = pltpu.make_async_copy(src, dst, w_sem.at[len(loads)])
        return loads[name]

    def before():
        for g in range(groups):
            which_q, _ = slot_lengths(lens, flag, g, True, count, 128)
            which_k, live_k = slot_lengths(lens, flag, g, False, count, 128)
            long = flag[g] > 0
            wq = which_q[:, :1]
            open_ = live_k[:1] & (long | (wq == which_k[:1]))
            mask[g] = jnp.where(open_, 0.0, -1000000000.0).astype(single)
        if remote:
            for made in stage:
                made.wait()
            third = width // 3
            for p in range(3):
                for i in range(3):
                    in_p[:, p * width + i * third : p * width + (i + 1) * third] = in_v[
                        :, i * width + p * third : i * width + (p + 1) * third
                    ]
            part = chunk // shards
            for fs in range(shards):
                for t in range(chunks):
                    up_p[:, t * chunk + fs * part : t * chunk + (fs + 1) * part] = up_v[
                        :, fs * (ff // shards) + t * part : fs * (ff // shards) + (t + 1) * part
                    ]

    cols = lambda ref, i, n: ref.at[:, pl.ds(i * n, n)]
    down_of = lambda t: w_down.at[:, pl.ds(t * (chunk // shards), chunk // shards), :] if remote else w_down.at[t]
    load("tab", w_tab, tab_v)
    for i in range(3):
        load("in%d" % i, cols(w_in, i, width), cols(v_in, i, width))
    load("out", w_out, v_out)
    for t in range(chunks):
        load("up%d" % t, cols(w_up, t, chunk), cols(v_up, t, chunk))
        load("down%d" % t, down_of(t), v_down.at[t])
    names = list(loads)
    if remote:
        send, recv, own_sem = wires
        here = place()
        x, y, z, c = here
        mine = 2 * z + c
        stage = [
            pltpu.make_async_copy(s, d, in_sem.at[1 + i])
            for i, (s, d) in enumerate(((tab_s, tab_p), (in_s, in_v), (up_s, up_v), (out_s, out_p), (down_s, down_p)))
        ]
        for made in stage:
            made.start()
        greet(neighbours(True), before)
        down_flat = w_down.reshape(ff, width)
        pieces = []
        for n, name in enumerate(names):
            part = int(name[-1]) if name[-1].isdigit() else 0
            kind = name.rstrip("0123456789")
            shard, full, pitch, rr, cc = {
                "tab": (tab_p, w_tab, width // shards, (0, width // shards), (0, count)),
                "in": (in_p, w_in, width // shards, (0, width // shards), (part * width, width)),
                "out": (out_p, w_out, width // shards, (0, width // shards), (0, width)),
                "up": (up_p, w_up, width // shards, (0, width // shards), (part * chunk, chunk)),
                "down": (down_p, down_flat, ff // shards, (part * (chunk // shards), chunk // shards), (0, width)),
            }[kind]
            pieces.append(Piece(n, (send, recv), here, shard, full, pitch, rr, cc))
        extra = Piece.COPIES * len(pieces)

        def small_copy(k, j):
            i = extra + 2 * k + j - 1
            return pltpu.make_async_remote_copy(
                src_ref=small, dst_ref=small_v.at[mine], send_sem=send.at[i], recv_sem=recv.at[i],
                device_id=device_at(x, y, (z + k) % 4, (c + j) % 2), device_id_type=MESH,
            )

        others = [(k, j) for k in range(4) for j in range(2) if (k, j) != (0, 0)]
        own = [
            pltpu.make_async_copy(s, d, own_sem.at[i])
            for i, (s, d) in enumerate(
                (
                    (small, small_v.at[mine]),
                    (tab_p, w_tab.at[pl.ds(pl.multiple_of(mine * (width // shards), 16), width // shards), :]),
                    (in_p, w_in.at[pl.ds(pl.multiple_of(mine * (width // shards), 16), width // shards), :]),
                    (out_p, w_out.at[pl.ds(pl.multiple_of(mine * (width // shards), 16), width // shards), :]),
                    (up_p, w_up.at[pl.ds(pl.multiple_of(mine * (width // shards), 16), width // shards), :]),
                    (down_p, w_down.at[mine]),
                )
            )
        ]
        own_of = {"tab": 1, "in": 2, "out": 3, "up": 4, "down": 5}

        first_done, kinds = [], []
        for stage, t in GATHER_EVENTS:
            kind = names[t].rstrip("0123456789")
            if stage == 4 and kind not in kinds:
                kinds.append(kind)
                first_done.append(t)

        def step(stage, t):
            getattr(pieces[t], ("begin", "plane", "diagonal", "core", "finish")[stage])()
            if stage == 4:
                kind = names[t].rstrip("0123456789")
                if t in first_done:
                    own[own_of[kind]].wait()
                loads[names[t]].start()

        steps = [functools.partial(step, *event) for event in GATHER_EVENTS]
        for k, j in others:
            small_copy(k, j).start()
        for n in range(GATHER_START):
            steps[n]()
        for i in (0, 1, 2, 3, 5):
            own[i].start()
        own[4].start()
    else:
        before()
        steps = []
        for n in names:
            loads[n].start()
        little = pltpu.make_async_copy(small, small_v, in_sem.at[1])
        little.start()
    done = [GATHER_START if remote else 0]

    def pump(upto):
        while done[0] < min(upto, len(steps)):
            steps[done[0]]()
            done[0] += 1

    def pump_in(i, marks):
        at_step = done[0]
        for count_, mark in enumerate(marks):
            mark = max(min(mark, len(steps)), at_step)
            if mark > at_step:

                @pl.when(i == count_)
                def _(a=at_step, b=mark):
                    for n in range(a, b):
                        steps[n]()

            at_step = mark

    def pumped(marks):
        done[0] = max([done[0]] + [min(m, len(steps)) for m in marks])

    def need(name):
        pump(GATHER_EVENTS.index((4, names.index(name))) + 1)
        loads[name].wait()

    stores = []

    def store(src, dst):
        made = pltpu.make_async_copy(src, dst, out_sem.at[len(stores)])
        made.start()
        stores.append(made)

    need("tab")
    load_tok.wait()
    for g in range(groups):
        long = flag[g] > 0
        for s in range(4):
            part = x_v[pl.ds(g * count + s * slot, slot), :].astype(single)
            place_ = jnp.where(
                long, tab_v[:, s * slot : (s + 1) * slot].T.astype(single), tab_v[:, :slot].T.astype(single)
            )
            both = part + place_
            hid[pl.ds(g * count + s * slot, slot), :] = both
            x_v[pl.ds(g * count + s * slot, slot), :] = both.astype(narrow)
    store(x_v, x_o)
    if remote:
        own[0].wait()
        for k, j in others:
            small_copy(k, j).wait_recv()
        total = small_v[0].astype(single)
        for i in range(1, shards):
            total = total + small_v[i].astype(single)
        vecs_o[...] = total
    else:
        little.wait()
        vecs_o[...] = small_v[...].astype(single)

    def vec(i, n=width):
        return vecs_o[i : i + 1, :n]

    lane = lax.broadcasted_iota(jnp.int32, (count, 128), 1)
    half = (lane < 64, lane >= 64)
    third = width // 3
    per_part = pairs // 3
    n = groups * per_part

    def prob_store(i, s_):
        return pltpu.make_async_copy(pst.at[s_], prob_o.at[i], p_sem.at[s_])

    for part in range(3):
        need("in%d" % part)
        cs = pl.ds(part * width, width)

        def project(b, _, cs=cs, part=part):
            r = at(b * 256, 256)
            mine = slice(part * third, (part + 1) * third)
            bias = jnp.concatenate([vec(0)[:, mine], jnp.zeros((1, third), single), vec(1)[:, mine]], 1)
            mixed[r, cs] = (dot(x_v[r, :], v_in[:, cs]) + bias).astype(narrow)
            return 0

        lax.fori_loop(0, rows // 256, project, 0)

        def attend(j, _, part=part):
            g = j // per_part
            w = j % per_part
            i = g * pairs + part * per_part + w
            s_ = j % 2
            r = at(g * count, count)
            if part == 0:

                @pl.when(j >= 2)
                def _():
                    prob_store(i, s_).wait()

            else:
                prob_store(i, s_).wait()

            q = mixed[r, at(part * width + w * 128, 128)]
            k = mixed[r, at(part * width + third + w * 128, 128)]
            v = mixed[r, at(part * width + 2 * third + w * 128, 128)]
            zero = jnp.zeros_like(q)
            out = [None] * (count // 256)
            for h in range(2):
                qh = jnp.where(half[h], q, zero) * jnp.asarray(0.125, narrow)
                vh = jnp.where(half[h], v, zero)
                for b in range(count // 256):
                    sc = dot_nt(qh[b * 256 : (b + 1) * 256], k) + mask[g, b * 256 : (b + 1) * 256, :]
                    e = jnp.exp(sc - jnp.max(sc, -1, keepdims=True))
                    low = (e * (1.0 / jnp.sum(e, -1, keepdims=True))).astype(narrow)
                    pst[s_, h, b * 256 : (b + 1) * 256, :] = low
                    o = dot(low, vh)
                    out[b] = o if out[b] is None else out[b] + o
            for b in range(count // 256):
                ctx[at(g * count + b * 256, 256), at(part * third + w * 128, 128)] = out[b].astype(narrow)
            prob_store(i, s_).start()
            pump_in(j, GATHER_ATTEND[part])
            return 0

        pump(GATHER_PROJECT[part])
        lax.fori_loop(0, n, attend, 0)
        pumped(GATHER_ATTEND[part])
    store(mixed, mixed_o)
    for s_ in range(2):
        prob_store(0, s_).wait()
    store(ctx, ctx_o)

    need("out")

    def first(b, _):
        r = at(b * 256, 256)
        total = hid[r, :] + dot(ctx[r, :], v_out[...]) + vec(2)
        unit, rstd = norm_rows(total)
        n_st[r, :] = unit
        r1_v[r, :] = jnp.broadcast_to(rstd, (256, 128))
        h = unit * vec(3) + vec(4)
        hid_low[r, :] = h.astype(narrow)
        acc[r, :] = h + vec(5)
        pump_in(b, GATHER_FIRST)
        return 0

    lax.fori_loop(0, rows // 256, first, 0)
    pumped(GATHER_FIRST)
    store(n_st, n1_o)
    n1_store = stores[-1]
    store(r1_v, r1_o)
    store(hid_low, hid_o)

    def act_copies(j, s_):
        return (
            pltpu.make_async_copy(ast.at[s_], act_o.at[j], a_sem.at[s_]),
            pltpu.make_async_copy(gst.at[s_], gp_o.at[j], a_sem.at[2 + s_]),
        )

    for j in range(chunks):
        s_ = j % 2
        need("up%d" % j)
        need("down%d" % j)
        if j >= 2:
            for made in act_copies(j - 2, s_):
                made.wait()
        cs = pl.ds(j * chunk, chunk)

        def feed(b, _, s_=s_, j=j, cs=cs):
            r = at(b * 256, 256)
            u = dot(hid_low[r, :], v_up[:, cs]) + vec(8 + j, chunk)
            a, d = gelu_pair(u)
            a = a.astype(narrow)
            ast[s_, r, :] = a
            gst[s_, r, :] = d.astype(narrow)
            acc[r, :] += dot(a, v_down[j].reshape(chunk, width))
            pltpu.make_async_copy(ast.at[s_, r], act_o.at[j, r], a_sem.at[s_]).start()
            pltpu.make_async_copy(gst.at[s_, r], gp_o.at[j, r], a_sem.at[2 + s_]).start()
            pump_in(b, GATHER_FEED[j])
            return 0

        lax.fori_loop(0, rows // 256, feed, 0)
        pumped(GATHER_FEED[j])

    n1_store.wait()
    for g in range(groups):
        _, live = slot_lengths(lens, flag, g, True, count, 128)
        sums = []
        for s in range(4):
            r = pl.ds(g * count + s * slot, slot)
            unit, rstd = norm_rows(acc[r, :])
            n_st[r, :] = unit
            r2_v[r, :] = jnp.broadcast_to(rstd, (slot, 128))
            out = unit * vec(6) + vec(7)
            pltpu.make_async_copy(n_st.at[r], n2_o.at[r], out_sem.at[8]).start()
            pltpu.make_async_copy(r2_v.at[r], r2_o.at[r], out_sem.at[9]).start()
            keep = live[s * slot : (s + 1) * slot, :1]
            sums.append(jnp.sum(jnp.where(keep, out, 0.0), 0, keepdims=True))
        long = flag[g] > 0
        for s in range(4):
            div = jnp.maximum(lens[g, s], 1).astype(single)
            if s == 0:
                total = jnp.where(long, sums[0] + sums[1] + sums[2] + sums[3], sums[0])
            else:
                total = jnp.where(long, 0.0, sums[s])
            pooled_o[4 * g + s : 4 * g + s + 1, :] = total / div
    pltpu.make_async_copy(n_st, n2_o, out_sem.at[8]).wait()
    pltpu.make_async_copy(r2_v, r2_o, out_sem.at[9]).wait()
    for j in range(max(chunks - 2, 0), chunks):
        for made in act_copies(j, j % 2):
            made.wait()
    for made in stores:
        if made is not n1_store:
            made.wait()
    if remote:
        for p in pieces:
            p.sent()
        for k, j in others:
            small_copy(k, j).wait_send()


def normalize_rows(pooled):
    return pooled * lax.rsqrt(jnp.sum(pooled * pooled, -1, keepdims=True) + 1e-06)


def slot_roles(bucket):
    long_slot = jnp.repeat(jnp.repeat(bucket, 2), 4) > 0
    slots = jnp.arange(long_slot.shape[0], dtype=jnp.int32)
    within = slots % 4
    odd_group = slots // 4 % 2
    query = jnp.where(long_slot, (within == 0) & (odd_group == 0), within % 2 == 0)
    passage = jnp.where(long_slot, (within == 0) & (odd_group == 1), within % 2 == 1)
    partner = jnp.where(long_slot, slots + 4, slots + 1)
    return (query, passage, partner)


def contrast(every, own, start, rows, bucket):
    query, passage, partner = slot_roles(bucket)
    pair_count = jnp.sum(4 - 3 * bucket).astype(single)
    logits = jnp.einsum("id,jd->ij", every, every, preferred_element_type=single) * 100.0
    columns = jnp.arange(logits.shape[1], dtype=jnp.int32)
    masked = jnp.where(passage[None, :], logits, -1000000000.0)
    top = jnp.max(masked, -1, keepdims=True)
    raised = jnp.exp(masked - top)
    total = jnp.sum(raised, -1, keepdims=True)
    spread = top[:, 0] + jnp.log(total[:, 0])
    match = columns[None, :] == partner[:, None]
    positive = jnp.sum(jnp.where(match, logits, 0.0), -1)
    loss = jnp.sum(jnp.where(query, spread - positive, 0.0)) / pair_count
    row_weight = jnp.where(query, 1.0, 0.0) / pair_count
    logit_grad = (row_weight[:, None] * (raised / total - match.astype(single))).astype(narrow)
    by_row = lax.dynamic_slice_in_dim(logit_grad, start, rows, 0)
    by_column = lax.dynamic_slice_in_dim(logit_grad, start, rows, 1)
    both = jnp.dot(by_row, every, preferred_element_type=single) + jnp.einsum(
        "ij,id->jd", by_column, every, preferred_element_type=single
    )
    return loss, both * 100.0


MESH = pl.DeviceIdType.MESH


def place():
    dp, fs = lax.axis_index("dp"), lax.axis_index("fsdp")
    return dp % 2, dp // 2, fs // 2, fs % 2


def device_at(x, y, z, c):
    return (y * 2 + x, z * 2 + c)


class Wires:
    def __init__(self, send, recv):
        self.send, self.recv, self.next, self.sent = send, recv, 0, []

    def copy(self, src, dst, device):
        i = self.next
        self.next += 1
        made = pltpu.make_async_remote_copy(
            src_ref=src, dst_ref=dst, send_sem=self.send.at[i], recv_sem=self.recv.at[i],
            device_id=device, device_id_type=MESH,
        )
        made.start()
        self.sent.append(made)
        return made

    def finish(self):
        for made in self.sent:
            made.wait_send()


def greet(devices, between=None):
    barrier = pltpu.get_barrier_semaphore()
    for d in devices:
        pl.semaphore_signal(barrier, inc=1, device_id=d, device_id_type=MESH)
    if between is not None:
        between()
    pl.semaphore_wait(barrier, len(devices))


def neighbours(small_too):
    x, y, z, c = place()
    found = [device_at(1 - x, y, z, c), device_at(x, 1 - y, z, c), device_at(x, y, z, 1 - c)]
    for k in (1, 2, 3):
        found.append(device_at(x, y, (z + k) % 4, c))
        if small_too:
            found.append(device_at(x, y, (z + k) % 4, 1 - c))
    return found


GATHER_EVENTS = ((0, 0), (0, 1), (1, 0), (0, 2), (1, 1), (0, 3), (2, 0), (1, 2), (0, 4), (2, 1), (0, 5), (3, 0), (1, 3), (4, 0), (0, 6), (2, 2), (3, 1), (1, 4), (2, 3), (1, 5), (0, 7), (4, 1), (0, 8), (3, 2), (2, 4), (1, 6), (3, 3), (4, 2), (0, 9), (4, 3), (2, 5), (1, 7), (3, 4), (0, 10), (1, 8), (4, 4), (2, 6), (3, 5), (1, 9), (4, 5), (2, 7), (1, 10), (2, 8), (3, 6), (4, 6), (2, 9), (3, 7), (4, 7), (2, 10), (3, 8), (3, 9), (4, 8), (3, 10), (4, 9), (4, 10))
GATHER_START = 2
GATHER_PROJECT = (27, 38, 44)
GATHER_ATTEND = ((28, 32, 33, 34), (38, 41, 41, 43), (44, 46, 47, 47))
GATHER_FIRST = (47, 49, 49, 50)
GATHER_FEED = ((51, 53, 54, 54), (55, 55, 55, 55), (55, 55, 55, 55))


class Piece:
    COPIES = 17

    def __init__(self, index, sems, at_, shard, full, pitch, rows, cols):
        self.send, self.recv = sems
        self.x, self.y, self.z, self.c = at_
        self.base = index * self.COPIES
        self.shard, self.full, self.pitch = shard, full, pitch
        self.r0, self.rows = rows
        self.c0, self.cols = cols
        self.both = self.rows % 64 == 0
        self.ways = ("x", "y", "both" if self.both else ("x" if index % 2 else "y"))

    def block(self, ref, fs, a=None, b=None, part=None):
        start = self.r0 if fs is None else fs * self.pitch + self.r0
        rows, col, cols = self.rows, self.c0, self.cols
        if a is not None:
            rows, cols = rows // 2, cols // 2
            start, col = start + a * rows, col + b * cols
        if part is not None:
            rows = rows // 2
            start = start + part * rows
        return ref.at[pl.ds(pl.multiple_of(start, 16), rows), pl.ds(pl.multiple_of(col, 128), cols)]

    def copy(self, i, src, dst, device):
        return pltpu.make_async_remote_copy(
            src_ref=src, dst_ref=dst, send_sem=self.send.at[self.base + i], recv_sem=self.recv.at[self.base + i],
            device_id=device, device_id_type=MESH,
        )

    def from_z(self, k):
        return 2 * ((self.z - k + 4) % 4) + self.c

    def by_z(self, k):
        mine = 2 * self.z + self.c
        there = device_at(self.x, self.y, (self.z + k) % 4, self.c)
        return self.copy(k - 1, self.block(self.shard, None, self.x, self.y), self.block(self.full, mine, self.x, self.y), there)

    def by_x(self, k):
        mine = self.block(self.full, self.from_z(k), self.x, self.y)
        return self.copy(2 + k, mine, mine, device_at(1 - self.x, self.y, self.z, self.c))

    def by_y(self, k):
        mine = self.block(self.full, self.from_z(k), self.x, self.y)
        return self.copy(5 + k, mine, mine, device_at(self.x, 1 - self.y, self.z, self.c))

    def corners(self, k):
        way = self.ways[k - 1]
        parts = (0, 1) if way == "both" else (None, None)
        made = []
        if way != "y":
            got = self.block(self.full, self.from_z(k), 1 - self.x, self.y, parts[0])
            made.append(self.copy(8 + k, got, got, device_at(self.x, 1 - self.y, self.z, self.c)))
        if way != "x":
            got = self.block(self.full, self.from_z(k), self.x, 1 - self.y, parts[1])
            made.append(self.copy(10 if k == 2 else 12, got, got, device_at(1 - self.x, self.y, self.z, self.c)))
        return made

    def by_core(self, k):
        there = device_at(self.x, self.y, self.z, 1 - self.c)
        got = self.block(self.full, self.from_z(k))
        src = self.block(self.shard, None) if k == 0 else got
        return self.copy(13 + k, src, got, there)

    def begin(self):
        for k in (1, 2, 3):
            self.by_z(k).start()
        self.by_core(0).start()

    def plane(self):
        for k in (1, 2, 3):
            self.by_z(k).wait_recv()
            self.by_x(k).start()
            self.by_y(k).start()

    def diagonal(self):
        for k in (1, 2, 3):
            self.by_x(k).wait_recv()
            self.by_y(k).wait_recv()
            for made in self.corners(k):
                made.start()

    def core(self):
        for k in (1, 2, 3):
            for made in self.corners(k):
                made.wait_recv()
            self.by_core(k).start()

    def finish(self):
        for k in range(4):
            self.by_core(k).wait_recv()

    def sent(self):
        for k in (1, 2, 3):
            for made in [self.by_z(k), self.by_x(k), self.by_y(k), self.by_core(k)] + self.corners(k):
                made.wait_send()
        self.by_core(0).wait_send()


class Sum:
    COPIES = 11

    def __init__(self, index, sems, at_, own, b1x, b1y, b2x, b2y, from_z, final):
        self.send, self.recv = sems
        self.x, self.y, self.z, self.c = at_
        self.base = index * self.COPIES
        self.own, self.b1x, self.b1y, self.b2x, self.b2y, self.from_z, self.final = own, b1x, b1y, b2x, b2y, from_z, final
        _, self.rows, self.cols = own.shape

    def rh(self, a):
        return pl.ds(pl.multiple_of(a * (self.rows // 2), 16), self.rows // 2)

    def ch(self, b):
        return pl.ds(pl.multiple_of(b * (self.cols // 2), 128), self.cols // 2)

    def copy(self, i, src, dst, device):
        return pltpu.make_async_remote_copy(
            src_ref=src, dst_ref=dst, send_sem=self.send.at[self.base + i], recv_sem=self.recv.at[self.base + i],
            device_id=device, device_id_type=MESH,
        )

    def to_x(self):
        return device_at(1 - self.x, self.y, self.z, self.c)

    def to_y(self):
        return device_at(self.x, 1 - self.y, self.z, self.c)

    def to_core(self, src, dst):
        return self.copy(0, src, dst, device_at(self.x, self.y, self.z, 1 - self.c))

    def halves(self):
        lo, hi = pl.ds(0, 2), pl.ds(2, 2)
        return (
            self.copy(1, self.own.at[lo, self.rh(1 - self.x), :], self.b1x, self.to_x()),
            self.copy(2, self.own.at[hi, :, self.ch(1 - self.y)], self.b1y, self.to_y()),
        )

    def quarters(self):
        lo, hi = pl.ds(0, 2), pl.ds(2, 2)
        return (
            self.copy(3, self.own.at[lo, self.rh(self.x), self.ch(1 - self.y)], self.b2y, self.to_y()),
            self.copy(4, self.own.at[hi, self.rh(1 - self.x), self.ch(self.y)], self.b2x, self.to_x()),
        )

    def along(self):
        return [
            self.copy(
                4 + k, self.own.at[(self.z + k) % 4, self.rh(self.x), self.ch(self.y)], self.from_z.at[k - 1],
                device_at(self.x, self.y, (self.z + k) % 4, self.c),
            )
            for k in (1, 2, 3)
        ]

    def back(self):
        mine = self.final.at[self.rh(self.x), self.ch(self.y)]
        return [
            self.copy(8, mine, mine, self.to_x()),
            self.copy(9, mine, mine, self.to_y()),
            self.copy(10, mine, mine, device_at(1 - self.x, 1 - self.y, self.z, self.c)),
        ]

    def add(self, zs, row0, rows, cols, other):
        step = self.rows // 2
        blocks = rows // step

        def body(i, _):
            zi = i // blocks
            r = i % blocks * step
            mine = (zs + zi, pl.ds(pl.multiple_of(row0 + r, 16), step), cols)
            theirs = other[zi, pl.ds(pl.multiple_of(r, 16), step), :]
            self.own[mine] = (self.own[mine].astype(single) + theirs.astype(single)).astype(narrow)
            return 0

        lax.fori_loop(0, 2 * blocks, body, 0)

    def first(self, stage, got):
        def body(i, _):
            self.own[i] = (stage[i, self.c].astype(single) + got[i].astype(single)).astype(narrow)
            return 0

        lax.fori_loop(0, 4, body, 0)
        for made in self.halves():
            made.start()

    def second(self):
        for made in self.halves():
            made.wait_recv()
        self.add(0, self.x * (self.rows // 2), self.rows // 2, slice(None), self.b1x)
        self.add(2, 0, self.rows, self.ch(self.y), self.b1y)
        for made in self.quarters():
            made.start()

    def third(self):
        for made in self.quarters():
            made.wait_recv()
        self.add(0, self.x * (self.rows // 2), self.rows // 2, self.ch(self.y), self.b2y)
        self.add(2, self.x * (self.rows // 2), self.rows // 2, self.ch(self.y), self.b2x)
        for made in self.along():
            made.start()

    def fourth(self):
        for made in self.along():
            made.wait_recv()
        total = self.own[self.z, self.rh(self.x), self.ch(self.y)].astype(single)
        for k in range(3):
            total = total + self.from_z[k].astype(single)
        self.final[self.rh(self.x), self.ch(self.y)] = total.astype(narrow)
        for made in self.back():
            made.start()

    def finish(self):
        for made in self.back():
            made.wait_recv()

    def sent(self):
        for made in list(self.halves()) + list(self.quarters()) + self.along() + self.back():
            made.wait_send()


class SumDeep(Sum):
    def __init__(self, index, sems, at_, own, half, quarter, from_z, final):
        super().__init__(index, sems, at_, own, None, None, None, None, from_z, final)
        self.half, self.quarter = half, quarter
        self.x_first = index % 4 == 1

    def shard(self, *where):
        return self.own.at[(self.z,) + where]

    def along(self):
        return [
            self.copy(4 + k, self.own.at[(self.z + k) % 4], self.from_z.at[k - 1], device_at(self.x, self.y, (self.z + k) % 4, self.c))
            for k in (1, 2, 3)
        ]

    def halves(self):
        if self.x_first:
            return (self.copy(1, self.shard(self.rh(1 - self.x), slice(None)), self.half, self.to_x()),)
        return (self.copy(1, self.shard(slice(None), self.ch(1 - self.y)), self.half, self.to_y()),)

    def quarters(self):
        if self.x_first:
            return (self.copy(3, self.shard(self.rh(self.x), self.ch(1 - self.y)), self.quarter, self.to_y()),)
        return (self.copy(3, self.shard(self.rh(1 - self.x), self.ch(self.y)), self.quarter, self.to_x()),)

    def first(self, stage, got):
        def body(i, _):
            self.own[i] = (stage[i, self.c].astype(single) + got[i].astype(single)).astype(narrow)
            return 0

        lax.fori_loop(0, 4, body, 0)
        for made in self.along():
            made.start()

    def second(self):
        for made in self.along():
            made.wait_recv()
        total = self.own[self.z].astype(single)
        for k in range(3):
            total = total + self.from_z[k].astype(single)
        self.own[self.z] = total.astype(narrow)
        for made in self.halves():
            made.start()

    def third(self):
        for made in self.halves():
            made.wait_recv()
        mine = (self.z, self.rh(self.x), slice(None)) if self.x_first else (self.z, slice(None), self.ch(self.y))
        self.own[mine] = (self.own[mine].astype(single) + self.half[...].astype(single)).astype(narrow)
        for made in self.quarters():
            made.start()

    def fourth(self):
        for made in self.quarters():
            made.wait_recv()
        total = self.own[self.z, self.rh(self.x), self.ch(self.y)].astype(single) + self.quarter[...].astype(single)
        self.final[self.rh(self.x), self.ch(self.y)] = total.astype(narrow)
        for made in self.back():
            made.start()


DEEP = (1, 3, 8)


class SumSmall:
    COPIES = 6

    def __init__(self, base, sems, at_, total, got):
        self.send, self.recv = sems
        self.x, self.y, self.z, self.c = at_
        self.base, self.total, self.got = base, total, got

    def copies(self, i):
        x, y, z, c = self.x, self.y, self.z, self.c
        to = [[device_at(x, y, z, 1 - c)], [device_at(1 - x, y, z, c)], [device_at(x, 1 - y, z, c)]]
        to.append([device_at(x, y, (z + k) % 4, c) for k in (1, 2, 3)])
        return [
            pltpu.make_async_remote_copy(
                src_ref=self.total.at[i], dst_ref=self.got.at[i + n], send_sem=self.send.at[self.base + i + n],
                recv_sem=self.recv.at[self.base + i + n], device_id=d, device_id_type=MESH,
            )
            for n, d in enumerate(to[i])
        ]

    def begin(self):
        for made in self.copies(0):
            made.start()

    def step(self, i):
        for made in self.copies(i):
            made.wait_recv()
        self.total[i + 1] = self.total[i] + self.got[i]
        for made in self.copies(i + 1):
            made.start()

    def finish(self, out):
        for made in self.copies(3):
            made.wait_recv()
        terms = []
        for i in range(4):
            term = self.total[3]
            for k in (1, 2, 3):
                term = jnp.where((self.z - k + 4) % 4 == i, self.got[2 + k], term)
            terms.append(term)
        out[...] = ((terms[0] + terms[1]) + terms[2]) + terms[3]
        for i in range(4):
            for made in self.copies(i):
                made.wait_send()


def contrast_kernel(slots, buckets, bucket, pooled, loss_o, grad_o, mine, every, full, send, recv, sem):
    x, y, z, c = place()
    device = (y * 2 + x) * 8 + 2 * z + c
    greet(neighbours(False))
    wires = Wires(send, recv)
    p = pooled[...]
    scale = lax.rsqrt(jnp.sum(p * p, -1, keepdims=True) + 1e-06)
    e = p * scale
    width = e.shape[1]
    hw = width // 2
    mine[...] = jnp.concatenate([e[:, :hw], e[:, hw:]], 0).astype(narrow)

    def slot_of(xx, yy, zz):
        return (yy * 2 + xx) * 8 + 2 * zz + c

    def block(xx, yy, zz):
        return every.at[slot_of(xx, yy, zz)]

    keep = pltpu.make_async_copy(mine, every.at[device], sem)
    keep.start()
    by_x = wires.copy(mine, block(x, y, z), device_at(1 - x, y, z, c))
    by_y = [wires.copy(mine, block(x, y, z), device_at(x, 1 - y, z, c))]
    by_z = [wires.copy(mine, block(x, y, z), device_at(x, y, (z + k) % 4, c)) for k in (1, 2, 3)]
    by_x.wait_recv()
    by_y.append(wires.copy(block(1 - x, y, z), block(1 - x, y, z), device_at(x, 1 - y, z, c)))
    by_z += [wires.copy(block(1 - x, y, z), block(1 - x, y, z), device_at(x, y, (z + k) % 4, c)) for k in (1, 2, 3)]
    for s in by_y:
        s.wait_recv()
    for xx in (x, 1 - x):
        by_z += [
            wires.copy(block(xx, 1 - y, z), block(xx, 1 - y, z), device_at(x, y, (z + k) % 4, c)) for k in (1, 2, 3)
        ]
    pair_size = 8

    def long_of(shape, axis):
        pair = lax.broadcasted_iota(jnp.int32, shape, axis) // pair_size
        found = jnp.zeros(shape, jnp.int32)
        for b in range(buckets):
            found = jnp.where(pair == b, bucket[b], found)
        return found > 0

    def roles(shape, axis):
        t = lax.broadcasted_iota(jnp.int32, shape, axis)
        long = long_of(shape, axis)
        within, odd = t % 4, t // 4 % 2
        query = jnp.where(long, jnp.where((within == 0) & (odd == 0), 1, 0), jnp.where(within % 2 == 0, 1, 0))
        passage = jnp.where(long, jnp.where((within == 0) & (odd == 1), 1, 0), jnp.where(within % 2 == 1, 1, 0))
        return query > 0, passage > 0, jnp.where(long, t + 4, t + 1)

    _, passage, _ = roles((8, slots), 1)
    query, _, partner = roles((slots, 128), 0)
    passage, query, partner = passage[:1], query[:, :1], partner[:, :1]
    pair_count = jnp.zeros((), single)
    for b in range(buckets):
        pair_count = pair_count + (4 - 3 * bucket[b]).astype(single)
    keep.wait()
    for s in by_z:
        s.wait_recv()
    others = []
    for yy in range(2):
        for xx in range(2):
            for zz in range(4):
                others.append(wires.copy(block(xx, yy, zz), block(xx, yy, zz), device_at(x, y, z, 1 - c)))
    for s in others:
        s.wait_recv()
    both = every[...].astype(single)
    left = both[:, :8, :].reshape(slots, hw).astype(narrow)
    right = both[:, 8:, :].reshape(slots, hw).astype(narrow)
    logits = (dot_nt(left, left) + dot_nt(right, right)) * 100.0
    masked = jnp.where(passage, logits, -1000000000.0)
    top = jnp.max(masked, -1, keepdims=True)
    raised = jnp.exp(masked - top)
    total = jnp.sum(raised, -1, keepdims=True)
    match = lax.broadcasted_iota(jnp.int32, (slots, slots), 1) == partner
    positive = jnp.sum(jnp.where(match, logits, 0.0), -1, keepdims=True)
    terms = jnp.where(query, top + jnp.log(total) - positive, 0.0)
    loss = jnp.sum(terms, 0, keepdims=True) / pair_count
    loss_o[...] = jnp.broadcast_to(loss, loss_o.shape)
    weight = jnp.where(query, 1.0, 0.0) / pair_count
    logit_grad = weight * (raised / total - jnp.where(match, 1.0, 0.0))
    by_row = logit_grad.astype(narrow)
    by_column = logit_grad.T.astype(narrow)
    full[:, :hw] = dot(by_row, left) + dot(by_column, left)
    full[:, hw:] = dot(by_row, right) + dot(by_column, right)
    g = full[pl.ds(pl.multiple_of(device * 8, 8), 8), :] * 100.0
    grad_o[...] = scale * g - p * (scale * scale * scale) * jnp.sum(p * g, -1, keepdims=True)
    wires.finish()


def run_contrast(bucket, pooled, devices):
    rows, width = pooled.shape
    slots = rows * devices
    dma = pltpu.SemaphoreType.DMA
    spec_v = pl.BlockSpec(memory_space=VM)
    copies = 1 + 2 + 12 + 16
    loss, grad = pl.pallas_call(
        functools.partial(contrast_kernel, slots, bucket.shape[0]),
        out_shape=[jax.ShapeDtypeStruct((8, 128), single), jax.ShapeDtypeStruct(pooled.shape, single)],
        in_specs=[pl.BlockSpec(memory_space=SM), spec_v],
        out_specs=[spec_v, spec_v],
        scratch_shapes=[
            VM((2 * rows, width // 2), narrow), VM((devices, 2 * rows, width // 2), narrow), VM((slots, width), single),
            dma((copies,)), dma((copies,)), dma(()),
        ],
        compiler_params=pltpu.CompilerParams(collective_id=3, has_side_effects=True),
        name="contrast",
    )(bucket, pooled)
    return loss[0, 0], grad


def gather_weights(tab, w_in, w_out, w_up, w_down, small):
    gat = lambda a: lax.all_gather(a, "fsdp", axis=0, tiled=True)
    return lax.all_gather(tab, "fsdp", axis=1, tiled=True), gat(w_in), gat(w_out), gat(w_up), gat(w_down), gat(small)


def reduce_all(grads, small):
    done = []
    for a in grads:
        part = lax.psum_scatter(a.astype(single), "fsdp", scatter_dimension=0, tiled=True)
        done.append(lax.psum(part.astype(narrow), "dp").astype(single))
    return done, lax.psum(small, ("dp", "fsdp"))


def local(
    tokens, lengths, bucket, position_table, in_projection, query_bias, value_bias, out_projection, out_bias,
    first_gain, first_shift, up_projection, up_bias, down_projection, down_bias, second_gain, second_shift,
):
    groups = lengths.shape[0]
    width = tokens.shape[1]
    count = tokens.shape[0] // groups
    shards = lax.axis_size("fsdp")
    ff = up_projection.shape[1]
    fs = lax.axis_index("fsdp")
    device = lax.axis_index("dp") * shards + fs
    small_parts = (query_bias, value_bias, out_bias, first_gain, first_shift, down_bias, second_gain, second_shift)
    piece = query_bias.shape[0]
    wide_piece = up_bias.shape[0]
    flag = lax.dynamic_slice_in_dim(jnp.repeat(bucket, 2), device * groups, groups)
    chunk = 1024
    chunks, per = ff // chunk, chunk // 8
    grid = lax.axis_size("dp") == 4 and shards == 8
    if grid:
        line = jnp.concatenate([v[None] for v in small_parts] + [jnp.zeros((8, piece), narrow)], 0)
        spread = lax.dynamic_update_slice(jnp.zeros((16, chunk), narrow), line, (0, fs * piece))
        ups = up_bias.reshape(chunks, per)
        small = lax.dynamic_update_slice(spread, ups, (8, fs * per))
        table = position_table.T
        weights = (in_projection, out_projection, up_projection, down_projection)
    else:
        vectors = jnp.concatenate(small_parts + (up_bias,))[None, :]
        table, w_in, w_out, w_up, w_down, small_all = gather_weights(
            position_table, in_projection, out_projection, up_projection, down_projection, vectors
        )
        table = table.T
        heads = small_all[:, : 8 * piece].reshape(shards, 8, piece).transpose(1, 0, 2).reshape(8, width)
        ups = small_all[:, 8 * piece :].reshape(8, chunks, per).transpose(1, 0, 2).reshape(chunks, chunk)
        small = jnp.concatenate(
            [jnp.pad(heads, ((0, 0), (0, chunk - width))), ups, jnp.zeros((8 - chunks, chunk), narrow)]
        )
        w_in = w_in.reshape(width, 3, 3, width // 3).transpose(0, 2, 1, 3).reshape(width, 3 * width)
        w_up = w_up.reshape(width, 8, chunks, per).transpose(0, 2, 1, 3).reshape(width, ff)
        w_down = w_down.reshape(8, chunks, per, width).transpose(1, 0, 2, 3)
        weights = (w_in, w_out, w_up, w_down)
    outs = run_forward(grid, groups, count, width, ff, chunk, lengths, flag, small, tokens, table, weights)
    saved, pooled, vecs = outs[:11], outs[11], outs[12]
    if grid:
        weights = tuple(outs[14:18])
    slots = groups * 4
    if grid:
        loss, pooled_grad = run_contrast(bucket, pooled, 4 * shards)
    else:
        embedded, norm_grad = jax.vjp(normalize_rows, pooled)
        every = lax.all_gather(embedded.astype(narrow), ("dp", "fsdp"), axis=0, tiled=True)
        loss, embed_grad = contrast(every, embedded, device * slots, slots, bucket)
        pooled_grad = norm_grad(embed_grad)[0]
    tokens_grad, blocks, gvec = run_backward(
        grid, groups, count, width, ff, chunk, lengths, flag, vecs, pooled_grad, weights, saved
    )
    shapes = item_shapes(count, width, ff, chunk)
    if grid:
        tokens_grad, gdown, gup, gout, gin, gtab = run_finish(shapes, chunks, tokens_grad, blocks)
    else:
        blocks = [b.reshape(8 * r, k) for b, (r, k) in zip(blocks, shapes)]
        gdown = jnp.stack([b.reshape(8, per, width) for b in blocks[0 : 2 * chunks : 2]], 1).reshape(ff, width)
        gup = jnp.stack([b.reshape(width, 8, per) for b in blocks[1 : 2 * chunks : 2]], 2).reshape(width, ff)
        gin = jnp.stack([b.reshape(width, 3, width // 3) for b in blocks[2 * chunks + 1 : 2 * chunks + 4]], 2)
        gin = gin.reshape(width, 3 * width)
        (gin, gout, gup, gdown, gtab), gvec = reduce_all((gin, blocks[2 * chunks], gup, gdown, blocks[-1]), gvec)
        gtab = gtab.T
    own = [lax.dynamic_slice_in_dim(gvec[i], fs * piece, piece) for i in range(8)]
    ups = gvec[8 : 8 + chunks].reshape(chunks, 8, per).transpose(1, 0, 2).reshape(ff)
    up_own = lax.dynamic_slice_in_dim(ups, fs * wide_piece, wide_piece)
    return (
        loss, pooled, tokens_grad, gtab, gin, own[0], own[1], gout, own[2], own[3], own[4], gup, up_own, gdown,
        own[5], own[6], own[7],
    )


def solution(mesh):
    rows = P(("dp", "fsdp"), None)
    vec = P("fsdp")
    mat = P("fsdp", None)
    in_specs = (rows, rows, P(), P(None, "fsdp"), mat, vec, vec, mat, vec, vec, vec, mat, vec, mat, vec, vec, vec)
    out_specs = (P(), rows, rows, P(None, "fsdp"), mat, vec, vec, mat, vec, vec, vec, mat, vec, mat, vec, vec, vec)
    return jax.shard_map(local, mesh=mesh, in_specs=in_specs, out_specs=out_specs, check_vma=False)
```

```python
import functools

import jax
import jax.numpy as jnp
from jax import lax
from jax.experimental import pallas as pl
from jax.experimental.pallas import tpu as pltpu
from jax.sharding import PartitionSpec as P

H = 12
narrow = jnp.bfloat16
single = jnp.float32
ANY = pl.ANY
VM = pltpu.VMEM
SM = pltpu.SMEM
LIMIT = 60 * 2**20


def dot(a, b):
    return lax.dot_general(a, b, (((1,), (0,)), ((), ())), preferred_element_type=single)


def dot_nt(a, b):
    return lax.dot_general(a, b, (((1,), (1,)), ((), ())), preferred_element_type=single)


def at(start, size):
    return pl.ds(pl.multiple_of(start, 128), size)


def gelu_pair(u):
    t = 1.0 / (1.0 + 0.23164189 * jnp.abs(u))
    e = jnp.exp(-0.5 * (u * u))
    tail = t * (
        0.127414796 + t * (-0.142248368 + t * (0.7107068705 + t * (-0.7265760135 + t * 0.5307027145)))
    )
    tail = tail * e
    phi = jnp.where(u < 0, tail, 1.0 - tail)
    return u * phi, phi + u * (e * 0.3989422804)


def norm_rows(value):
    mean = jnp.mean(value, -1, keepdims=True)
    centred = value - mean
    rstd = lax.rsqrt(jnp.mean(centred * centred, -1, keepdims=True) + 1e-06)
    return centred * rstd, rstd


def norm_back(grad, unit, rstd):
    one = jnp.mean(grad, -1, keepdims=True)
    two = jnp.mean(grad * unit, -1, keepdims=True)
    return rstd * (grad - one - unit * two)


def slot_lengths(lens, flag, g, along_rows, count, width):
    slot = count // 4
    shape = (count, width) if along_rows else (8, count)
    t = lax.broadcasted_iota(jnp.int32, shape, 0 if along_rows else 1)
    which = t // slot
    long = flag[g] > 0
    limit = jnp.where(which == 0, lens[g, 0], lens[g, 1])
    limit = jnp.where(which == 2, lens[g, 2], limit)
    limit = jnp.where(which == 3, lens[g, 3], limit)
    limit = jnp.where(long, lens[g, 0], limit)
    inside = jnp.where(long, t, t % slot)
    return which, inside < limit


SUM_EVENTS = ((0, 0), (0, 2), (1, 0), (0, 1), (0, 4), (0, 5), (1, 2), (0, 6), (0, 3), (1, 1), (1, 4), (2, 0), (0, 7), (2, 2), (1, 5), (1, 6), (1, 3), (2, 1), (2, 4), (3, 0), (1, 7), (3, 2), (2, 3), (3, 1), (3, 4), (0, 8), (0, 9), (2, 5), (3, 3), (0, 10), (2, 6), (1, 8), (1, 9), (2, 7), (3, 5), (1, 10), (3, 6), (2, 8), (3, 7), (2, 9), (2, 10), (3, 8), (3, 9), (3, 10))
SUMS_FEED = ((0, 0, 0, 0), (0, 0, 0, 0), (0, 0, 1, 1))
SUMS_UP = ((0, 0, 0, 0), (0, 0, 0, 0), (1, 1, 1, 1))
SUMS_NORM, SUMS_CTX, SUMS_XT, SUMS_BIAS = 2, 3, 3, 22
SUMS_ATTEND = ((4, 4, 5, 5), (7, 7, 10, 11), (13, 15, 19, 21))
SUMS_IN = (5, 12, 21)
SUMS_TOKEN = (23, 23, 23, 24)


def item_shapes(count, width, ff, chunk):
    found = []
    for _ in range(ff // chunk):
        found += [(chunk // 8, width), (width // 8, chunk)]
    return found + [(width // 8, width)] * 4 + [(width // 8, count)]


def backward_kernel(
    sizes, remote,
    lens, flag, vecs, pg, w_in, w_out, w_up, w_down, x_i, mixed_i, prob_i, ctx_i, hid_i, n1_i, r1_i, act_i, gp_i, n2_i, r2_i,
    *refs,
):
    groups, count, width, ff, chunk = sizes
    rows = groups * count
    pairs = width // 128
    slot = count // 4
    wide = ff // chunk
    blocks = rows // 256
    per = chunk // 8
    shapes = item_shapes(count, width, ff, chunk)
    items = len(shapes)
    tok_o, item_o, gvec_o, refs = refs[0], refs[1 : 1 + items], refs[1 + items], refs[2 + items :]
    (
        v_in, v_out, v_up, v_down, mixed, ctx, unit_v, rstd_v, ast, gst, low, hid_t, up_low, grad, dctx, stage_a, stage_b,
        gsmall, in_sem, p_sem, o_sem, i_sem,
    ) = refs[:22]
    wires = refs[22:]
    load = [
        pltpu.make_async_copy(s, d, in_sem.at[i])
        for i, (s, d) in enumerate(
            (
                (n2_i, unit_v), (r2_i, rstd_v), (hid_i, dctx), (n1_i, unit_v), (r1_i, rstd_v), (ctx_i, ctx),
                (w_out, v_out), (mixed_i, mixed), (x_i.reshape(8, per, width), v_down), (w_in, v_in),
            )
        )
    ]
    l_n2, l_r2, l_hid, l_n1, l_r1, l_ctx, l_wout, l_mixed, l_x, l_win = load

    def chunk_loads(j):
        down = w_down.at[j] if len(w_down.shape) == 4 else w_down.at[:, pl.ds(j * per, per), :]
        return (
            pltpu.make_async_copy(down, v_down, in_sem.at[10]),
            pltpu.make_async_copy(gp_i.at[j], gst, in_sem.at[11]),
            pltpu.make_async_copy(w_up.at[:, pl.ds(j * chunk, chunk)], v_up, in_sem.at[12]),
        )

    def act_load(j):
        return pltpu.make_async_copy(act_i.at[j], ast, in_sem.at[13])

    def prob_loads(i, s_):
        return [
            pltpu.make_async_copy(
                prob_i.at[i, h],
                up_low.at[pl.ds(pl.multiple_of(s_ * count, count), count), pl.ds(h * count, count)],
                p_sem.at[2 * s_ + h],
            )
            for h in range(2)
        ]

    l_n2.start()
    l_r2.start()
    l_hid.start()
    for made in chunk_loads(0):
        made.start()
    act_load(0).start()
    for made in (l_ctx, l_wout, l_mixed, l_win):
        made.start()

    def vec(i):
        return vecs[i : i + 1, :width]

    def staged(t, lead=None):
        r, k = shapes[t]
        ref = stage_a if t % 2 == 0 else stage_b
        if lead is None:
            return ref.at[:, :, pl.ds(0, r), pl.ds(0, k)]
        return ref.at[:, lead, pl.ds(0, r), pl.ds(0, k)]

    steps = []
    done = [0]
    firsts = [0]
    if remote:
        send, recv, free, total_v, got_v, ring = wires[:6]
        held = wires[6:]
        here = place()
        x, y, z, c = here
        sums = []
        for t in range(items):
            n_held = 5 if t in DEEP else 7
            sums.append((SumDeep if t in DEEP else Sum)(t, (send, recv), here, *held[:n_held]))
            held = held[n_held:]
        tiny = SumSmall(Sum.COPIES * items, (send, recv), here, total_v, got_v)

        def slot_of(t):
            r, k = shapes[t]
            return ring.at[t % 3, :, pl.ds(0, r), pl.ds(0, k)]

        def crossing(t):
            return sums[t].to_core(staged(t, 1 - c), slot_of(t))

        def item_store(t):
            return pltpu.make_async_copy(sums[t].final, item_o[t], i_sem.at[t])

        def first_of(n):
            crossing(n).wait_recv()
            sums[n].first(staged(n), slot_of(n))
            if n + 3 < items:
                pl.semaphore_signal(free, inc=1, device_id=device_at(x, y, z, 1 - c), device_id_type=MESH)

        def first(t):
            while firsts[0] <= t:
                first_of(firsts[0])
                firsts[0] += 1

        def first_in(i, which):
            for count_, t in which.items():
                pl.when(i == count_)(functools.partial(first_of, t))

        def ready(t):
            if t >= 2:
                first(t - 2)
                crossing(t - 2).wait_send()

        def produced(t):
            if t >= 3:
                pl.semaphore_wait(free, 1)
            crossing(t).start()

        def step(stage, t):
            getattr(sums[t], ("second", "third", "fourth", "finish")[stage])()
            if stage == 3:
                item_store(t).start()

        steps = [functools.partial(step, *event) for event in SUM_EVENTS]
    else:

        def item_store(t):
            return pltpu.make_async_copy(staged(t), item_o[t], i_sem.at[t])

        def first(t):
            pass

        def first_in(i, which):
            pass

        def ready(t):
            if t >= 2:
                item_store(t - 2).wait()

        def produced(t):
            item_store(t).start()

    def pump(upto):
        while done[0] < min(upto, len(steps)):
            steps[done[0]]()
            done[0] += 1

    def pump_in(i, marks):
        at_step = done[0]
        for count_, mark in enumerate(marks):
            mark = max(min(mark, len(steps)), at_step)
            if mark > at_step:

                @pl.when(i == count_)
                def _(a=at_step, b=mark):
                    for n in range(a, b):
                        steps[n]()

            at_step = mark

    def pumped(marks):
        done[0] = max([done[0]] + [min(m, len(steps)) for m in marks])

    def put(t, b, out):
        r, k = shapes[t]
        ref = stage_a if t % 2 == 0 else stage_b
        out = out.astype(narrow)
        ref[b, 0, :r, :k] = out[:r]
        ref[b, 1, :r, :k] = out[r:]

    def second_norm():
        l_n2.wait()
        l_r2.wait()
        gain_sum = jnp.zeros((1, width), single)
        shift_sum = jnp.zeros((1, width), single)
        bias_sum = jnp.zeros((1, width), single)
        for g in range(groups):
            _, live = slot_lengths(lens, flag, g, True, count, 128)
            long = flag[g] > 0
            for s in range(4):
                r = pl.ds(g * count + s * slot, slot)
                mine = pg[4 * g + s : 4 * g + s + 1, :] / jnp.maximum(lens[g, s], 1).astype(single)
                whole = pg[4 * g : 4 * g + 1, :] / jnp.maximum(lens[g, 0], 1).astype(single)
                row = jnp.where(long, whole, mine)
                keep = live[s * slot : (s + 1) * slot, :1]
                d = jnp.where(keep, row, 0.0)
                unit = unit_v[r, :]
                gain_sum = gain_sum + jnp.sum(d * unit, 0, keepdims=True)
                shift_sum = shift_sum + jnp.sum(d, 0, keepdims=True)
                back = norm_back(d * vec(6), unit, rstd_v[r, :1])
                grad[r, :] = back
                lowered = back.astype(narrow)
                low[r, :] = lowered
                bias_sum = bias_sum + jnp.sum(lowered.astype(single), 0, keepdims=True)
        gsmall[...] = jnp.zeros_like(gsmall)
        gsmall[6:7, :width] = gain_sum
        gsmall[7:8, :width] = shift_sum
        gsmall[5:6, :width] = bias_sum
        l_n1.start()
        l_r1.start()
        l_hid.wait()
        for b in range(rows // slot):
            r = pl.ds(b * slot, slot)
            hid_t[:, r] = dctx[r, :].T

    if remote:
        greet(neighbours(False) + [device_at(1 - x, 1 - y, z, c)], second_norm)
    else:
        second_norm()

    for j in range(wide):
        for made in chunk_loads(j):
            made.wait()

        def feed(b, total, j=j):
            r = at(b * 256, 256)
            up = (dot_nt(low[r, :], v_down[...].reshape(chunk, width)) * gst[r, :].astype(single)).astype(narrow)
            up_low[r, :] = up
            grad[r, :] += dot_nt(up, v_up[...])
            if j >= 1:
                first_in(b, {0: 2 * j - 2, 2: 2 * j - 1})
            pump_in(b, SUMS_FEED[j])
            return total + jnp.sum(up.astype(single), 0, keepdims=True)

        gsmall[8 + j : 9 + j, :] = lax.fori_loop(0, blocks, feed, jnp.zeros((1, chunk), single))
        firsts[0] = max(firsts[0], 2 * j)
        pumped(SUMS_FEED[j])
        if j + 1 < wide:
            for made in chunk_loads(j + 1):
                made.start()
        act_load(j).wait()
        ready(2 * j)

        def weigh(b, _, j=j):
            put(2 * j, b, dot(ast[:, at(b * 256, 256)].T, low[...]))
            return 0

        lax.fori_loop(0, 4, weigh, 0)
        produced(2 * j)
        if j + 1 < wide:
            act_load(j + 1).start()
        ready(2 * j + 1)

        def weigh_up(b, _, j=j):
            put(2 * j + 1, b, dot(hid_t[pl.ds(pl.multiple_of(b * (width // 4), 64), width // 4), :], up_low[...]))
            pump_in(b, SUMS_UP[j])
            return 0

        lax.fori_loop(0, 4, weigh_up, 0)
        pumped(SUMS_UP[j])
        produced(2 * j + 1)

    for made in prob_loads(0, 0) + prob_loads(1, 1):
        made.start()

    l_x.start()

    l_n1.wait()
    l_r1.wait()
    l_ctx.wait()
    l_wout.wait()
    gain_sum = jnp.zeros((1, width), single)
    shift_sum = jnp.zeros((1, width), single)
    bias_sum = jnp.zeros((1, width), single)
    for b in range(rows // slot):
        r = pl.ds(b * slot, slot)
        d = grad[r, :]
        unit = unit_v[r, :]
        gain_sum = gain_sum + jnp.sum(d * unit, 0, keepdims=True)
        shift_sum = shift_sum + jnp.sum(d, 0, keepdims=True)
        back = norm_back(d * vec(3), unit, rstd_v[r, :1])
        grad[r, :] = back
        lowered = back.astype(narrow)
        low[r, :] = lowered
        bias_sum = bias_sum + jnp.sum(lowered.astype(single), 0, keepdims=True)
        hid_t[:, r] = ctx[r, :].T
    gsmall[3:4, :width] = gain_sum
    gsmall[4:5, :width] = shift_sum
    gsmall[2:3, :width] = bias_sum
    first(2 * wide - 1)
    pump(SUMS_NORM)

    def weigh_by_columns(t, other):
        def body(b, _):
            put(t, b, dot(hid_t[pl.ds(pl.multiple_of(b * (width // 4), 64), width // 4), :], other()))
            return 0

        lax.fori_loop(0, 4, body, 0)

    t_out = 2 * wide
    ready(t_out)
    weigh_by_columns(t_out, lambda: low[...])
    produced(t_out)

    def context_back(b, _):
        r = at(b * 256, 256)
        dctx[r, :] = dot_nt(low[r, :], v_out[...]).astype(narrow)
        return 0

    lax.fori_loop(0, blocks, context_back, 0)
    first(t_out)
    pump(SUMS_CTX)
    l_x.wait()
    for b in range(8):
        hid_t[:, pl.ds(b * per, per)] = v_down[b].T
    pump(SUMS_XT)

    l_mixed.wait()
    lane = lax.broadcasted_iota(jnp.int32, (count, 128), 1)
    half = (lane < 64, lane >= 64)
    scale = jnp.asarray(0.125, narrow)
    third = width // 3
    per_part = pairs // 3
    n = groups * per_part

    def prob_index(j, part):
        return j // per_part * pairs + part * per_part + j % per_part

    def attend(j, _, part):
        g = j // per_part
        s_ = j % 2
        r = at(g * count, count)
        for made in prob_loads(prob_index(j, part), s_):
            made.wait()
        base = part * width + j % per_part * 128
        c_q = at(base, 128)
        c_k = at(base + third, 128)
        c_v = at(base + 2 * third, 128)
        c_c = at(part * third + j % per_part * 128, 128)
        q = mixed[r, c_q] * scale
        k = mixed[r, c_k]
        v = mixed[r, c_v]
        dc = dctx[r, c_c]
        c = ctx[r, c_c]
        q_t = q.T
        dc_t = dc.T
        zero = jnp.zeros_like(q)
        prod = dc.astype(single) * c.astype(single)
        dq = [None] * (count // 512)
        dk_t = []
        dv_t = []
        for h in range(2):
            dch = jnp.where(half[h], dc, zero)
            kh = jnp.where(half[h], k, zero)
            d = jnp.sum(jnp.where(half[h], prod, 0.0), -1, keepdims=True)
            dkh = None
            dvh = None
            for b in range(count // 512):
                rb = slice(b * 512, (b + 1) * 512)
                prob = up_low[pl.ds(pl.multiple_of(s_ * count + b * 512, 512), 512), h * count : (h + 1) * count]
                dp = dot_nt(dch[rb], v)
                ds = (prob.astype(single) * (dp - d[rb])).astype(narrow)
                o = dot(ds, kh)
                dq[b] = o if dq[b] is None else dq[b] + o
                hr = slice(h * 64, (h + 1) * 64)
                one = dot(q_t[hr, rb], ds)
                two = dot(dc_t[hr, rb], prob)
                dkh = one if dkh is None else dkh + one
                dvh = two if dvh is None else dvh + two
            dk_t.append(dkh)
            dv_t.append(dvh)
        for b in range(count // 512):
            mixed[at(g * count + b * 512, 512), c_q] = (dq[b] * 0.125).astype(narrow)
        mixed[r, c_k] = jnp.concatenate(dk_t, 0).T.astype(narrow)
        mixed[r, c_v] = jnp.concatenate(dv_t, 0).T.astype(narrow)

        @pl.when(part * n + j + 2 < 3 * n)
        def _():
            for made in prob_loads(prob_index((j + 2) % n, part + (j + 2) // n), s_):
                made.start()

        if part >= 1:
            first_in(j, {0: t_out + part})
        pump_in(j, SUMS_ATTEND[part])
        return 0

    l_win.wait()
    for part in range(3):
        lax.fori_loop(0, n, functools.partial(attend, part=part), 0)
        if part >= 1:
            firsts[0] = max(firsts[0], t_out + part + 1)
        pumped(SUMS_ATTEND[part])
        cols = pl.ds(part * width, width)
        ready(t_out + 1 + part)

        def in_weigh(b, _, cols=cols, part=part):
            put(t_out + 1 + part, b, dot(hid_t[pl.ds(pl.multiple_of(b * (width // 4), 64), width // 4), :], mixed[:, cols]))
            return 0

        lax.fori_loop(0, 4, in_weigh, 0)
        produced(t_out + 1 + part)
        pump(SUMS_IN[part])

    for p in range(3):

        def bias(b, total, p=p):
            r = at(b * 256, 256)
            q_cols = slice(p * width, p * width + third)
            v_cols = slice(p * width + 2 * third, (p + 1) * width)
            return (
                total[0] + jnp.sum(mixed[r, q_cols].astype(single), 0, keepdims=True),
                total[1] + jnp.sum(mixed[r, v_cols].astype(single), 0, keepdims=True),
            )

        zero_row = jnp.zeros((1, third), single)
        q_sum, v_sum = lax.fori_loop(0, blocks, bias, (zero_row, zero_row))
        gsmall[0:1, p * third : (p + 1) * third] = q_sum
        gsmall[1:2, p * third : (p + 1) * third] = v_sum
    first(t_out + 3)
    pump(SUMS_BIAS)
    if remote:
        total_v[0] = gsmall[...]
        tiny.begin()

    def token_back(b, _):
        r = at(b * 256, 256)
        grad[r, :] += dot_nt(mixed[r, :], v_in[...])
        pump_in(b, SUMS_TOKEN)
        return 0

    lax.fori_loop(0, blocks, token_back, 0)
    pumped(SUMS_TOKEN)
    tok_store = pltpu.make_async_copy(grad, tok_o, o_sem.at[0])
    tok_store.start()
    last = items - 1
    ready(last)
    ref = stage_a if last % 2 == 0 else stage_b
    for s in range(4):
        total = None
        for g in range(groups):
            long = flag[g] > 0
            r = pl.ds(g * count + s * slot, slot)
            if s == 0:
                other = grad[r, :]
                for o in range(1, 4):
                    other = other + grad[pl.ds(g * count + o * slot, slot), :]
                piece = jnp.where(long, grad[r, :], other)
            else:
                piece = jnp.where(long, grad[r, :], 0.0)
            total = piece if total is None else total + piece
        turned = total.T.astype(narrow)
        for fs in range(8):
            ref[fs // 2, fs % 2, : width // 8, s * slot : (s + 1) * slot] = turned[
                fs * (width // 8) : (fs + 1) * (width // 8), :
            ]
    produced(last)
    if remote:
        first(last)
        for i in range(3):
            pump(done[0] + 2)
            tiny.step(i)
        pump(len(steps))
        tiny.finish(gvec_o)
        for t in range(items):
            item_store(t).wait()
            sums[t].sent()
        for t in (items - 2, items - 1):
            crossing(t).wait_send()
    else:
        gvec_o[...] = gsmall[...]
        for t in (items - 2, items - 1):
            item_store(t).wait()
    tok_store.wait()


def finish_kernel(shapes, wide, tok, *refs):
    given, (tok_o, down, up, out, qkv, tab, buf, load_sem, store_sem) = refs[: len(shapes)], refs[len(shapes) :]
    parts = 4
    n = tok.shape[0] // parts
    moves = [
        (
            pltpu.make_async_copy(tok.at[pl.ds(i * n, n), :], buf.at[i], load_sem.at[i]),
            pltpu.make_async_copy(buf.at[i], tok_o.at[pl.ds(i * n, n), :], store_sem.at[i]),
        )
        for i in range(parts)
    ]
    for load, _ in moves:
        load.start()
    for t in range(wide):
        r, k = shapes[2 * t]
        down[t * r : (t + 1) * r, :] = given[2 * t][...].astype(single)
        _, k = shapes[2 * t + 1]
        part = k // 8
        for fs in range(8):
            up[:, fs * wide * part + t * part : fs * wide * part + (t + 1) * part] = given[2 * t + 1][
                :, fs * part : (fs + 1) * part
            ].astype(single)
    out[...] = given[2 * wide][...].astype(single)
    n = shapes[2 * wide + 1][1]
    third = n // 3
    for p in range(3):
        for i in range(3):
            qkv[:, i * n + p * third : i * n + (p + 1) * third] = given[2 * wide + 1 + p][
                :, i * third : (i + 1) * third
            ].astype(single)
    tab[...] = given[2 * wide + 4][...].astype(single)
    for load, keep in moves:
        load.wait()
        keep.start()
    for _, keep in moves:
        keep.wait()


def run_finish(shapes, wide, tok, given):
    (r_down, width), (r, chunk) = shapes[0], shapes[1]
    count = shapes[-1][1]
    sds = jax.ShapeDtypeStruct
    return pl.pallas_call(
        functools.partial(finish_kernel, shapes, wide),
        in_specs=[pl.BlockSpec(memory_space=ANY)] + [pl.BlockSpec(memory_space=VM)] * len(given),
        out_specs=[pl.BlockSpec(memory_space=ANY)] + [pl.BlockSpec(memory_space=VM)] * 5,
        out_shape=[
            sds(tok.shape, single),
            sds((r_down * wide, width), single), sds((r, chunk * wide), single), sds((r, width), single),
            sds((r, 3 * width), single), sds((r, count), single),
        ],
        scratch_shapes=[
            VM((4, tok.shape[0] // 4, width), single), pltpu.SemaphoreType.DMA((4,)), pltpu.SemaphoreType.DMA((4,)),
        ],
        compiler_params=pltpu.CompilerParams(vmem_limit_bytes=LIMIT),
        name="finish",
    )(tok, *given)


def shapes_of(groups, count, width, ff, chunk):
    rows = groups * count
    pairs = width // 128
    chunks = ff // chunk
    return dict(
        x=((rows, width), narrow),
        mixed=((rows, 3 * width), narrow),
        prob=((groups * pairs, 2, count, count), narrow),
        ctx=((rows, width), narrow),
        hid=((rows, width), narrow),
        n1=((rows, width), single),
        r1=((rows, 128), single),
        act=((chunks, rows, chunk), narrow),
        gp=((chunks, rows, chunk), narrow),
        n2=((rows, width), single),
        r2=((rows, 128), single),
    )


def run_forward(remote, groups, count, width, ff, chunk, lens, flag, small, tok, tab, weights):
    rows = groups * count
    chunks = ff // chunk
    saved = shapes_of(groups, count, width, ff, chunk)
    outs = [jax.ShapeDtypeStruct(*v) for v in saved.values()]
    outs.append(jax.ShapeDtypeStruct((groups * 4, width), single))
    outs.append(jax.ShapeDtypeStruct((16, chunk), single))
    spec_any = pl.BlockSpec(memory_space=ANY)
    spec_v = pl.BlockSpec(memory_space=VM)
    spec_s = pl.BlockSpec(memory_space=SM)
    dma = pltpu.SemaphoreType.DMA
    n_items = 5 + 2 * chunks
    extra = []
    if remote:
        whole = [
            jax.ShapeDtypeStruct((width, count), narrow),
            jax.ShapeDtypeStruct((width, 3 * width), narrow),
            jax.ShapeDtypeStruct((width, width), narrow),
            jax.ShapeDtypeStruct((width, ff), narrow),
            jax.ShapeDtypeStruct((8, ff // 8, width), narrow),
        ]
        outs += whole
        copies = Piece.COPIES * n_items + 8
        extra = [dma((copies,)), dma((copies,)), dma((6,))]
        body = functools.partial(forward_kernel, (groups, count, width, ff, chunk), True)
    else:

        def body(*refs):
            head = 9
            given = refs[4:head]
            rest = refs[head:]
            return forward_kernel((groups, count, width, ff, chunk), False, *refs[:head], *rest[:13], *given, *rest[13:])

    per = chunk // 8
    return pl.pallas_call(
        body,
        out_shape=outs,
        in_specs=[spec_s, spec_s, spec_any] + [spec_any] * 6,
        out_specs=[spec_any] * 11 + [spec_v, spec_v] + [spec_any] * (5 if remote else 0),
        scratch_shapes=[
            VM((width, 3 * width), narrow),
            VM((width, width), narrow),
            VM((width, ff), narrow),
            VM((chunks, 8, per, width), narrow),
            VM((width, count), narrow),
            VM((rows, width), narrow),
            VM((rows, 3 * width), narrow),
            VM((groups, count, count), single),
            VM((2, 2, count, count), narrow),
            VM((rows, width), narrow),
            VM((rows, width), single),
            VM((rows, width), narrow),
            VM((rows, width), single),
            VM((rows, 128), single),
            VM((rows, 128), single),
            VM((2, rows, chunk), narrow),
            VM((2, rows, chunk), narrow),
            VM((rows, width), single),
            VM((8, 16, chunk) if remote else (16, chunk), narrow),
            VM((width // 8, ff) if remote else (16, 128), narrow),
            VM((width // 8, ff) if remote else (16, 128), narrow),
            VM((width // 8, count) if remote else (16, 128), narrow),
            VM((width // 8, 3 * width) if remote else (16, 128), narrow),
            VM((width // 8, 3 * width) if remote else (16, 128), narrow),
            VM((width // 8, width) if remote else (16, 128), narrow),
            VM((ff // 8, width) if remote else (16, 128), narrow),
            dma((6,)), dma((10,)), dma((2,)), dma((4,)), dma((n_items,)),
        ]
        + extra,
        compiler_params=pltpu.CompilerParams(
            vmem_limit_bytes=LIMIT, **(dict(collective_id=1, has_side_effects=True) if remote else {})
        ),
        cost_estimate=pl.CostEstimate(flops=2 * rows * width * (4 * width + 2 * ff), bytes_accessed=80 * 2**20, transcendentals=10**7),
        name="encoder_forward",
    )(lens, flag, small, tok, tab, *weights)


def run_backward(remote, groups, count, width, ff, chunk, lens, flag, vecs, pooled_grad, weights, saved):
    rows = groups * count
    chunks, per = ff // chunk, chunk // 8
    shapes = item_shapes(count, width, ff, chunk)
    items = len(shapes)
    spec_any = pl.BlockSpec(memory_space=ANY)
    spec_v = pl.BlockSpec(memory_space=VM)
    spec_s = pl.BlockSpec(memory_space=SM)
    dma = pltpu.SemaphoreType.DMA
    tall = max(r for r, _ in shapes)
    broad = max(k for _, k in shapes)
    extra = []
    if remote:
        copies = Sum.COPIES * items + SumSmall.COPIES
        extra = [
            dma((copies,)), dma((copies,)), pltpu.SemaphoreType.REGULAR, VM((4, 16, chunk), single), VM((6, 16, chunk), single),
            VM((3, 4, tall, broad), narrow),
        ]
        for t, (r, k) in enumerate(shapes):
            if t in DEEP:
                half = (r // 2, k) if t % 4 == 1 else (r, k // 2)
                extra += [
                    VM((4, r, k), narrow), VM(half, narrow), VM((r // 2, k // 2), narrow), VM((3, r, k), narrow),
                    VM((r, k), narrow),
                ]
                continue
            extra += [
                VM((4, r, k), narrow), VM((2, r // 2, k), narrow), VM((2, r, k // 2), narrow), VM((2, r // 2, k // 2), narrow),
                VM((2, r // 2, k // 2), narrow), VM((3, r // 2, k // 2), narrow), VM((r, k), narrow),
            ]
    outs = [jax.ShapeDtypeStruct((rows, width), single)]
    outs += [jax.ShapeDtypeStruct((r, k) if remote else (4, 2, r, k), narrow) for r, k in shapes]
    outs += [jax.ShapeDtypeStruct((16, chunk), single)]
    tok, *blocks, gvec = pl.pallas_call(
        functools.partial(backward_kernel, (groups, count, width, ff, chunk), remote),
        out_shape=outs,
        in_specs=[spec_s, spec_s, spec_v, spec_v] + [spec_any] * 15,
        out_specs=[spec_any] * (1 + items) + [spec_v],
        scratch_shapes=[
            VM((width, 3 * width), narrow),
            VM((width, width), narrow),
            VM((width, chunk), narrow),
            VM((8, per, width), narrow),
            VM((rows, 3 * width), narrow),
            VM((rows, width), narrow),
            VM((rows, width), single),
            VM((rows, 128), single),
            VM((rows, chunk), narrow),
            VM((rows, chunk), narrow),
            VM((rows, width), narrow),
            VM((width, rows), narrow),
            VM((rows, chunk), narrow),
            VM((rows, width), single),
            VM((rows, width), narrow),
            VM((4, 2, tall, max(k for _, k in shapes[::2])), narrow),
            VM((4, 2, max(r for r, _ in shapes[1::2]), broad), narrow),
            VM((16, chunk), single),
            dma((14,)), dma((4,)), dma((1,)), dma((items,)),
        ]
        + extra,
        compiler_params=pltpu.CompilerParams(
            vmem_limit_bytes=62 * 2**20, **(dict(collective_id=2, has_side_effects=True) if remote else {})
        ),
        cost_estimate=pl.CostEstimate(flops=4 * rows * width * (4 * width + 2 * ff), bytes_accessed=100 * 2**20, transcendentals=0),
        name="encoder_backward",
    )(lens, flag, vecs, pooled_grad, *weights, *saved)
    return tok, blocks, gvec


def forward_kernel(
    sizes, remote,
    lens, flag, small, tok, tab_s, in_s, out_s, up_s, down_s,
    x_o, mixed_o, prob_o, ctx_o, hid_o, n1_o, r1_o, act_o, gp_o, n2_o, r2_o, pooled_o, vecs_o, w_tab, w_in, w_out, w_up, w_down,
    v_in, v_out, v_up, v_down, tab_v, x_v, mixed, mask, pst, ctx, hid, hid_low, n_st, r1_v, r2_v, ast, gst, acc, small_v, up_v, up_p, tab_p, in_v, in_p, out_p, down_p,
    in_sem, out_sem, p_sem, a_sem, w_sem, *wires,
):
    groups, count, width, ff, chunk = sizes
    rows = groups * count
    pairs = width // 128
    slot = count // 4
    chunks = ff // chunk
    shards = 8
    load_tok = pltpu.make_async_copy(tok, x_v, in_sem.at[0])
    load_tok.start()
    loads = {}

    def load(name, src, dst):
        loads[name] = pltpu.make_async_copy(src, dst, w_sem.at[len(loads)])
        return loads[name]

    def before():
        for g in range(groups):
            which_q, _ = slot_lengths(lens, flag, g, True, count, 128)
            which_k, live_k = slot_lengths(lens, flag, g, False, count, 128)
            long = flag[g] > 0
            wq = which_q[:, :1]
            open_ = live_k[:1] & (long | (wq == which_k[:1]))
            mask[g] = jnp.where(open_, 0.0, -1000000000.0).astype(single)
        if remote:
            for made in stage:
                made.wait()
            third = width // 3
            for p in range(3):
                for i in range(3):
                    in_p[:, p * width + i * third : p * width + (i + 1) * third] = in_v[
                        :, i * width + p * third : i * width + (p + 1) * third
                    ]
            part = chunk // shards
            for fs in range(shards):
                for t in range(chunks):
                    up_p[:, t * chunk + fs * part : t * chunk + (fs + 1) * part] = up_v[
                        :, fs * (ff // shards) + t * part : fs * (ff // shards) + (t + 1) * part
                    ]

    cols = lambda ref, i, n: ref.at[:, pl.ds(i * n, n)]
    down_of = lambda t: w_down.at[:, pl.ds(t * (chunk // shards), chunk // shards), :] if remote else w_down.at[t]
    load("tab", w_tab, tab_v)
    for i in range(3):
        load("in%d" % i, cols(w_in, i, width), cols(v_in, i, width))
    load("out", w_out, v_out)
    for t in range(chunks):
        load("up%d" % t, cols(w_up, t, chunk), cols(v_up, t, chunk))
        load("down%d" % t, down_of(t), v_down.at[t])
    names = list(loads)
    if remote:
        send, recv, own_sem = wires
        here = place()
        x, y, z, c = here
        mine = 2 * z + c
        stage = [
            pltpu.make_async_copy(s, d, in_sem.at[1 + i])
            for i, (s, d) in enumerate(((tab_s, tab_p), (in_s, in_v), (up_s, up_v), (out_s, out_p), (down_s, down_p)))
        ]
        for made in stage:
            made.start()
        greet(neighbours(True), before)
        down_flat = w_down.reshape(ff, width)
        pieces = []
        for n, name in enumerate(names):
            part = int(name[-1]) if name[-1].isdigit() else 0
            kind = name.rstrip("0123456789")
            shard, full, pitch, rr, cc = {
                "tab": (tab_p, w_tab, width // shards, (0, width // shards), (0, count)),
                "in": (in_p, w_in, width // shards, (0, width // shards), (part * width, width)),
                "out": (out_p, w_out, width // shards, (0, width // shards), (0, width)),
                "up": (up_p, w_up, width // shards, (0, width // shards), (part * chunk, chunk)),
                "down": (down_p, down_flat, ff // shards, (part * (chunk // shards), chunk // shards), (0, width)),
            }[kind]
            pieces.append(Piece(n, (send, recv), here, shard, full, pitch, rr, cc))
        extra = Piece.COPIES * len(pieces)

        def small_copy(k, j):
            i = extra + 2 * k + j - 1
            return pltpu.make_async_remote_copy(
                src_ref=small, dst_ref=small_v.at[mine], send_sem=send.at[i], recv_sem=recv.at[i],
                device_id=device_at(x, y, (z + k) % 4, (c + j) % 2), device_id_type=MESH,
            )

        others = [(k, j) for k in range(4) for j in range(2) if (k, j) != (0, 0)]
        own = [
            pltpu.make_async_copy(s, d, own_sem.at[i])
            for i, (s, d) in enumerate(
                (
                    (small, small_v.at[mine]),
                    (tab_p, w_tab.at[pl.ds(pl.multiple_of(mine * (width // shards), 16), width // shards), :]),
                    (in_p, w_in.at[pl.ds(pl.multiple_of(mine * (width // shards), 16), width // shards), :]),
                    (out_p, w_out.at[pl.ds(pl.multiple_of(mine * (width // shards), 16), width // shards), :]),
                    (up_p, w_up.at[pl.ds(pl.multiple_of(mine * (width // shards), 16), width // shards), :]),
                    (down_p, w_down.at[mine]),
                )
            )
        ]
        own_of = {"tab": 1, "in": 2, "out": 3, "up": 4, "down": 5}

        first_done, kinds = [], []
        for stage, t in GATHER_EVENTS:
            kind = names[t].rstrip("0123456789")
            if stage == 4 and kind not in kinds:
                kinds.append(kind)
                first_done.append(t)

        def step(stage, t):
            getattr(pieces[t], ("begin", "plane", "diagonal", "core", "finish")[stage])()
            if stage == 4:
                kind = names[t].rstrip("0123456789")
                if t in first_done:
                    own[own_of[kind]].wait()
                loads[names[t]].start()

        steps = [functools.partial(step, *event) for event in GATHER_EVENTS]
        for k, j in others:
            small_copy(k, j).start()
        for n in range(GATHER_START):
            steps[n]()
        for i in (0, 1, 2, 3, 5):
            own[i].start()
        own[4].start()
    else:
        before()
        steps = []
        for n in names:
            loads[n].start()
        little = pltpu.make_async_copy(small, small_v, in_sem.at[1])
        little.start()
    done = [GATHER_START if remote else 0]

    def pump(upto):
        while done[0] < min(upto, len(steps)):
            steps[done[0]]()
            done[0] += 1

    def pump_in(i, marks):
        at_step = done[0]
        for count_, mark in enumerate(marks):
            mark = max(min(mark, len(steps)), at_step)
            if mark > at_step:

                @pl.when(i == count_)
                def _(a=at_step, b=mark):
                    for n in range(a, b):
                        steps[n]()

            at_step = mark

    def pumped(marks):
        done[0] = max([done[0]] + [min(m, len(steps)) for m in marks])

    def need(name):
        pump(GATHER_EVENTS.index((4, names.index(name))) + 1)
        loads[name].wait()

    stores = []

    def store(src, dst):
        made = pltpu.make_async_copy(src, dst, out_sem.at[len(stores)])
        made.start()
        stores.append(made)

    need("tab")
    load_tok.wait()
    for g in range(groups):
        long = flag[g] > 0
        for s in range(4):
            part = x_v[pl.ds(g * count + s * slot, slot), :].astype(single)
            place_ = jnp.where(
                long, tab_v[:, s * slot : (s + 1) * slot].T.astype(single), tab_v[:, :slot].T.astype(single)
            )
            both = part + place_
            hid[pl.ds(g * count + s * slot, slot), :] = both
            x_v[pl.ds(g * count + s * slot, slot), :] = both.astype(narrow)
    store(x_v, x_o)
    if remote:
        own[0].wait()
        for k, j in others:
            small_copy(k, j).wait_recv()
        total = small_v[0].astype(single)
        for i in range(1, shards):
            total = total + small_v[i].astype(single)
        vecs_o[...] = total
    else:
        little.wait()
        vecs_o[...] = small_v[...].astype(single)

    def vec(i, n=width):
        return vecs_o[i : i + 1, :n]

    lane = lax.broadcasted_iota(jnp.int32, (count, 128), 1)
    half = (lane < 64, lane >= 64)
    third = width // 3
    per_part = pairs // 3
    n = groups * per_part

    def prob_store(i, s_):
        return pltpu.make_async_copy(pst.at[s_], prob_o.at[i], p_sem.at[s_])

    for part in range(3):
        need("in%d" % part)
        cs = pl.ds(part * width, width)

        def project(b, _, cs=cs, part=part):
            r = at(b * 256, 256)
            mine = slice(part * third, (part + 1) * third)
            bias = jnp.concatenate([vec(0)[:, mine], jnp.zeros((1, third), single), vec(1)[:, mine]], 1)
            mixed[r, cs] = (dot(x_v[r, :], v_in[:, cs]) + bias).astype(narrow)
            return 0

        lax.fori_loop(0, rows // 256, project, 0)

        def attend(j, _, part=part):
            g = j // per_part
            w = j % per_part
            i = g * pairs + part * per_part + w
            s_ = j % 2
            r = at(g * count, count)
            if part == 0:

                @pl.when(j >= 2)
                def _():
                    prob_store(i, s_).wait()

            else:
                prob_store(i, s_).wait()

            q = mixed[r, at(part * width + w * 128, 128)]
            k = mixed[r, at(part * width + third + w * 128, 128)]
            v = mixed[r, at(part * width + 2 * third + w * 128, 128)]
            zero = jnp.zeros_like(q)
            out = [None] * (count // 256)
            for h in range(2):
                qh = jnp.where(half[h], q, zero) * jnp.asarray(0.125, narrow)
                vh = jnp.where(half[h], v, zero)
                for b in range(count // 256):
                    sc = dot_nt(qh[b * 256 : (b + 1) * 256], k) + mask[g, b * 256 : (b + 1) * 256, :]
                    e = jnp.exp(sc - jnp.max(sc, -1, keepdims=True))
                    low = (e * (1.0 / jnp.sum(e, -1, keepdims=True))).astype(narrow)
                    pst[s_, h, b * 256 : (b + 1) * 256, :] = low
                    o = dot(low, vh)
                    out[b] = o if out[b] is None else out[b] + o
            for b in range(count // 256):
                ctx[at(g * count + b * 256, 256), at(part * third + w * 128, 128)] = out[b].astype(narrow)
            prob_store(i, s_).start()
            pump_in(j, GATHER_ATTEND[part])
            return 0

        pump(GATHER_PROJECT[part])
        lax.fori_loop(0, n, attend, 0)
        pumped(GATHER_ATTEND[part])
    store(mixed, mixed_o)
    for s_ in range(2):
        prob_store(0, s_).wait()
    store(ctx, ctx_o)

    need("out")

    def first(b, _):
        r = at(b * 256, 256)
        total = hid[r, :] + dot(ctx[r, :], v_out[...]) + vec(2)
        unit, rstd = norm_rows(total)
        n_st[r, :] = unit
        r1_v[r, :] = jnp.broadcast_to(rstd, (256, 128))
        h = unit * vec(3) + vec(4)
        hid_low[r, :] = h.astype(narrow)
        acc[r, :] = h + vec(5)
        pump_in(b, GATHER_FIRST)
        return 0

    lax.fori_loop(0, rows // 256, first, 0)
    pumped(GATHER_FIRST)
    store(n_st, n1_o)
    n1_store = stores[-1]
    store(r1_v, r1_o)
    store(hid_low, hid_o)

    def act_copies(j, s_):
        return (
            pltpu.make_async_copy(ast.at[s_], act_o.at[j], a_sem.at[s_]),
            pltpu.make_async_copy(gst.at[s_], gp_o.at[j], a_sem.at[2 + s_]),
        )

    for j in range(chunks):
        s_ = j % 2
        need("up%d" % j)
        need("down%d" % j)
        if j >= 2:
            for made in act_copies(j - 2, s_):
                made.wait()
        cs = pl.ds(j * chunk, chunk)

        def feed(b, _, s_=s_, j=j, cs=cs):
            r = at(b * 256, 256)
            u = dot(hid_low[r, :], v_up[:, cs]) + vec(8 + j, chunk)
            a, d = gelu_pair(u)
            a = a.astype(narrow)
            ast[s_, r, :] = a
            gst[s_, r, :] = d.astype(narrow)
            acc[r, :] += dot(a, v_down[j].reshape(chunk, width))
            pltpu.make_async_copy(ast.at[s_, r], act_o.at[j, r], a_sem.at[s_]).start()
            pltpu.make_async_copy(gst.at[s_, r], gp_o.at[j, r], a_sem.at[2 + s_]).start()
            pump_in(b, GATHER_FEED[j])
            return 0

        lax.fori_loop(0, rows // 256, feed, 0)
        pumped(GATHER_FEED[j])

    n1_store.wait()
    for g in range(groups):
        _, live = slot_lengths(lens, flag, g, True, count, 128)
        sums = []
        for s in range(4):
            r = pl.ds(g * count + s * slot, slot)
            unit, rstd = norm_rows(acc[r, :])
            n_st[r, :] = unit
            r2_v[r, :] = jnp.broadcast_to(rstd, (slot, 128))
            out = unit * vec(6) + vec(7)
            pltpu.make_async_copy(n_st.at[r], n2_o.at[r], out_sem.at[8]).start()
            pltpu.make_async_copy(r2_v.at[r], r2_o.at[r], out_sem.at[9]).start()
            keep = live[s * slot : (s + 1) * slot, :1]
            sums.append(jnp.sum(jnp.where(keep, out, 0.0), 0, keepdims=True))
        long = flag[g] > 0
        for s in range(4):
            div = jnp.maximum(lens[g, s], 1).astype(single)
            if s == 0:
                total = jnp.where(long, sums[0] + sums[1] + sums[2] + sums[3], sums[0])
            else:
                total = jnp.where(long, 0.0, sums[s])
            pooled_o[4 * g + s : 4 * g + s + 1, :] = total / div
    pltpu.make_async_copy(n_st, n2_o, out_sem.at[8]).wait()
    pltpu.make_async_copy(r2_v, r2_o, out_sem.at[9]).wait()
    for j in range(max(chunks - 2, 0), chunks):
        for made in act_copies(j, j % 2):
            made.wait()
    for made in stores:
        if made is not n1_store:
            made.wait()
    if remote:
        for p in pieces:
            p.sent()
        for k, j in others:
            small_copy(k, j).wait_send()


def normalize_rows(pooled):
    return pooled * lax.rsqrt(jnp.sum(pooled * pooled, -1, keepdims=True) + 1e-06)


def slot_roles(bucket):
    long_slot = jnp.repeat(jnp.repeat(bucket, 2), 4) > 0
    slots = jnp.arange(long_slot.shape[0], dtype=jnp.int32)
    within = slots % 4
    odd_group = slots // 4 % 2
    query = jnp.where(long_slot, (within == 0) & (odd_group == 0), within % 2 == 0)
    passage = jnp.where(long_slot, (within == 0) & (odd_group == 1), within % 2 == 1)
    partner = jnp.where(long_slot, slots + 4, slots + 1)
    return (query, passage, partner)


def contrast(every, own, start, rows, bucket):
    query, passage, partner = slot_roles(bucket)
    pair_count = jnp.sum(4 - 3 * bucket).astype(single)
    logits = jnp.einsum("id,jd->ij", every, every, preferred_element_type=single) * 100.0
    columns = jnp.arange(logits.shape[1], dtype=jnp.int32)
    masked = jnp.where(passage[None, :], logits, -1000000000.0)
    top = jnp.max(masked, -1, keepdims=True)
    raised = jnp.exp(masked - top)
    total = jnp.sum(raised, -1, keepdims=True)
    spread = top[:, 0] + jnp.log(total[:, 0])
    match = columns[None, :] == partner[:, None]
    positive = jnp.sum(jnp.where(match, logits, 0.0), -1)
    loss = jnp.sum(jnp.where(query, spread - positive, 0.0)) / pair_count
    row_weight = jnp.where(query, 1.0, 0.0) / pair_count
    logit_grad = (row_weight[:, None] * (raised / total - match.astype(single))).astype(narrow)
    by_row = lax.dynamic_slice_in_dim(logit_grad, start, rows, 0)
    by_column = lax.dynamic_slice_in_dim(logit_grad, start, rows, 1)
    both = jnp.dot(by_row, every, preferred_element_type=single) + jnp.einsum(
        "ij,id->jd", by_column, every, preferred_element_type=single
    )
    return loss, both * 100.0


MESH = pl.DeviceIdType.MESH


def place():
    dp, fs = lax.axis_index("dp"), lax.axis_index("fsdp")
    return dp % 2, dp // 2, fs // 2, fs % 2


def device_at(x, y, z, c):
    return (y * 2 + x, z * 2 + c)


class Wires:
    def __init__(self, send, recv):
        self.send, self.recv, self.next, self.sent = send, recv, 0, []

    def copy(self, src, dst, device):
        i = self.next
        self.next += 1
        made = pltpu.make_async_remote_copy(
            src_ref=src, dst_ref=dst, send_sem=self.send.at[i], recv_sem=self.recv.at[i],
            device_id=device, device_id_type=MESH,
        )
        made.start()
        self.sent.append(made)
        return made

    def finish(self):
        for made in self.sent:
            made.wait_send()


def greet(devices, between=None):
    barrier = pltpu.get_barrier_semaphore()
    for d in devices:
        pl.semaphore_signal(barrier, inc=1, device_id=d, device_id_type=MESH)
    if between is not None:
        between()
    pl.semaphore_wait(barrier, len(devices))


def neighbours(small_too):
    x, y, z, c = place()
    found = [device_at(1 - x, y, z, c), device_at(x, 1 - y, z, c), device_at(x, y, z, 1 - c)]
    for k in (1, 2, 3):
        found.append(device_at(x, y, (z + k) % 4, c))
        if small_too:
            found.append(device_at(x, y, (z + k) % 4, 1 - c))
    return found


GATHER_EVENTS = ((0, 0), (0, 1), (1, 0), (0, 2), (1, 1), (0, 3), (2, 0), (1, 2), (0, 4), (2, 1), (0, 5), (3, 0), (1, 3), (4, 0), (0, 6), (2, 2), (3, 1), (1, 4), (2, 3), (1, 5), (0, 7), (4, 1), (0, 8), (3, 2), (2, 4), (1, 6), (3, 3), (4, 2), (0, 9), (4, 3), (2, 5), (1, 7), (3, 4), (0, 10), (1, 8), (4, 4), (2, 6), (3, 5), (1, 9), (4, 5), (2, 7), (1, 10), (2, 8), (3, 6), (4, 6), (2, 9), (3, 7), (4, 7), (2, 10), (3, 8), (3, 9), (4, 8), (3, 10), (4, 9), (4, 10))
GATHER_START = 2
GATHER_PROJECT = (27, 38, 44)
GATHER_ATTEND = ((28, 32, 33, 34), (38, 41, 41, 43), (44, 46, 47, 47))
GATHER_FIRST = (47, 49, 49, 50)
GATHER_FEED = ((51, 53, 54, 54), (55, 55, 55, 55), (55, 55, 55, 55))


class Piece:
    COPIES = 17

    def __init__(self, index, sems, at_, shard, full, pitch, rows, cols):
        self.send, self.recv = sems
        self.x, self.y, self.z, self.c = at_
        self.base = index * self.COPIES
        self.shard, self.full, self.pitch = shard, full, pitch
        self.r0, self.rows = rows
        self.c0, self.cols = cols
        self.both = self.rows % 64 == 0
        self.ways = ("x", "y", "both" if self.both else ("x" if index % 2 else "y"))

    def block(self, ref, fs, a=None, b=None, part=None):
        start = self.r0 if fs is None else fs * self.pitch + self.r0
        rows, col, cols = self.rows, self.c0, self.cols
        if a is not None:
            rows, cols = rows // 2, cols // 2
            start, col = start + a * rows, col + b * cols
        if part is not None:
            rows = rows // 2
            start = start + part * rows
        return ref.at[pl.ds(pl.multiple_of(start, 16), rows), pl.ds(pl.multiple_of(col, 128), cols)]

    def copy(self, i, src, dst, device):
        return pltpu.make_async_remote_copy(
            src_ref=src, dst_ref=dst, send_sem=self.send.at[self.base + i], recv_sem=self.recv.at[self.base + i],
            device_id=device, device_id_type=MESH,
        )

    def from_z(self, k):
        return 2 * ((self.z - k + 4) % 4) + self.c

    def by_z(self, k):
        mine = 2 * self.z + self.c
        there = device_at(self.x, self.y, (self.z + k) % 4, self.c)
        return self.copy(k - 1, self.block(self.shard, None, self.x, self.y), self.block(self.full, mine, self.x, self.y), there)

    def by_x(self, k):
        mine = self.block(self.full, self.from_z(k), self.x, self.y)
        return self.copy(2 + k, mine, mine, device_at(1 - self.x, self.y, self.z, self.c))

    def by_y(self, k):
        mine = self.block(self.full, self.from_z(k), self.x, self.y)
        return self.copy(5 + k, mine, mine, device_at(self.x, 1 - self.y, self.z, self.c))

    def corners(self, k):
        way = self.ways[k - 1]
        parts = (0, 1) if way == "both" else (None, None)
        made = []
        if way != "y":
            got = self.block(self.full, self.from_z(k), 1 - self.x, self.y, parts[0])
            made.append(self.copy(8 + k, got, got, device_at(self.x, 1 - self.y, self.z, self.c)))
        if way != "x":
            got = self.block(self.full, self.from_z(k), self.x, 1 - self.y, parts[1])
            made.append(self.copy(10 if k == 2 else 12, got, got, device_at(1 - self.x, self.y, self.z, self.c)))
        return made

    def by_core(self, k):
        there = device_at(self.x, self.y, self.z, 1 - self.c)
        got = self.block(self.full, self.from_z(k))
        src = self.block(self.shard, None) if k == 0 else got
        return self.copy(13 + k, src, got, there)

    def begin(self):
        for k in (1, 2, 3):
            self.by_z(k).start()
        self.by_core(0).start()

    def plane(self):
        for k in (1, 2, 3):
            self.by_z(k).wait_recv()
            self.by_x(k).start()
            self.by_y(k).start()

    def diagonal(self):
        for k in (1, 2, 3):
            self.by_x(k).wait_recv()
            self.by_y(k).wait_recv()
            for made in self.corners(k):
                made.start()

    def core(self):
        for k in (1, 2, 3):
            for made in self.corners(k):
                made.wait_recv()
            self.by_core(k).start()

    def finish(self):
        for k in range(4):
            self.by_core(k).wait_recv()

    def sent(self):
        for k in (1, 2, 3):
            for made in [self.by_z(k), self.by_x(k), self.by_y(k), self.by_core(k)] + self.corners(k):
                made.wait_send()
        self.by_core(0).wait_send()


class Sum:
    COPIES = 11

    def __init__(self, index, sems, at_, own, b1x, b1y, b2x, b2y, from_z, final):
        self.send, self.recv = sems
        self.x, self.y, self.z, self.c = at_
        self.base = index * self.COPIES
        self.own, self.b1x, self.b1y, self.b2x, self.b2y, self.from_z, self.final = own, b1x, b1y, b2x, b2y, from_z, final
        _, self.rows, self.cols = own.shape

    def rh(self, a):
        return pl.ds(pl.multiple_of(a * (self.rows // 2), 16), self.rows // 2)

    def ch(self, b):
        return pl.ds(pl.multiple_of(b * (self.cols // 2), 128), self.cols // 2)

    def copy(self, i, src, dst, device):
        return pltpu.make_async_remote_copy(
            src_ref=src, dst_ref=dst, send_sem=self.send.at[self.base + i], recv_sem=self.recv.at[self.base + i],
            device_id=device, device_id_type=MESH,
        )

    def to_x(self):
        return device_at(1 - self.x, self.y, self.z, self.c)

    def to_y(self):
        return device_at(self.x, 1 - self.y, self.z, self.c)

    def to_core(self, src, dst):
        return self.copy(0, src, dst, device_at(self.x, self.y, self.z, 1 - self.c))

    def halves(self):
        lo, hi = pl.ds(0, 2), pl.ds(2, 2)
        return (
            self.copy(1, self.own.at[lo, self.rh(1 - self.x), :], self.b1x, self.to_x()),
            self.copy(2, self.own.at[hi, :, self.ch(1 - self.y)], self.b1y, self.to_y()),
        )

    def quarters(self):
        lo, hi = pl.ds(0, 2), pl.ds(2, 2)
        return (
            self.copy(3, self.own.at[lo, self.rh(self.x), self.ch(1 - self.y)], self.b2y, self.to_y()),
            self.copy(4, self.own.at[hi, self.rh(1 - self.x), self.ch(self.y)], self.b2x, self.to_x()),
        )

    def along(self):
        return [
            self.copy(
                4 + k, self.own.at[(self.z + k) % 4, self.rh(self.x), self.ch(self.y)], self.from_z.at[k - 1],
                device_at(self.x, self.y, (self.z + k) % 4, self.c),
            )
            for k in (1, 2, 3)
        ]

    def back(self):
        mine = self.final.at[self.rh(self.x), self.ch(self.y)]
        return [
            self.copy(8, mine, mine, self.to_x()),
            self.copy(9, mine, mine, self.to_y()),
            self.copy(10, mine, mine, device_at(1 - self.x, 1 - self.y, self.z, self.c)),
        ]

    def add(self, zs, row0, rows, cols, other):
        step = self.rows // 2
        blocks = rows // step

        def body(i, _):
            zi = i // blocks
            r = i % blocks * step
            mine = (zs + zi, pl.ds(pl.multiple_of(row0 + r, 16), step), cols)
            theirs = other[zi, pl.ds(pl.multiple_of(r, 16), step), :]
            self.own[mine] = (self.own[mine].astype(single) + theirs.astype(single)).astype(narrow)
            return 0

        lax.fori_loop(0, 2 * blocks, body, 0)

    def first(self, stage, got):
        def body(i, _):
            self.own[i] = (stage[i, self.c].astype(single) + got[i].astype(single)).astype(narrow)
            return 0

        lax.fori_loop(0, 4, body, 0)
        for made in self.halves():
            made.start()

    def second(self):
        for made in self.halves():
            made.wait_recv()
        self.add(0, self.x * (self.rows // 2), self.rows // 2, slice(None), self.b1x)
        self.add(2, 0, self.rows, self.ch(self.y), self.b1y)
        for made in self.quarters():
            made.start()

    def third(self):
        for made in self.quarters():
            made.wait_recv()
        self.add(0, self.x * (self.rows // 2), self.rows // 2, self.ch(self.y), self.b2y)
        self.add(2, self.x * (self.rows // 2), self.rows // 2, self.ch(self.y), self.b2x)
        for made in self.along():
            made.start()

    def fourth(self):
        for made in self.along():
            made.wait_recv()
        total = self.own[self.z, self.rh(self.x), self.ch(self.y)].astype(single)
        for k in range(3):
            total = total + self.from_z[k].astype(single)
        self.final[self.rh(self.x), self.ch(self.y)] = total.astype(narrow)
        for made in self.back():
            made.start()

    def finish(self):
        for made in self.back():
            made.wait_recv()

    def sent(self):
        for made in list(self.halves()) + list(self.quarters()) + self.along() + self.back():
            made.wait_send()


class SumDeep(Sum):
    def __init__(self, index, sems, at_, own, half, quarter, from_z, final):
        super().__init__(index, sems, at_, own, None, None, None, None, from_z, final)
        self.half, self.quarter = half, quarter
        self.x_first = index % 4 == 1

    def shard(self, *where):
        return self.own.at[(self.z,) + where]

    def along(self):
        return [
            self.copy(4 + k, self.own.at[(self.z + k) % 4], self.from_z.at[k - 1], device_at(self.x, self.y, (self.z + k) % 4, self.c))
            for k in (1, 2, 3)
        ]

    def halves(self):
        if self.x_first:
            return (self.copy(1, self.shard(self.rh(1 - self.x), slice(None)), self.half, self.to_x()),)
        return (self.copy(1, self.shard(slice(None), self.ch(1 - self.y)), self.half, self.to_y()),)

    def quarters(self):
        if self.x_first:
            return (self.copy(3, self.shard(self.rh(self.x), self.ch(1 - self.y)), self.quarter, self.to_y()),)
        return (self.copy(3, self.shard(self.rh(1 - self.x), self.ch(self.y)), self.quarter, self.to_x()),)

    def first(self, stage, got):
        def body(i, _):
            self.own[i] = (stage[i, self.c].astype(single) + got[i].astype(single)).astype(narrow)
            return 0

        lax.fori_loop(0, 4, body, 0)
        for made in self.along():
            made.start()

    def second(self):
        for made in self.along():
            made.wait_recv()
        total = self.own[self.z].astype(single)
        for k in range(3):
            total = total + self.from_z[k].astype(single)
        self.own[self.z] = total.astype(narrow)
        for made in self.halves():
            made.start()

    def third(self):
        for made in self.halves():
            made.wait_recv()
        mine = (self.z, self.rh(self.x), slice(None)) if self.x_first else (self.z, slice(None), self.ch(self.y))
        self.own[mine] = (self.own[mine].astype(single) + self.half[...].astype(single)).astype(narrow)
        for made in self.quarters():
            made.start()

    def fourth(self):
        for made in self.quarters():
            made.wait_recv()
        total = self.own[self.z, self.rh(self.x), self.ch(self.y)].astype(single) + self.quarter[...].astype(single)
        self.final[self.rh(self.x), self.ch(self.y)] = total.astype(narrow)
        for made in self.back():
            made.start()


DEEP = (1, 3, 8)


class SumSmall:
    COPIES = 6

    def __init__(self, base, sems, at_, total, got):
        self.send, self.recv = sems
        self.x, self.y, self.z, self.c = at_
        self.base, self.total, self.got = base, total, got

    def copies(self, i):
        x, y, z, c = self.x, self.y, self.z, self.c
        to = [[device_at(x, y, z, 1 - c)], [device_at(1 - x, y, z, c)], [device_at(x, 1 - y, z, c)]]
        to.append([device_at(x, y, (z + k) % 4, c) for k in (1, 2, 3)])
        return [
            pltpu.make_async_remote_copy(
                src_ref=self.total.at[i], dst_ref=self.got.at[i + n], send_sem=self.send.at[self.base + i + n],
                recv_sem=self.recv.at[self.base + i + n], device_id=d, device_id_type=MESH,
            )
            for n, d in enumerate(to[i])
        ]

    def begin(self):
        for made in self.copies(0):
            made.start()

    def step(self, i):
        for made in self.copies(i):
            made.wait_recv()
        self.total[i + 1] = self.total[i] + self.got[i]
        for made in self.copies(i + 1):
            made.start()

    def finish(self, out):
        for made in self.copies(3):
            made.wait_recv()
        terms = []
        for i in range(4):
            term = self.total[3]
            for k in (1, 2, 3):
                term = jnp.where((self.z - k + 4) % 4 == i, self.got[2 + k], term)
            terms.append(term)
        out[...] = ((terms[0] + terms[1]) + terms[2]) + terms[3]
        for i in range(4):
            for made in self.copies(i):
                made.wait_send()


def contrast_kernel(slots, buckets, bucket, pooled, loss_o, grad_o, mine, every, full, send, recv, sem):
    x, y, z, c = place()
    device = (y * 2 + x) * 8 + 2 * z + c
    greet(neighbours(False))
    wires = Wires(send, recv)
    p = pooled[...]
    scale = lax.rsqrt(jnp.sum(p * p, -1, keepdims=True) + 1e-06)
    e = p * scale
    width = e.shape[1]
    hw = width // 2
    mine[...] = jnp.concatenate([e[:, :hw], e[:, hw:]], 0).astype(narrow)

    def block(xx, yy, zz):
        return every.at[(yy * 2 + xx) * 4 + zz, c]

    keep = pltpu.make_async_copy(mine, block(x, y, z), sem)
    keep.start()
    by_x = wires.copy(mine, block(x, y, z), device_at(1 - x, y, z, c))
    by_y = [wires.copy(mine, block(x, y, z), device_at(x, 1 - y, z, c))]
    by_z = [wires.copy(mine, block(x, y, z), device_at(x, y, (z + k) % 4, c)) for k in (1, 2, 3)]
    by_x.wait_recv()
    by_y.append(wires.copy(block(1 - x, y, z), block(1 - x, y, z), device_at(x, 1 - y, z, c)))
    by_z += [wires.copy(block(1 - x, y, z), block(1 - x, y, z), device_at(x, y, (z + k) % 4, c)) for k in (1, 2, 3)]
    for s in by_y:
        s.wait_recv()
    for xx in (x, 1 - x):
        by_z += [
            wires.copy(block(xx, 1 - y, z), block(xx, 1 - y, z), device_at(x, y, (z + k) % 4, c)) for k in (1, 2, 3)
        ]
    pair_size = 8

    def long_of(shape, axis):
        pair = lax.broadcasted_iota(jnp.int32, shape, axis) // pair_size
        found = jnp.zeros(shape, jnp.int32)
        for b in range(buckets):
            found = jnp.where(pair == b, bucket[b], found)
        return found > 0

    def roles(shape, axis):
        t = lax.broadcasted_iota(jnp.int32, shape, axis)
        long = long_of(shape, axis)
        within, odd = t % 4, t // 4 % 2
        query = jnp.where(long, jnp.where((within == 0) & (odd == 0), 1, 0), jnp.where(within % 2 == 0, 1, 0))
        passage = jnp.where(long, jnp.where((within == 0) & (odd == 1), 1, 0), jnp.where(within % 2 == 1, 1, 0))
        return query > 0, passage > 0, jnp.where(long, t + 4, t + 1)

    _, passage, _ = roles((8, slots), 1)
    query, _, partner = roles((slots, 128), 0)
    passage, query, partner = passage[:1], query[:, :1], partner[:, :1]
    pair_count = jnp.zeros((), single)
    for b in range(buckets):
        pair_count = pair_count + (4 - 3 * bucket[b]).astype(single)
    keep.wait()
    for s in by_z:
        s.wait_recv()
    wires.copy(every.at[:, c], every.at[:, c], device_at(x, y, z, 1 - c)).wait_recv()
    both = every[...].astype(single).reshape(slots // 8, 16, hw)
    left = both[:, :8, :].reshape(slots, hw).astype(narrow)
    right = both[:, 8:, :].reshape(slots, hw).astype(narrow)
    logits = (dot_nt(left, left) + dot_nt(right, right)) * 100.0
    masked = jnp.where(passage, logits, -1000000000.0)
    top = jnp.max(masked, -1, keepdims=True)
    raised = jnp.exp(masked - top)
    total = jnp.sum(raised, -1, keepdims=True)
    match = lax.broadcasted_iota(jnp.int32, (slots, slots), 1) == partner
    positive = jnp.sum(jnp.where(match, logits, 0.0), -1, keepdims=True)
    terms = jnp.where(query, top + jnp.log(total) - positive, 0.0)
    loss = jnp.sum(terms, 0, keepdims=True) / pair_count
    loss_o[...] = loss
    weight = jnp.where(query, 1.0, 0.0) / pair_count
    logit_grad = weight * (raised / total - jnp.where(match, 1.0, 0.0))
    by_row = logit_grad.astype(narrow)
    by_column = logit_grad.T.astype(narrow)
    full[:, :hw] = dot(by_row, left) + dot(by_column, left)
    full[:, hw:] = dot(by_row, right) + dot(by_column, right)
    g = full[pl.ds(pl.multiple_of(device * 8, 8), 8), :] * 100.0
    grad_o[...] = scale * g - p * (scale * scale * scale) * jnp.sum(p * g, -1, keepdims=True)
    wires.finish()


def run_contrast(bucket, pooled, devices):
    rows, width = pooled.shape
    slots = rows * devices
    dma = pltpu.SemaphoreType.DMA
    spec_v = pl.BlockSpec(memory_space=VM)
    copies = 1 + 2 + 12 + 1
    loss, grad = pl.pallas_call(
        functools.partial(contrast_kernel, slots, bucket.shape[0]),
        out_shape=[jax.ShapeDtypeStruct((1, 1), single), jax.ShapeDtypeStruct(pooled.shape, single)],
        in_specs=[pl.BlockSpec(memory_space=SM), spec_v],
        out_specs=[spec_v, spec_v],
        scratch_shapes=[
            VM((2 * rows, width // 2), narrow), VM((devices // 2, 2, 2 * rows, width // 2), narrow), VM((slots, width), single),
            dma((copies,)), dma((copies,)), dma(()),
        ],
        compiler_params=pltpu.CompilerParams(collective_id=3, has_side_effects=True),
        name="contrast",
    )(bucket, pooled)
    return loss.reshape(()), grad


def gather_weights(tab, w_in, w_out, w_up, w_down, small):
    gat = lambda a: lax.all_gather(a, "fsdp", axis=0, tiled=True)
    return lax.all_gather(tab, "fsdp", axis=1, tiled=True), gat(w_in), gat(w_out), gat(w_up), gat(w_down), gat(small)


def reduce_all(grads, small):
    done = []
    for a in grads:
        part = lax.psum_scatter(a.astype(single), "fsdp", scatter_dimension=0, tiled=True)
        done.append(lax.psum(part.astype(narrow), "dp").astype(single))
    return done, lax.psum(small, ("dp", "fsdp"))


def local(
    tokens, lengths, bucket, position_table, in_projection, query_bias, value_bias, out_projection, out_bias,
    first_gain, first_shift, up_projection, up_bias, down_projection, down_bias, second_gain, second_shift,
):
    groups = lengths.shape[0]
    width = tokens.shape[1]
    count = tokens.shape[0] // groups
    shards = lax.axis_size("fsdp")
    ff = up_projection.shape[1]
    fs = lax.axis_index("fsdp")
    device = lax.axis_index("dp") * shards + fs
    small_parts = (query_bias, value_bias, out_bias, first_gain, first_shift, down_bias, second_gain, second_shift)
    piece = query_bias.shape[0]
    wide_piece = up_bias.shape[0]
    flag = lax.dynamic_slice_in_dim(jnp.repeat(bucket, 2), device * groups, groups)
    chunk = 1024
    chunks, per = ff // chunk, chunk // 8
    grid = lax.axis_size("dp") == 4 and shards == 8
    if grid:
        line = jnp.concatenate([v[None] for v in small_parts] + [jnp.zeros((8, piece), narrow)], 0)
        spread = lax.dynamic_update_slice(jnp.zeros((16, chunk), narrow), line, (0, fs * piece))
        ups = up_bias.reshape(chunks, per)
        small = lax.dynamic_update_slice(spread, ups, (8, fs * per))
        table = position_table.T
        weights = (in_projection, out_projection, up_projection, down_projection)
    else:
        vectors = jnp.concatenate(small_parts + (up_bias,))[None, :]
        table, w_in, w_out, w_up, w_down, small_all = gather_weights(
            position_table, in_projection, out_projection, up_projection, down_projection, vectors
        )
        table = table.T
        heads = small_all[:, : 8 * piece].reshape(shards, 8, piece).transpose(1, 0, 2).reshape(8, width)
        ups = small_all[:, 8 * piece :].reshape(8, chunks, per).transpose(1, 0, 2).reshape(chunks, chunk)
        small = jnp.concatenate(
            [jnp.pad(heads, ((0, 0), (0, chunk - width))), ups, jnp.zeros((8 - chunks, chunk), narrow)]
        )
        w_in = w_in.reshape(width, 3, 3, width // 3).transpose(0, 2, 1, 3).reshape(width, 3 * width)
        w_up = w_up.reshape(width, 8, chunks, per).transpose(0, 2, 1, 3).reshape(width, ff)
        w_down = w_down.reshape(8, chunks, per, width).transpose(1, 0, 2, 3)
        weights = (w_in, w_out, w_up, w_down)
    outs = run_forward(grid, groups, count, width, ff, chunk, lengths, flag, small, tokens, table, weights)
    saved, pooled, vecs = outs[:11], outs[11], outs[12]
    if grid:
        weights = tuple(outs[14:18])
    slots = groups * 4
    if grid:
        loss, pooled_grad = run_contrast(bucket, pooled, 4 * shards)
    else:
        embedded, norm_grad = jax.vjp(normalize_rows, pooled)
        every = lax.all_gather(embedded.astype(narrow), ("dp", "fsdp"), axis=0, tiled=True)
        loss, embed_grad = contrast(every, embedded, device * slots, slots, bucket)
        pooled_grad = norm_grad(embed_grad)[0]
    tokens_grad, blocks, gvec = run_backward(
        grid, groups, count, width, ff, chunk, lengths, flag, vecs, pooled_grad, weights, saved
    )
    shapes = item_shapes(count, width, ff, chunk)
    if grid:
        tokens_grad, gdown, gup, gout, gin, gtab = run_finish(shapes, chunks, tokens_grad, blocks)
        gtab = gtab.T
    else:
        blocks = [b.reshape(8 * r, k) for b, (r, k) in zip(blocks, shapes)]
        gdown = jnp.stack([b.reshape(8, per, width) for b in blocks[0 : 2 * chunks : 2]], 1).reshape(ff, width)
        gup = jnp.stack([b.reshape(width, 8, per) for b in blocks[1 : 2 * chunks : 2]], 2).reshape(width, ff)
        gin = jnp.stack([b.reshape(width, 3, width // 3) for b in blocks[2 * chunks + 1 : 2 * chunks + 4]], 2)
        gin = gin.reshape(width, 3 * width)
        (gin, gout, gup, gdown, gtab), gvec = reduce_all((gin, blocks[2 * chunks], gup, gdown, blocks[-1]), gvec)
        gtab = gtab.T
    own = [lax.dynamic_slice_in_dim(gvec[i], fs * piece, piece) for i in range(8)]
    ups = gvec[8 : 8 + chunks].reshape(chunks, 8, per).transpose(1, 0, 2).reshape(ff)
    up_own = lax.dynamic_slice_in_dim(ups, fs * wide_piece, wide_piece)
    return (
        loss, pooled, tokens_grad, gtab, gin, own[0], own[1], gout, own[2], own[3], own[4], gup, up_own, gdown,
        own[5], own[6], own[7],
    )


def solution(mesh):
    rows = P(("dp", "fsdp"), None)
    vec = P("fsdp")
    mat = P("fsdp", None)
    in_specs = (rows, rows, P(), P(None, "fsdp"), mat, vec, vec, mat, vec, vec, vec, mat, vec, mat, vec, vec, vec)
    out_specs = (P(), rows, rows, P(None, "fsdp"), mat, vec, vec, mat, vec, vec, vec, mat, vec, mat, vec, vec, vec)
    return jax.shard_map(local, mesh=mesh, in_specs=in_specs, out_specs=out_specs, check_vma=False)
```
